32 devices in a mesh: clip: 4 (over y, core), space: 8 (over z, x).
Axes of the slice: x: 2, y: 2, z: 4, core: 2. Of those that a mesh axis runs over, the one named last changes fastest.
Arguments:
- teacher_input: bfloat16 [4, 2, 64, 32, 512], P('clip', None, 'space'), may hold values from -6 to 6
- conv_first: bfloat16 [3, 3, 3, 512, 256], replicated, may hold values from -0.0546875 to 0.0546875
- conv_second: bfloat16 [3, 3, 3, 256, 256], replicated, may hold values from -0.078125 to 0.078125
- student_low: bfloat16 [4, 2, 64, 32, 256], P('clip', None, 'space'), may hold values from -6 to 6
- student_high: bfloat16 [4, 2, 128, 64, 128], P('clip', None, 'space'), may hold values from -6 to 6
- kernel_low: float32 [3, 3, 3, 256], replicated, may hold values from -1 to 1
- kernel_high: float32 [3, 3, 3, 128], replicated, may hold values from -1 to 1
- adapter_low: bfloat16 [256, 256], replicated, may hold values from -0.0078125 to 0.0078125
- adapter_high: bfloat16 [128, 256], replicated, may hold values from -0.009765625 to 0.009765625
Outputs:
- adapter_low_gradient: float32 [256, 256], P('clip')
- kernel_low_gradient: float32 [3, 3, 3, 256], P(None, None, None, 'clip')
- adapter_high_gradient: float32 [128, 256], P('clip')
- kernel_high_gradient: float32 [3, 3, 3, 128], P(None, None, None, 'clip')
- fine_mismatch: bfloat16 [4, 2, 128, 64, 256], P('clip', None, 'space')
The draws below stay inside these ranges and needn't reach their ends.
All inputs are finite; a program needn't handle non-finite values.
Results may differ from the reference program's by a relative error of at most 0.0067.
Values may be sent and summed in bfloat16 or wider, within the bound.
No kernel may reach another device: no remote copies, remote signals or barrier semaphores. Data moves between devices by JAX's collectives and lax.ppermute only.
A program may use at most 192 MiB of HBM per device.

```python
import jax
import jax.numpy as jnp
from jax import lax

TEACH_IN = 512
TEACH_OUT = 256
STU_LOW = 256
STU_HIGH = 128
FRAMES = 2
COLS = 32
CLIPS = 4
ROWS = 64


def with_spikes(entries, own_key, source, target, shards_of, factor):
    def block_of(axis_at):
        return (jnp.arange(entries.shape[axis_at]) // (entries.shape[axis_at] // shards_of)).reshape((-1,) + (1,) * (entries.ndim - 1 - axis_at))

    first = jax.random.permutation(own_key, shards_of)[block_of(target)]
    far = (block_of(target) + shards_of // 2) % shards_of
    return jnp.where((block_of(source) == first) | (block_of(source) == far), factor * entries, entries)


def block_scale(own_key, shape, pieces, least, top_value):
    gain = 1.0
    for dim, shards_of in pieces:
        steps = jax.random.uniform(jax.random.fold_in(jax.random.fold_in(own_key, 6), dim), (shards_of,), jnp.float32, least / len(pieces), top_value / len(pieces))
        gain = gain * jnp.repeat(jnp.exp(steps), shape[dim] // shards_of).reshape((-1,) + (1,) * (len(shape) - 1 - dim))
    return gain


def noise(rng, dims, deviation, reach, split=(), dtype=jnp.bfloat16):
    result = deviation * jax.random.normal(rng, dims, jnp.float32)
    if split:
        result = result * block_scale(rng, dims, split, -0.22, 0.18)
    return jnp.clip(result, -reach, reach).astype(dtype)


def noise_with(stream_key, shape, spread, limit, shards, heavy, held_as=jnp.bfloat16):
    result = spread * jax.random.normal(stream_key, shape, jnp.float32)
    if shards:
        result = result * block_scale(stream_key, shape, shards, -0.22, 0.18)
    return jnp.clip(with_spikes(result, jax.random.fold_in(stream_key, 3), *heavy), -limit, limit).astype(held_as)


def setup_inputs(seed: int = 0) -> dict:
    arg_keys = jax.random.split(jax.random.key(seed), 10)
    teacher_input = noise(arg_keys[0], (CLIPS, FRAMES, ROWS, COLS, TEACH_IN), 1.0, 6.0, ((0, 4), (2, 8)))
    conv_first = noise(arg_keys[1], (3, 3, 3, TEACH_IN, TEACH_OUT), (27 * TEACH_IN) ** -0.5, 0.0546875)
    conv_second = noise(arg_keys[2], (3, 3, 3, TEACH_OUT, TEACH_OUT), (27 * TEACH_OUT) ** -0.5, 0.078125)
    student_low = noise_with(arg_keys[3], (CLIPS, FRAMES, ROWS, COLS, STU_LOW), 1.0, 6.0, ((0, 4), (2, 8)), (0, 4, 4, 2.0))
    student_high = noise_with(arg_keys[4], (CLIPS, FRAMES, 2 * ROWS, 2 * COLS, STU_HIGH), 1.0, 6.0, ((0, 4), (2, 8)), (0, 4, 4, 2.0))
    kernel_low = noise(arg_keys[5], (3, 3, 3, STU_LOW), 0.2, 1.0, (), jnp.float32)
    kernel_high = noise(arg_keys[6], (3, 3, 3, STU_HIGH), 0.2, 1.0, (), jnp.float32)
    adapter_low = noise(arg_keys[7], (STU_LOW, TEACH_OUT), (2500 * STU_LOW) ** -0.5, 0.0078125)
    adapter_high = noise(arg_keys[8], (STU_HIGH, TEACH_OUT), (2500 * STU_HIGH) ** -0.5, 0.009765625)
    return dict(teacher_input=teacher_input, conv_first=conv_first, conv_second=conv_second, student_low=student_low, student_high=student_high, kernel_low=kernel_low, kernel_high=kernel_high, adapter_low=adapter_low, adapter_high=adapter_high)


def conv_full(field, weight):
    padded = jnp.pad(field, ((1, 1), (1, 1), (1, 1), (0, 0)))
    frames, row_count, col_count = field.shape[0], field.shape[1], field.shape[2]
    summed = jnp.zeros((frames, row_count, col_count, weight.shape[-1]), jnp.float32)
    for tap_t in range(3):
        for tap_h in range(3):
            for tap_w in range(3):
                window_part = padded[tap_t:tap_t + frames, tap_h:tap_h + row_count, tap_w:tap_w + col_count, :]
                summed = summed + jnp.dot(window_part, weight[tap_t, tap_h, tap_w], preferred_element_type=jnp.float32)
    return summed


def level_grads(field, kernel, adapter, target, scale):
    padded = jnp.pad(field, ((1, 1), (1, 1), (1, 1), (0, 0)))
    frames, row_count, col_count = field.shape[0], field.shape[1], field.shape[2]
    mixed = field.astype(jnp.float32)
    for tap_t in range(3):
        for tap_h in range(3):
            for tap_w in range(3):
                shifted = padded[tap_t:tap_t + frames, tap_h:tap_h + row_count, tap_w:tap_w + col_count, :].astype(jnp.float32)
                mixed = mixed + shifted * kernel[tap_t, tap_h, tap_w]
    student = mixed.astype(jnp.bfloat16)
    output = jnp.dot(student, adapter, preferred_element_type=jnp.float32)
    mismatch = output - target.astype(jnp.float32)
    resid = (mismatch * scale).astype(jnp.bfloat16)
    adapter_part = jnp.einsum("fhwc,fhwd->cd", student.astype(jnp.float32), resid.astype(jnp.float32))
    back = jnp.einsum("fhwd,cd->fhwc", resid.astype(jnp.float32), adapter.astype(jnp.float32))
    kernel_rows = []
    for tap_t in range(3):
        for tap_h in range(3):
            for tap_w in range(3):
                shifted = padded[tap_t:tap_t + frames, tap_h:tap_h + row_count, tap_w:tap_w + col_count, :].astype(jnp.float32)
                kernel_rows.append(jnp.sum(back * shifted, axis=(0, 1, 2)))
    kernel_part = jnp.stack(kernel_rows).reshape(kernel.shape)
    return adapter_part, kernel_part, mismatch.astype(jnp.bfloat16)


def reference(teacher_input, conv_first, conv_second, student_low, student_high, kernel_low, kernel_high, adapter_low, adapter_high):
    low_count = teacher_input.shape[0] * teacher_input.shape[1] * teacher_input.shape[2] * teacher_input.shape[3]
    scale_low = 1.0 / low_count
    scale_high = 1.0 / (4 * low_count)

    def one_clip(items):
        clip_input, clip_low, clip_high = items
        first_feature = conv_full(clip_input, conv_first).astype(jnp.bfloat16)
        gated = jax.nn.silu(first_feature.astype(jnp.float32)).astype(jnp.bfloat16)
        upsampled = jnp.repeat(jnp.repeat(gated, 2, axis=1), 2, axis=2)
        second_feature = conv_full(upsampled, conv_second).astype(jnp.bfloat16)
        adapter_one, kernel_one, unused_low = level_grads(clip_low, kernel_low, adapter_low, first_feature, scale_low)
        adapter_two, kernel_two, mismatch_two = level_grads(clip_high, kernel_high, adapter_high, second_feature, scale_high)
        return adapter_one, kernel_one, adapter_two, kernel_two, mismatch_two

    results = lax.map(one_clip, (teacher_input, student_low, student_high))
    return (jnp.sum(results[0], axis=0), jnp.sum(results[1], axis=0),
            jnp.sum(results[2], axis=0), jnp.sum(results[3], axis=0), results[4])
```

```python
import functools

import jax
import jax.numpy as jnp
from jax import lax
from jax.experimental import pallas as pl
from jax.experimental.pallas import tpu as pltpu
from jax.sharding import PartitionSpec as P

F32, BF16 = jnp.float32, jnp.bfloat16
HBM = pl.BlockSpec(memory_space=pltpu.HBM)
MIB = 1 << 20


def shift_cols(value, by):
    axis = value.ndim - 2
    count = value.shape[axis]
    column = lax.broadcasted_iota(jnp.int32, value.shape, axis)
    edge = 0 if by > 0 else count - 1
    return jnp.where(column == edge, 0.0, pltpu.roll(value, by % count, axis))


def silu(value):
    return value / (1.0 + jnp.exp(-value))


def dot(a, b):
    return jnp.dot(a, b, preferred_element_type=F32)


def dot_nt(a, b):
    return lax.dot_general(a, b, (((1,), (1,)), ((), ())), preferred_element_type=F32)


def dot_tn(a, b):
    return lax.dot_general(a, b, (((0,), (0,)), ((), ())), preferred_element_type=F32)


def frame_spans(frames):
    spans = []
    for tap in (1, 0, 2):
        off = tap - 1
        count = frames - abs(off)
        if count > 0:
            spans.append((tap, max(0, -off), max(0, off), count))
    return spans


def near_frames(cell, frames):
    frame = cell % frames
    near = [cell + t for t in (-1, 0, 1) if 0 <= frame + t < frames]
    return near, near[0] - cell + 1


class Copies:
    def __init__(self, sems):
        self.sems, self.count = sems, 0

    def start(self, src, dst):
        copy = pltpu.make_async_copy(src, dst, self.sems.at[self.count])
        self.count += 1
        copy.start()
        return copy


def first_kernel(frames, x_hbm, w_hbm, low_hbm, high_hbm, inner_hbm, edge_hbm, up_hbm, down_hbm, x_ref, w_buf, acc, inner, edge, up, down, low_row, high_row, sems):
    cells, rows, cols, depth = x_ref.shape
    out = w_buf.shape[-1]
    clips = cells // frames
    spans = frame_spans(frames)
    copies = Copies(sems)
    load_x = copies.start(x_hbm, x_ref)
    loads = {}
    for tap, _, _, _ in spans:
        for tap_h in (1, 0, 2):
            loads[tap, tap_h] = copies.start(w_hbm.at[tap, tap_h], w_buf.at[tap, tap_h])
    borders = []
    for k, row, fine_row in ((0, 0, 0), (1, rows - 1, 2 * rows - 1)):
        borders.append(copies.start(low_hbm.at[:, row], low_row.at[k]))
        borders.append(copies.start(high_hbm.at[:, fine_row], high_row.at[k]))
    for tap_w in range(3):
        acc[tap_w, :, 0:1] = jnp.zeros((cells, 1, cols, out), F32)
        acc[tap_w, :, rows + 1 : rows + 2] = jnp.zeros((cells, 1, cols, out), F32)
    load_x.wait()
    for tap, to, src, count in spans:
        for tap_h in (1, 0, 2):
            loads[tap, tap_h].wait()
            at = 2 - tap_h
            for tap_w in range(3):
                weight = w_buf[tap, tap_h, tap_w]
                for clip in range(clips):
                    first = clip * frames
                    rowset = x_ref[first + src : first + src + count].reshape(-1, depth)
                    product = dot(rowset, weight).reshape(count, rows, cols, out)
                    spot = (tap_w, pl.ds(first + to, count), pl.ds(at, rows))
                    if tap == 1 and tap_h == 1:
                        acc[spot] = product
                    else:
                        acc[spot] = acc[spot] + product

    def gathered(cell, row):
        return acc[1, cell, row] + shift_cols(acc[0, cell, row], 1) + shift_cols(acc[2, cell, row], -1)

    for copy in borders:
        copy.wait()
    low_ch, high_ch = low_row.shape[-1], high_row.shape[-1]
    for k, packet in ((0, up), (1, down)):
        for cell in range(cells):
            for j in range(2):
                value = gathered(cell, k * rows + j)
                edge[k, cell, j] = value
                packet[cell, j, :, 0:out] = value.astype(BF16)
            packet[cell, 2, :, 0:low_ch] = low_row[k, cell]
            packet[cell, 3, :, 0:high_ch] = high_row[k, cell, 0:cols]
            packet[cell, 3, :, high_ch : 2 * high_ch] = high_row[k, cell, cols:]
    stores = [copies.start(up, up_hbm), copies.start(down, down_hbm), copies.start(edge, edge_hbm)]
    for cell in range(cells):

        def gather(row, _, cell=cell):
            inner[cell, row] = gathered(cell, row + 2).astype(BF16)
            return 0

        lax.fori_loop(0, rows - 2, gather, 0)
    stores.append(copies.start(inner, inner_hbm))
    for copy in stores:
        copy.wait()


def phase_weights(w_ref, wc_ref):
    depth = w_ref.shape[-2]
    chunk = 16
    for tap in range(3):

        def body(step, _, tap=tap):
            rows = pl.ds(pl.multiple_of(step * chunk, chunk), chunk)
            taps = [[w_ref[tap, h, w, rows].astype(F32) for w in range(3)] for h in range(3)]
            for p in range(2):
                if p == 0:
                    merged = (taps[0], [taps[1][w] + taps[2][w] for w in range(3)])
                else:
                    merged = ([taps[0][w] + taps[1][w] for w in range(3)], taps[2])
                for a in range(2):
                    m = merged[a]
                    wc_ref[p, 0, tap, a, 0, rows] = m[0].astype(BF16)
                    wc_ref[p, 0, tap, a, 1, rows] = (m[1] + m[2]).astype(BF16)
                    wc_ref[p, 1, tap, a, 0, rows] = (m[0] + m[1]).astype(BF16)
                    wc_ref[p, 1, tap, a, 1, rows] = m[2].astype(BF16)
            return 0

        lax.fori_loop(0, depth // chunk, body, 0)


def gate_rows(feature):
    gated = silu(feature)
    return shift_cols(gated, 1).astype(BF16), gated.astype(BF16), shift_cols(gated, -1).astype(BF16)


def second_feature(frames, gated, wc_ref, count, fine):
    _, groups, cells, _, cols, out = gated.shape
    for cell in range(cells):
        near, first_tap = near_frames(cell, frames)
        for p in range(2):
            for q in range(2):
                field = jnp.concatenate(
                    [
                        gated[q + b, :, other, p + a : p + a + count].reshape(groups * count * cols, out)
                        for other in near
                        for a in range(2)
                        for b in range(2)
                    ],
                    axis=1,
                )
                weight = wc_ref[p, q, first_tap : first_tap + len(near)].reshape(-1, out)
                product = dot(field, weight).reshape(groups, count, cols, out)
                for group in range(groups):
                    for row in range(count):
                        for block in range(out // 128):
                            fine[group, cell, row, p, block, pl.ds(q, cols, stride=2), :] = product[
                                group, row, :, 128 * block : 128 * block + 128
                            ]


def depthwise(frames, padded, kernel_ref, student):
    cells, rows, _, channels = student.shape
    for cell in range(cells):
        near, first_tap = near_frames(cell, frames)
        for lane in range(0, channels, 128):
            lanes = pl.ds(lane, 128)

            def body(row, _, cell=cell, near=near, first_tap=first_tap, lanes=lanes):
                sums = [None, None, None]
                for t, other in enumerate(near):
                    for h in range(3):
                        field = padded[other, row + h, :, lanes]
                        for w in range(3):
                            k = 9 * (t + first_tap) + 3 * h + w
                            term = field * kernel_ref[k : k + 1, lanes]
                            sums[w] = term if sums[w] is None else sums[w] + term
                student[cell, row, :, lanes] = (
                    padded[cell, row + 1, :, lanes]
                    + sums[1]
                    + shift_cols(sums[0], 1)
                    + shift_cols(sums[2], -1)
                ).astype(BF16)
                return 0

            lax.fori_loop(0, rows, body, 0)


def kernel_gradient(frames, padded, back, total, first):
    cells, rows, _, channels = back.shape
    for lane in range(0, channels, 128):
        lanes = pl.ds(lane, 128)
        sums = tuple(jnp.zeros((8, 128), F32) for _ in range(27))
        for cell in range(cells):
            near, first_tap = near_frames(cell, frames)

            def body(row, sums, cell=cell, near=near, first_tap=first_tap, lanes=lanes):
                sums = list(sums)
                center = back[cell, row, :, lanes]
                moved = (shift_cols(center, -1), center, shift_cols(center, 1))
                for t, other in enumerate(near):
                    for h in range(3):
                        field = padded[other, row + h, :, lanes]
                        for w in range(3):
                            k = 9 * (t + first_tap) + 3 * h + w
                            term = (moved[w] * field).reshape(-1, 8, 128)
                            sums[k] = sums[k] + jnp.sum(term, axis=0)
                return tuple(sums)

            sums = lax.fori_loop(0, rows, body, sums)
        for k in range(27):
            value = jnp.sum(sums[k], axis=0, keepdims=True)
            total[k : k + 1, lanes] = value if first else total[k : k + 1, lanes] + value


def level(student, target, adapter, scale, back, grad):
    mismatch = dot(student, adapter) - target
    residual = (mismatch * scale).astype(BF16)
    grad[...] += dot_tn(student, residual)
    return mismatch, dot_nt(residual, adapter)


def fine_target(fine, rows):
    blocks = fine.shape[2]
    value = jnp.concatenate([fine[rows, :, block].reshape(-1, 128) for block in range(blocks)], axis=1)
    return value.astype(BF16).astype(F32)


def second_kernel(
    frames, scale_low, scale_high,
    inner_hbm, w_hbm, low_hbm, high_hbm, klow_hbm, khigh_hbm, plow_hbm, phigh_hbm,
    wc_hbm, mismatch_hbm, glow_hbm, ghigh_hbm, gklow_hbm, gkhigh_hbm,
    feature, w_ref, low, high, klow, khigh, plow, phigh,
    wc, mismatch, glow, ghigh, gklow, gkhigh,
    gated, fine, low_pad, high_pad, low_student, high_student, low_back, high_back, sems,
):
    cells, count, cols, out = feature.shape
    rows = count + 2
    inner = rows - 4
    copies = Copies(sems)
    load_high = copies.start(high_hbm.at[:, pl.ds(3, 2 * inner + 2)], high)
    load_khigh = copies.start(khigh_hbm, khigh)
    load_w = copies.start(w_hbm, w_ref)
    load_low = copies.start(low_hbm, low)
    load_klow = copies.start(klow_hbm, klow)
    load_inner = copies.start(inner_hbm, feature)
    load_plow = copies.start(plow_hbm, plow)
    load_phigh = copies.start(phigh_hbm, phigh)

    load_high.wait()
    load_khigh.wait()
    for cell in range(cells):

        def widen_high(row, _, cell=cell):
            high_pad[cell, row] = high[cell, row].astype(F32)
            return 0

        lax.fori_loop(0, 2 * inner + 2, widen_high, 0)
    depthwise(frames, high_pad, khigh, high_student)
    load_low.wait()
    load_klow.wait()
    for cell in range(cells):

        def widen_low(row, _, cell=cell):
            low_pad[cell, row] = low[cell, row].astype(F32)
            return 0

        lax.fori_loop(0, rows, widen_low, 0)
    depthwise(frames, low_pad, klow, low_student)

    load_w.wait()
    phase_weights(w_ref, wc)
    stores = [copies.start(wc, wc_hbm)]

    load_inner.wait()
    for cell in range(cells):

        def gate(row, _, cell=cell):
            for k, value in enumerate(gate_rows(feature[cell, row].astype(F32))):
                gated[k, 0, cell, row] = value
            return 0

        lax.fori_loop(0, count, gate, 0)
    second_feature(frames, gated, wc, inner, fine)

    load_plow.wait()
    load_phigh.wait()
    glow[...] = jnp.zeros_like(glow)
    ghigh[...] = jnp.zeros_like(ghigh)
    gklow[...] = jnp.zeros_like(gklow)
    gkhigh[...] = jnp.zeros_like(gkhigh)
    for cell in range(cells):
        for row in range(0, inner, 2):
            here = slice(2 * row, 2 * row + 4)
            student = high_student[cell, here].reshape(-1, high.shape[-1])
            target = fine_target(fine.at[0, cell], slice(row, row + 2))
            value, back = level(student, target, phigh[...], scale_high, high_back, ghigh)
            mismatch[cell, here] = value.astype(BF16).reshape(4, 2 * cols, out)
            high_back[cell, here] = back.reshape(4, 2 * cols, -1)
    stores.append(copies.start(mismatch, mismatch_hbm.at[:, pl.ds(4, 2 * inner)]))
    stores.append(copies.start(ghigh, ghigh_hbm))
    for cell in range(cells):
        student = low_student[cell].reshape(-1, low.shape[-1])
        target = feature[cell].reshape(-1, out).astype(F32)
        _, back = level(student, target, plow[...], scale_low, low_back, glow)
        low_back[cell] = back.reshape(count, cols, -1)
    stores.append(copies.start(glow, glow_hbm))
    kernel_gradient(frames, low_pad, low_back, gklow, True)
    kernel_gradient(frames, high_pad, high_back, gkhigh, True)
    stores.append(copies.start(gklow, gklow_hbm))
    stores.append(copies.start(gkhigh, gkhigh_hbm))
    for copy in stores:
        copy.wait()


def third_kernel(
    frames, shards, scale_low, scale_high,
    place, above_hbm, below_hbm, edge_hbm, inner_hbm, low_hbm, high_hbm, klow_hbm, khigh_hbm, plow_hbm, phigh_hbm,
    wc_hbm, glow_hbm, ghigh_hbm, gklow_hbm, gkhigh_hbm, mismatch_in,
    mismatch_hbm, keep_hbm, send_hbm,
    packets, edge, inside, low, high, klow, khigh, plow, phigh, wc, glow, ghigh, gklow, gkhigh,
    mismatch, keep, send,
    feature, gated, fine, low_pad, high_pad, low_student, high_student, low_back, high_back, shard_sums, sems,
):
    del mismatch_in
    _, cells, _, cols, out = edge.shape
    rows = inner_hbm.shape[1] + 2
    low_ch, high_ch = low.shape[-1], high.shape[-1]
    mine = place[0]
    copies = Copies(sems)
    loads = [
        copies.start(above_hbm, packets.at[0]),
        copies.start(below_hbm, packets.at[1]),
        copies.start(high_hbm.at[:, pl.ds(0, 5)], high.at[0]),
        copies.start(high_hbm.at[:, pl.ds(2 * rows - 5, 5)], high.at[1]),
        copies.start(low_hbm.at[:, pl.ds(0, 2)], low.at[0]),
        copies.start(low_hbm.at[:, pl.ds(rows - 2, 2)], low.at[1]),
        copies.start(khigh_hbm, khigh),
        copies.start(klow_hbm, klow),
        copies.start(edge_hbm, edge),
        copies.start(inner_hbm.at[:, pl.ds(0, 2)], inside.at[0]),
        copies.start(inner_hbm.at[:, pl.ds(rows - 4, 2)], inside.at[1]),
    ]
    load_wc = copies.start(wc_hbm, wc)
    late = [
        copies.start(plow_hbm, plow),
        copies.start(phigh_hbm, phigh),
        copies.start(glow_hbm, glow),
        copies.start(ghigh_hbm, ghigh),
        copies.start(gklow_hbm, gklow),
        copies.start(gkhigh_hbm, gkhigh),
    ]
    for copy in loads:
        copy.wait()

    for side in range(2):
        for cell in range(cells):
            halo = packets.at[side, cell]
            at = 0 if side == 0 else 2
            low_pad[side, cell, at] = halo[2, :, 0:low_ch].astype(F32)
            low_pad[side, cell, pl.ds(1 - side, 2)] = low[side, cell].astype(F32)
            at = 0 if side == 0 else 5
            high_pad[side, cell, at, 0:cols] = halo[3, :, 0:high_ch].astype(F32)
            high_pad[side, cell, at, cols:] = halo[3, :, high_ch : 2 * high_ch].astype(F32)
            high_pad[side, cell, pl.ds(1 - side, 5)] = high[side, cell].astype(F32)
        depthwise(frames, high_pad.at[side], khigh, high_student.at[side])
        depthwise(frames, low_pad.at[side], klow, low_student.at[side])

    for side in range(2):
        for cell in range(cells):
            for k in range(2):
                whole = (edge[side, cell, k] + packets[side, cell, k, :, 0:out].astype(F32)).astype(BF16).astype(F32)
                if k == side:
                    whole = jnp.where(jnp.full(whole.shape, place[1 + side]) == 0, whole, 0.0)
                else:
                    feature[side, cell] = whole
                for j, value in enumerate(gate_rows(whole)):
                    gated[j, side, cell, 2 * side + k] = value
                for j, value in enumerate(gate_rows(inside[side, cell, k].astype(F32))):
                    gated[j, side, cell, 2 - 2 * side + k] = value

    for copy in late:
        copy.wait()
    student = low_student[...].reshape(-1, low_ch)
    _, back = level(student, feature[...].reshape(-1, out), plow[...], scale_low, low_back, glow)
    low_back[...] = back.reshape(low_back.shape)
    for side in range(2):
        kernel_gradient(frames, low_pad.at[side], low_back.at[side], gklow, False)

    load_wc.wait()
    second_feature(frames, gated, wc, 2, fine)
    for side in range(2):
        for cell in range(cells):
            student = high_student[side, cell].reshape(-1, high_ch)
            target = fine_target(fine.at[side, cell], slice(0, 2))
            value, back = level(student, target, phigh[...], scale_high, high_back, ghigh)
            mismatch[side, cell] = value.astype(BF16).reshape(4, 2 * cols, out)
            high_back[side, cell] = back.reshape(4, 2 * cols, high_ch)
    stores = [
        copies.start(mismatch.at[0], mismatch_hbm.at[:, pl.ds(0, 4)]),
        copies.start(mismatch.at[1], mismatch_hbm.at[:, pl.ds(2 * rows - 4, 4)]),
    ]
    for side in range(2):
        kernel_gradient(frames, high_pad.at[side], high_back.at[side], gkhigh, False)

    low_rows, high_rows = low_ch // shards, high_ch // shards
    shard_sums[...] = jnp.zeros_like(shard_sums)
    width = gklow.shape[1]
    lane = lax.broadcasted_iota(jnp.int32, gklow.shape, 1)
    wide_high = gkhigh[...]
    if high_ch < width:
        wide_high = jnp.concatenate([wide_high, jnp.zeros((wide_high.shape[0], width - high_ch), F32)], axis=1)
    for s in range(shards):
        shard_sums[s, 0:low_rows, 0:out] = glow[s * low_rows : (s + 1) * low_rows]
        shard_sums[s, low_rows : low_rows + high_rows, 0:out] = ghigh[s * high_rows : (s + 1) * high_rows]
        from_low = pltpu.roll(gklow[...], (width - s * low_rows) % width, 1)
        from_high = pltpu.roll(wide_high, (width + low_rows - s * high_rows) % width, 1)
        both = jnp.where(lane < low_rows, from_low, jnp.where(lane < low_rows + high_rows, from_high, 0.0))
        shard_sums[s, low_rows + high_rows : low_rows + high_rows + 32, 0:width] = both
    if shards == 1:
        keep[0] = shard_sums[0]
        send[0] = shard_sums[0].astype(BF16)
    else:
        bit = lax.rem(mine, 2)
        for k in range(shards // 2):
            keep[k] = shard_sums[2 * k + bit]
            send[k] = shard_sums[2 * k + 1 - bit].astype(BF16)
    stores.append(copies.start(send, send_hbm))
    stores.append(copies.start(keep, keep_hbm))
    for copy in stores:
        copy.wait()


def pairs(count, bit):
    return [(i, i ^ bit) for i in range(count)]


def sum_over_devices(keep, send, clips, tiles):
    if clips > 1:
        mine = lax.axis_index("clip")
        keep = keep + lax.ppermute(send, "clip", pairs(clips, 1)).astype(F32)
        bit = 2
        while bit < clips:
            halves = keep.reshape((keep.shape[0] // 2, 2) + keep.shape[1:])
            own = lax.rem(lax.div(mine, bit), 2)
            send = lax.dynamic_index_in_dim(halves, 1 - own, 1, False).astype(BF16)
            keep = lax.dynamic_index_in_dim(halves, own, 1, False)
            keep = keep + lax.ppermute(send, "clip", pairs(clips, bit)).astype(F32)
            bit *= 2
    total = keep[0]
    bit = 1
    while bit < tiles:
        bits = (bit, 2 * bit, 3 * bit) if 2 * bit < tiles else (bit,)
        out = total.astype(BF16)
        got = [lax.ppermute(out, "space", pairs(tiles, b)) for b in bits]
        for part in got:
            total = total + part.astype(F32)
        bit *= 2 ** (2 if len(bits) > 1 else 1)
    return total


def on_device(teacher_input, conv_first, conv_second, student_low, student_high, kernel_low, kernel_high, adapter_low, adapter_high):
    clips, tiles = lax.axis_size("clip"), lax.axis_size("space")
    held, frames, rows, cols, depth = teacher_input.shape
    cells = held * frames
    out = conv_first.shape[-1]
    low_ch, high_ch = student_low.shape[-1], student_high.shape[-1]
    low_count = held * frames * rows * cols * clips * tiles
    scales = (1.0 / low_count, 1.0 / (4 * low_count))
    inner = rows - 4
    x = teacher_input.reshape(cells, rows, cols, depth)
    low = student_low.reshape(cells, rows, cols, low_ch)
    high = student_high.reshape(cells, 2 * rows, 2 * cols, high_ch)
    klow, khigh = kernel_low.reshape(27, low_ch), kernel_high.reshape(27, high_ch)
    sems = pltpu.SemaphoreType.DMA

    def hbm(shape, dtype):
        return pltpu.HBM(shape, dtype)

    def vm(*specs):
        return [pltpu.VMEM(shape, dtype) for shape, dtype in specs]

    packet = ((cells, 4, cols, max(out, low_ch, 2 * high_ch)), BF16)
    inner_spec = ((cells, rows - 2, cols, out), BF16)
    edge_spec = ((2, cells, 2, cols, out), F32)
    inner_feature, edge, up, down = pl.pallas_call(
        functools.partial(first_kernel, frames),
        out_shape=(hbm(*inner_spec), hbm(*edge_spec), hbm(*packet), hbm(*packet)),
        in_specs=[HBM] * 4,
        out_specs=(HBM,) * 4,
        scratch_shapes=vm(
            (x.shape, BF16),
            (conv_first.shape, BF16),
            ((3, cells, rows + 2, cols, out), F32),
            inner_spec,
            edge_spec,
            packet,
            packet,
            ((2, cells, cols, low_ch), BF16),
            ((2, cells, 2 * cols, high_ch), BF16),
        )
        + [sems((18,))],
        compiler_params=pltpu.CompilerParams(vmem_limit_bytes=56 * MIB),
        cost_estimate=pl.CostEstimate(flops=3 * 10**9, bytes_accessed=9 * 10**6, transcendentals=0),
        name="teacher_first",
    )(x, conv_first, low, high)

    forward = [(i, i + 1) for i in range(tiles - 1)]
    above = lax.ppermute(down, "space", forward)
    below = lax.ppermute(up, "space", [(b, a) for a, b in forward])

    wc_spec = ((2, 2, 3, 2, 2, out, out), BF16)
    grads = (((low_ch, out), F32), ((high_ch, out), F32), ((32, low_ch), F32), ((32, high_ch), F32))
    weights = (((27, low_ch), F32), ((27, high_ch), F32), (adapter_low.shape, BF16), (adapter_high.shape, BF16))
    wc, mismatch, *sums = pl.pallas_call(
        functools.partial(second_kernel, frames, *scales),
        out_shape=(hbm(*wc_spec), hbm((cells, 2 * rows, 2 * cols, out), BF16)) + tuple(hbm(*g) for g in grads),
        in_specs=[HBM] * 8,
        out_specs=(HBM,) * 6,
        scratch_shapes=vm(
            inner_spec,
            (conv_second.shape, BF16),
            (low.shape, BF16),
            ((cells, 2 * inner + 2, 2 * cols, high_ch), BF16),
            *weights,
            wc_spec,
            ((cells, 2 * inner, 2 * cols, out), BF16),
            *grads,
            ((3, 1, cells, rows - 2, cols, out), BF16),
            ((1, cells, inner, 2, out // 128, 2 * cols, 128), F32),
            ((cells, rows, cols, low_ch), F32),
            ((cells, 2 * inner + 2, 2 * cols, high_ch), F32),
            ((cells, rows - 2, cols, low_ch), BF16),
            ((cells, 2 * inner, 2 * cols, high_ch), BF16),
            ((cells, rows - 2, cols, low_ch), F32),
            ((cells, 2 * inner, 2 * cols, high_ch), F32),
        )
        + [sems((14,))],
        compiler_params=pltpu.CompilerParams(vmem_limit_bytes=56 * MIB),
        cost_estimate=pl.CostEstimate(flops=5 * 10**9, bytes_accessed=20 * 10**6, transcendentals=0),
        name="inner_rows",
    )(inner_feature, conv_second, low, high, klow, khigh, adapter_low, adapter_high)

    clip, tile = lax.axis_index("clip"), lax.axis_index("space")
    place = jnp.stack([clip, (tile == 0).astype(jnp.int32), (tile == tiles - 1).astype(jnp.int32)])
    shard_rows = low_ch // clips + high_ch // clips + 32
    shard_rows += -shard_rows % 16
    shard = (max(clips // 2, 1), shard_rows, out)
    mismatch, keep, send = pl.pallas_call(
        functools.partial(third_kernel, frames, clips, *scales),
        out_shape=(hbm(mismatch.shape, BF16), hbm(shard, F32), hbm(shard, BF16)),
        in_specs=[pl.BlockSpec(memory_space=pltpu.SMEM)] + [HBM] * 16,
        out_specs=(HBM,) * 3,
        input_output_aliases={16: 0},
        scratch_shapes=vm(
            ((2,) + packet[0], BF16),
            edge_spec,
            ((2, cells, 2, cols, out), BF16),
            ((2, cells, 2, cols, low_ch), BF16),
            ((2, cells, 5, 2 * cols, high_ch), BF16),
            *weights,
            wc_spec,
            *grads,
            ((2, cells, 4, 2 * cols, out), BF16),
            (shard, F32),
            (shard, BF16),
            ((2, cells, cols, out), F32),
            ((3, 2, cells, 4, cols, out), BF16),
            ((2, cells, 2, 2, out // 128, 2 * cols, 128), F32),
            ((2, cells, 3, cols, low_ch), F32),
            ((2, cells, 6, 2 * cols, high_ch), F32),
            ((2, cells, 1, cols, low_ch), BF16),
            ((2, cells, 4, 2 * cols, high_ch), BF16),
            ((2, cells, 1, cols, low_ch), F32),
            ((2, cells, 4, 2 * cols, high_ch), F32),
            ((clips, shard_rows, out), F32),
        )
        + [sems((22,))],
        compiler_params=pltpu.CompilerParams(vmem_limit_bytes=56 * MIB),
        cost_estimate=pl.CostEstimate(flops=3 * 10**9, bytes_accessed=20 * 10**6, transcendentals=0),
        name="border_rows",
    )(place, above, below, edge, inner_feature, low, high, klow, khigh, adapter_low, adapter_high, wc, *sums, mismatch)

    total = sum_over_devices(keep, send, clips, tiles)
    low_rows, high_rows = low_ch // clips, high_ch // clips
    top = low_rows + high_rows
    return (
        total[:low_rows],
        total[top : top + 27, :low_rows].reshape(3, 3, 3, low_rows),
        total[low_rows:top],
        total[top : top + 27, low_rows : low_rows + high_rows].reshape(3, 3, 3, high_rows),
        mismatch.reshape(held, frames, 2 * rows, 2 * cols, out),
    )


def solution(mesh):
    tiled = P("clip", None, "space", None, None)
    return jax.shard_map(
        on_device,
        mesh=mesh,
        in_specs=(tiled, P(), P(), tiled, tiled, P(), P(), P(), P()),
        out_specs=(P("clip", None), P(None, None, None, "clip"), P("clip", None), P(None, None, None, "clip"), tiled),
        check_vma=False,
    )
```

```python
import functools

import jax
import jax.numpy as jnp
from jax import lax
from jax.experimental import pallas as pl
from jax.experimental.pallas import tpu as pltpu
from jax.sharding import PartitionSpec as P

F32, BF16 = jnp.float32, jnp.bfloat16
HBM = pl.BlockSpec(memory_space=pltpu.HBM)
VMEM = pl.BlockSpec(memory_space=pltpu.VMEM)
MIB = 1 << 20


def in_hbm(*arrays):
    return [pltpu.with_memory_space_constraint(array, pltpu.HBM) for array in arrays]


def shift_cols(value, by):
    axis = value.ndim - 2
    count = value.shape[axis]
    column = lax.broadcasted_iota(jnp.int32, value.shape, axis)
    edge = 0 if by > 0 else count - 1
    return jnp.where(column == edge, 0.0, pltpu.roll(value, by % count, axis))


def silu(value):
    return value / (1.0 + jnp.exp(-value))


def dot(a, b):
    return jnp.dot(a, b, preferred_element_type=F32)


def dot_nt(a, b):
    return lax.dot_general(a, b, (((1,), (1,)), ((), ())), preferred_element_type=F32)


def dot_tn(a, b):
    return lax.dot_general(a, b, (((0,), (0,)), ((), ())), preferred_element_type=F32)


def frame_spans(frames):
    spans = []
    for tap in (1, 0, 2):
        off = tap - 1
        count = frames - abs(off)
        if count > 0:
            spans.append((tap, max(0, -off), max(0, off), count))
    return spans


def near_frames(cell, frames):
    frame = cell % frames
    near = [cell + t for t in (-1, 0, 1) if 0 <= frame + t < frames]
    return near, near[0] - cell + 1


class Copies:
    def __init__(self, sems):
        self.sems, self.count = sems, 0

    def start(self, src, dst):
        copy = pltpu.make_async_copy(src, dst, self.sems.at[self.count])
        self.count += 1
        copy.start()
        return copy


def first_kernel(frames, x_hbm, w_hbm, low_hbm, high_hbm, inner, edge, first, second, x_ref, w_buf, acc, low_row, high_row, sems):
    cells, rows, cols, depth = x_ref.shape
    out = w_buf.shape[-1]
    clips = cells // frames
    spans = frame_spans(frames)
    copies = Copies(sems)
    load_x = copies.start(x_hbm, x_ref)
    loads = {}
    for tap, _, _, _ in spans:
        for tap_h in (1, 0, 2):
            loads[tap, tap_h] = copies.start(w_hbm.at[tap, tap_h], w_buf.at[tap, tap_h])
    borders = []
    for k, row, fine_row in ((0, 0, 0), (1, rows - 1, 2 * rows - 1)):
        borders.append(copies.start(low_hbm.at[:, row], low_row.at[k]))
        borders.append(copies.start(high_hbm.at[:, fine_row], high_row.at[k]))
    for tap_w in range(3):
        acc[tap_w, :, 0:1] = jnp.zeros((cells, 1, cols, out), F32)
        acc[tap_w, :, rows + 1 : rows + 2] = jnp.zeros((cells, 1, cols, out), F32)
    load_x.wait()
    for tap, to, src, count in spans:
        for tap_h in (1, 0, 2):
            loads[tap, tap_h].wait()
            at = 2 - tap_h
            for tap_w in range(3):
                weight = w_buf[tap, tap_h, tap_w]
                for clip in range(clips):
                    base = clip * frames
                    rowset = x_ref[base + src : base + src + count].reshape(-1, depth)
                    product = dot(rowset, weight).reshape(count, rows, cols, out)
                    spot = (tap_w, pl.ds(base + to, count), pl.ds(at, rows))
                    if tap == 1 and tap_h == 1:
                        acc[spot] = product
                    else:
                        acc[spot] = acc[spot] + product

    def gathered(cell, row):
        return acc[1, cell, row] + shift_cols(acc[0, cell, row], 1) + shift_cols(acc[2, cell, row], -1)

    for copy in borders:
        copy.wait()
    low_ch, high_ch = low_row.shape[-1], high_row.shape[-1]
    even = lax.rem(lax.axis_index("space"), 2) == 0
    for cell in range(cells):
        for j in range(2):
            up, down = gathered(cell, j), gathered(cell, rows + j)
            edge[0, cell, j], edge[1, cell, j] = up, down
            first[cell, j, :, 0:out] = jnp.where(even, down, up).astype(BF16)
            second[cell, j, :, 0:out] = jnp.where(even, up, down).astype(BF16)
        up, down = low_row[0, cell].astype(F32), low_row[1, cell].astype(F32)
        first[cell, 2, :, 0:low_ch] = jnp.where(even, down, up).astype(BF16)
        second[cell, 2, :, 0:low_ch] = jnp.where(even, up, down).astype(BF16)
        for half in range(2):
            here, lanes = slice(half * cols, (half + 1) * cols), slice(half * high_ch, (half + 1) * high_ch)
            up, down = high_row[0, cell, here].astype(F32), high_row[1, cell, here].astype(F32)
            first[cell, 3, :, lanes] = jnp.where(even, down, up).astype(BF16)
            second[cell, 3, :, lanes] = jnp.where(even, up, down).astype(BF16)
    for cell in range(cells):

        def gather(row, _, cell=cell):
            inner[cell, row] = gathered(cell, row + 2).astype(BF16)
            return 0

        lax.fori_loop(0, rows - 2, gather, 0)


def phase_weights(w_ref, wc_ref):
    depth = w_ref.shape[-2]
    chunk = 16
    for tap in range(3):

        def body(step, _, tap=tap):
            rows = pl.ds(pl.multiple_of(step * chunk, chunk), chunk)
            taps = [[w_ref[tap, h, w, rows].astype(F32) for w in range(3)] for h in range(3)]
            for p in range(2):
                if p == 0:
                    merged = (taps[0], [taps[1][w] + taps[2][w] for w in range(3)])
                else:
                    merged = ([taps[0][w] + taps[1][w] for w in range(3)], taps[2])
                for a in range(2):
                    m = merged[a]
                    wc_ref[p, 0, tap, a, 0, rows] = m[0].astype(BF16)
                    wc_ref[p, 0, tap, a, 1, rows] = (m[1] + m[2]).astype(BF16)
                    wc_ref[p, 1, tap, a, 0, rows] = (m[0] + m[1]).astype(BF16)
                    wc_ref[p, 1, tap, a, 1, rows] = m[2].astype(BF16)
            return 0

        lax.fori_loop(0, depth // chunk, body, 0)


def gate_rows(feature):
    gated = silu(feature)
    return shift_cols(gated, 1).astype(BF16), gated.astype(BF16), shift_cols(gated, -1).astype(BF16)


def second_feature(frames, gated, wc_ref, count, fine):
    _, groups, cells, _, cols, out = gated.shape
    for cell in range(cells):
        near, first_tap = near_frames(cell, frames)
        for p in range(2):
            for q in range(2):
                field = jnp.concatenate(
                    [
                        gated[q + b, :, other, p + a : p + a + count].reshape(groups * count * cols, out)
                        for other in near
                        for a in range(2)
                        for b in range(2)
                    ],
                    axis=1,
                )
                weight = wc_ref[p, q, first_tap : first_tap + len(near)].reshape(-1, out)
                product = dot(field, weight).reshape(groups, count, cols, out)
                for group in range(groups):
                    for row in range(count):
                        for block in range(out // 128):
                            fine[group, cell, row, p, block, pl.ds(q, cols, stride=2), :] = product[
                                group, row, :, 128 * block : 128 * block + 128
                            ]


def depthwise(frames, padded, kernel_ref, student):
    cells, rows, _, channels = student.shape
    for cell in range(cells):
        near, first_tap = near_frames(cell, frames)
        for lane in range(0, channels, 128):
            lanes = pl.ds(lane, 128)

            def body(row, _, cell=cell, near=near, first_tap=first_tap, lanes=lanes):
                sums = [None, None, None]
                for t, other in enumerate(near):
                    for h in range(3):
                        field = padded[other, row + h, :, lanes]
                        for w in range(3):
                            term = field * kernel_ref[t + first_tap, h, w : w + 1, lanes]
                            sums[w] = term if sums[w] is None else sums[w] + term
                student[cell, row, :, lanes] = (
                    padded[cell, row + 1, :, lanes]
                    + sums[1]
                    + shift_cols(sums[0], 1)
                    + shift_cols(sums[2], -1)
                ).astype(BF16)
                return 0

            lax.fori_loop(0, rows, body, 0)


def kernel_gradient(frames, padded, back, total, first):
    cells, rows, _, channels = back.shape
    for lane in range(0, channels, 128):
        lanes = pl.ds(lane, 128)
        sums = tuple(jnp.zeros((8, 128), F32) for _ in range(27))
        for cell in range(cells):
            near, first_tap = near_frames(cell, frames)

            def body(row, sums, cell=cell, near=near, first_tap=first_tap, lanes=lanes):
                sums = list(sums)
                center = back[cell, row, :, lanes]
                moved = (shift_cols(center, -1), center, shift_cols(center, 1))
                for t, other in enumerate(near):
                    for h in range(3):
                        field = padded[other, row + h, :, lanes]
                        for w in range(3):
                            k = 9 * (t + first_tap) + 3 * h + w
                            term = (moved[w] * field).reshape(-1, 8, 128)
                            sums[k] = sums[k] + jnp.sum(term, axis=0)
                return tuple(sums)

            sums = lax.fori_loop(0, rows, body, sums)
        for k in range(27):
            value = jnp.sum(sums[k], axis=0, keepdims=True)
            total[k : k + 1, lanes] = value if first else total[k : k + 1, lanes] + value


def level(student, target, adapter, scale, back, grad):
    mismatch = dot(student, adapter) - target
    residual = (mismatch * scale).astype(BF16)
    grad[...] += dot_tn(student, residual)
    return mismatch, dot_nt(residual, adapter)


def fine_target(fine, rows):
    blocks = fine.shape[2]
    value = jnp.concatenate([fine[rows, :, block].reshape(-1, 128) for block in range(blocks)], axis=1)
    return value.astype(BF16).astype(F32)


def second_kernel(
    frames, scale_low, scale_high,
    feature, w_hbm, low_hbm, high_hbm, klow_hbm, khigh_hbm, plow_hbm, phigh_hbm,
    wc, mismatch_hbm, glow, ghigh, gklow, gkhigh,
    w_ref, low, high, klow, khigh, plow, phigh, mismatch,
    gated, fine, low_pad, high_pad, low_student, high_student, low_back, high_back, sems,
):
    cells, count, cols, out = feature.shape
    rows = count + 2
    inner = rows - 4
    copies = Copies(sems)
    load_high = copies.start(high_hbm.at[:, pl.ds(3, 2 * inner + 2)], high)
    load_khigh = copies.start(khigh_hbm, khigh)
    load_low = copies.start(low_hbm, low)
    load_klow = copies.start(klow_hbm, klow)
    load_w = copies.start(w_hbm, w_ref)
    load_plow = copies.start(plow_hbm, plow)
    load_phigh = copies.start(phigh_hbm, phigh)

    for cell in range(cells):

        def gate(row, _, cell=cell):
            for k, value in enumerate(gate_rows(feature[cell, row].astype(F32))):
                gated[k, 0, cell, row] = value
            return 0

        lax.fori_loop(0, count, gate, 0)

    load_high.wait()
    load_khigh.wait()
    for cell in range(cells):

        def widen_high(row, _, cell=cell):
            high_pad[cell, row] = high[cell, row].astype(F32)
            return 0

        lax.fori_loop(0, 2 * inner + 2, widen_high, 0)
    depthwise(frames, high_pad, khigh, high_student)
    load_low.wait()
    load_klow.wait()
    for cell in range(cells):

        def widen_low(row, _, cell=cell):
            low_pad[cell, row] = low[cell, row].astype(F32)
            return 0

        lax.fori_loop(0, rows, widen_low, 0)
    depthwise(frames, low_pad, klow, low_student)

    load_w.wait()
    phase_weights(w_ref, wc)
    second_feature(frames, gated, wc, inner, fine)

    load_plow.wait()
    load_phigh.wait()
    glow[...] = jnp.zeros_like(glow)
    ghigh[...] = jnp.zeros_like(ghigh)
    gklow[...] = jnp.zeros_like(gklow)
    gkhigh[...] = jnp.zeros_like(gkhigh)
    for cell in range(cells):
        for row in range(0, inner, 2):
            here = slice(2 * row, 2 * row + 4)
            student = high_student[cell, here].reshape(-1, high.shape[-1])
            target = fine_target(fine.at[0, cell], slice(row, row + 2))
            value, back = level(student, target, phigh[...], scale_high, high_back, ghigh)
            mismatch[cell, here] = value.astype(BF16).reshape(4, 2 * cols, out)
            high_back[cell, here] = back.reshape(4, 2 * cols, -1)
    store = copies.start(mismatch, mismatch_hbm.at[:, pl.ds(4, 2 * inner)])
    for cell in range(cells):
        student = low_student[cell].reshape(-1, low.shape[-1])
        target = feature[cell].reshape(-1, out).astype(F32)
        _, back = level(student, target, plow[...], scale_low, low_back, glow)
        low_back[cell] = back.reshape(count, cols, -1)
    kernel_gradient(frames, low_pad, low_back, gklow, True)
    kernel_gradient(frames, high_pad, high_back, gkhigh, True)
    store.wait()


def third_kernel(
    frames, shards, tiles, scale_low, scale_high,
    first, second, edge, inner, wc, glow_in, ghigh_in, gklow_in, gkhigh_in,
    low_hbm, high_hbm, klow_hbm, khigh_hbm, plow_hbm, phigh_hbm, mismatch_in,
    mismatch_hbm, keep, send,
    low, high, klow, khigh, plow, phigh, glow, ghigh, gklow, gkhigh, mismatch,
    feature, gated, fine, low_pad, high_pad, low_student, high_student, low_back, high_back, shard_sums, sems,
):
    del mismatch_in
    _, cells, _, cols, out = edge.shape
    rows = inner.shape[1] + 2
    low_ch, high_ch = low.shape[-1], high.shape[-1]
    mine, tile = lax.axis_index("clip"), lax.axis_index("space")
    even = lax.rem(tile, 2) == 0
    outside = (tile == 0, tile == tiles - 1)
    copies = Copies(sems)
    loads = [
        copies.start(high_hbm.at[:, pl.ds(0, 5)], high.at[0]),
        copies.start(high_hbm.at[:, pl.ds(2 * rows - 5, 5)], high.at[1]),
        copies.start(khigh_hbm, khigh),
        copies.start(low_hbm.at[:, pl.ds(0, 2)], low.at[0]),
        copies.start(low_hbm.at[:, pl.ds(rows - 2, 2)], low.at[1]),
        copies.start(klow_hbm, klow),
        copies.start(plow_hbm, plow),
        copies.start(phigh_hbm, phigh),
    ]
    for total, part in ((glow, glow_in), (ghigh, ghigh_in), (gklow, gklow_in), (gkhigh, gkhigh_in)):
        total[...] = part[...]

    def halo(side, cell, row):
        ours, other = first[cell, row].astype(F32), second[cell, row].astype(F32)
        return jnp.where(even, other, ours) if side == 0 else jnp.where(even, ours, other)

    for side in range(2):
        for cell in range(cells):
            for k in range(2):
                whole = (edge[side, cell, k] + halo(side, cell, k)[:, 0:out]).astype(BF16).astype(F32)
                if k == side:
                    whole = jnp.where(outside[side], 0.0, whole)
                else:
                    feature[side, cell] = whole
                for j, value in enumerate(gate_rows(whole)):
                    gated[j, side, cell, 2 * side + k] = value
                for j, value in enumerate(gate_rows(inner[cell, side * (rows - 4) + k].astype(F32))):
                    gated[j, side, cell, 2 - 2 * side + k] = value

    second_feature(frames, gated, wc, 2, fine)
    for copy in loads:
        copy.wait()

    for side in range(2):
        for cell in range(cells):
            low_halo, high_halo = halo(side, cell, 2), halo(side, cell, 3)
            at = 0 if side == 0 else 2
            low_pad[side, cell, at] = low_halo[:, 0:low_ch]
            low_pad[side, cell, pl.ds(1 - side, 2)] = low[side, cell].astype(F32)
            at = 0 if side == 0 else 5
            high_pad[side, cell, at, 0:cols] = high_halo[:, 0:high_ch]
            high_pad[side, cell, at, cols:] = high_halo[:, high_ch : 2 * high_ch]
            high_pad[side, cell, pl.ds(1 - side, 5)] = high[side, cell].astype(F32)
        depthwise(frames, high_pad.at[side], khigh, high_student.at[side])
        depthwise(frames, low_pad.at[side], klow, low_student.at[side])

    student = low_student[...].reshape(-1, low_ch)
    _, back = level(student, feature[...].reshape(-1, out), plow[...], scale_low, low_back, glow)
    low_back[...] = back.reshape(low_back.shape)
    for side in range(2):
        kernel_gradient(frames, low_pad.at[side], low_back.at[side], gklow, False)

    for side in range(2):
        for cell in range(cells):
            student = high_student[side, cell].reshape(-1, high_ch)
            target = fine_target(fine.at[side, cell], slice(0, 2))
            value, back = level(student, target, phigh[...], scale_high, high_back, ghigh)
            mismatch[side, cell] = value.astype(BF16).reshape(4, 2 * cols, out)
            high_back[side, cell] = back.reshape(4, 2 * cols, high_ch)
    stores = [
        copies.start(mismatch.at[0], mismatch_hbm.at[:, pl.ds(0, 4)]),
        copies.start(mismatch.at[1], mismatch_hbm.at[:, pl.ds(2 * rows - 4, 4)]),
    ]
    for side in range(2):
        kernel_gradient(frames, high_pad.at[side], high_back.at[side], gkhigh, False)

    low_rows, high_rows = low_ch // shards, high_ch // shards
    shard_sums[...] = jnp.zeros_like(shard_sums)
    width = gklow.shape[1]
    lane = lax.broadcasted_iota(jnp.int32, gklow.shape, 1)
    wide_high = gkhigh[...]
    if high_ch < width:
        wide_high = jnp.concatenate([wide_high, jnp.zeros((wide_high.shape[0], width - high_ch), F32)], axis=1)
    for s in range(shards):
        shard_sums[s, 0:low_rows, 0:out] = glow[s * low_rows : (s + 1) * low_rows]
        shard_sums[s, low_rows : low_rows + high_rows, 0:out] = ghigh[s * high_rows : (s + 1) * high_rows]
        from_low = pltpu.roll(gklow[...], (width - s * low_rows) % width, 1)
        from_high = pltpu.roll(wide_high, (width + low_rows - s * high_rows) % width, 1)
        both = jnp.where(lane < low_rows, from_low, jnp.where(lane < low_rows + high_rows, from_high, 0.0))
        shard_sums[s, low_rows + high_rows : low_rows + high_rows + 32, 0:width] = both
    if shards == 1:
        keep[0] = shard_sums[0]
        send[0] = shard_sums[0].astype(BF16)
    else:
        bit = lax.rem(mine, 2)
        for k in range(shards // 2):
            keep[k] = shard_sums[2 * k + bit]
            send[k] = shard_sums[2 * k + 1 - bit].astype(BF16)
    for copy in stores:
        copy.wait()


def swaps(start, count):
    lower = range(start, count - 1, 2)
    return [(i, i + 1) for i in lower] + [(i + 1, i) for i in lower]


def pairs(count, bit):
    return [(i, i ^ bit) for i in range(count)]


def sum_over_devices(keep, send, clips, tiles):
    if clips > 1:
        mine = lax.axis_index("clip")
        keep = keep + lax.ppermute(send, "clip", pairs(clips, 1)).astype(F32)
        bit = 2
        while bit < clips:
            halves = keep.reshape((keep.shape[0] // 2, 2) + keep.shape[1:])
            own = lax.rem(lax.div(mine, bit), 2)
            send = lax.dynamic_index_in_dim(halves, 1 - own, 1, False).astype(BF16)
            keep = lax.dynamic_index_in_dim(halves, own, 1, False)
            keep = keep + lax.ppermute(send, "clip", pairs(clips, bit)).astype(F32)
            bit *= 2
    total = keep[0]
    bit = 1
    while bit < tiles:
        bits = (bit, 2 * bit, 3 * bit) if 2 * bit < tiles else (bit,)
        out = total.astype(BF16)
        got = [lax.ppermute(out, "space", pairs(tiles, b)) for b in bits]
        bit *= 2 ** (2 if len(bits) > 1 else 1)
        if bit >= tiles:
            return total, got
        for part in got:
            total = total + part.astype(F32)
    return total, []


def unpack_kernel(total_ref, *refs):
    got, (glow, gklow, ghigh, gkhigh), sums = refs[:-5], refs[-5:-1], refs[-1]
    value = total_ref[...]
    for part in got:
        value = value + part[...].astype(F32)
    sums[...] = value
    low_rows, high_rows, out = glow.shape[0], ghigh.shape[0], glow.shape[1]
    top = low_rows + high_rows
    glow[...] = sums[0:low_rows, 0:out]
    ghigh[...] = sums[low_rows:top, 0:out]
    for t in range(3):
        for h in range(3):
            at = top + 9 * t + 3 * h
            gklow[t, h] = sums[at : at + 3, 0:low_rows]
            gkhigh[t, h] = sums[at : at + 3, low_rows:top]


def on_device(teacher_input, conv_first, conv_second, student_low, student_high, kernel_low, kernel_high, adapter_low, adapter_high):
    clips, tiles = lax.axis_size("clip"), lax.axis_size("space")
    held, frames, rows, cols, depth = teacher_input.shape
    cells = held * frames
    out = conv_first.shape[-1]
    low_ch, high_ch = student_low.shape[-1], student_high.shape[-1]
    low_count = held * frames * rows * cols * clips * tiles
    scales = (1.0 / low_count, 1.0 / (4 * low_count))
    inner = rows - 4
    x = teacher_input.reshape(cells, rows, cols, depth)
    low = student_low.reshape(cells, rows, cols, low_ch)
    high = student_high.reshape(cells, 2 * rows, 2 * cols, high_ch)
    sems = pltpu.SemaphoreType.DMA

    def vm(*specs):
        return [pltpu.VMEM(shape, dtype) for shape, dtype in specs]

    packet = ((cells, 4, cols, max(out, low_ch, 2 * high_ch)), BF16)
    inner_spec = ((cells, rows - 2, cols, out), BF16)
    edge_spec = ((2, cells, 2, cols, out), F32)
    inner_feature, edge, first, second = pl.pallas_call(
        functools.partial(first_kernel, frames),
        out_shape=tuple(vm(inner_spec, edge_spec, packet, packet)),
        in_specs=[HBM] * 4,
        out_specs=(VMEM,) * 4,
        scratch_shapes=vm(
            (x.shape, BF16),
            (conv_first.shape, BF16),
            ((3, cells, rows + 2, cols, out), F32),
            ((2, cells, cols, low_ch), BF16),
            ((2, cells, 2 * cols, high_ch), BF16),
        )
        + [sems((18,))],
        compiler_params=pltpu.CompilerParams(vmem_limit_bytes=20 * MIB),
        cost_estimate=pl.CostEstimate(flops=3 * 10**9, bytes_accessed=9 * 10**6, transcendentals=0),
        name="teacher_first",
    )(*in_hbm(x, conv_first, low, high))

    first_got = lax.ppermute(first, "space", swaps(0, tiles))
    second_got = lax.ppermute(second, "space", swaps(1, tiles))

    wc_spec = ((2, 2, 3, 2, 2, out, out), BF16)
    grads = (((low_ch, out), F32), ((high_ch, out), F32), ((32, low_ch), F32), ((32, high_ch), F32))
    weights = ((kernel_low.shape, F32), (kernel_high.shape, F32), (adapter_low.shape, BF16), (adapter_high.shape, BF16))
    wc, mismatch, *sums = pl.pallas_call(
        functools.partial(second_kernel, frames, *scales),
        out_shape=(*vm(wc_spec), pltpu.HBM((cells, 2 * rows, 2 * cols, out), BF16), *vm(*grads)),
        in_specs=[VMEM] + [HBM] * 7,
        out_specs=(VMEM, HBM) + (VMEM,) * 4,
        scratch_shapes=vm(
            (conv_second.shape, BF16),
            (low.shape, BF16),
            ((cells, 2 * inner + 2, 2 * cols, high_ch), BF16),
            *weights,
            ((cells, 2 * inner, 2 * cols, out), BF16),
            ((3, 1, cells, rows - 2, cols, out), BF16),
            ((1, cells, inner, 2, out // 128, 2 * cols, 128), F32),
            ((cells, rows, cols, low_ch), F32),
            ((cells, 2 * inner + 2, 2 * cols, high_ch), F32),
            ((cells, rows - 2, cols, low_ch), BF16),
            ((cells, 2 * inner, 2 * cols, high_ch), BF16),
            ((cells, rows - 2, cols, low_ch), F32),
            ((cells, 2 * inner, 2 * cols, high_ch), F32),
        )
        + [sems((14,))],
        compiler_params=pltpu.CompilerParams(vmem_limit_bytes=20 * MIB),
        cost_estimate=pl.CostEstimate(flops=5 * 10**9, bytes_accessed=20 * 10**6, transcendentals=0),
        name="inner_rows",
    )(inner_feature, *in_hbm(conv_second, low, high, kernel_low, kernel_high, adapter_low, adapter_high))

    shard_rows = low_ch // clips + high_ch // clips + 32
    shard_rows += -shard_rows % 16
    shard = (max(clips // 2, 1), shard_rows, out)
    mismatch, keep, send = pl.pallas_call(
        functools.partial(third_kernel, frames, clips, tiles, *scales),
        out_shape=(pltpu.HBM(mismatch.shape, BF16), *vm((shard, F32), (shard, BF16))),
        in_specs=[VMEM] * 9 + [HBM] * 7,
        out_specs=(HBM, VMEM, VMEM),
        input_output_aliases={15: 0},
        scratch_shapes=vm(
            ((2, cells, 2, cols, low_ch), BF16),
            ((2, cells, 5, 2 * cols, high_ch), BF16),
            *weights,
            *grads,
            ((2, cells, 4, 2 * cols, out), BF16),
            ((2, cells, cols, out), F32),
            ((3, 2, cells, 4, cols, out), BF16),
            ((2, cells, 2, 2, out // 128, 2 * cols, 128), F32),
            ((2, cells, 3, cols, low_ch), F32),
            ((2, cells, 6, 2 * cols, high_ch), F32),
            ((2, cells, 1, cols, low_ch), BF16),
            ((2, cells, 4, 2 * cols, high_ch), BF16),
            ((2, cells, 1, cols, low_ch), F32),
            ((2, cells, 4, 2 * cols, high_ch), F32),
            ((clips, shard_rows, out), F32),
        )
        + [sems((22,))],
        compiler_params=pltpu.CompilerParams(vmem_limit_bytes=20 * MIB),
        cost_estimate=pl.CostEstimate(flops=3 * 10**9, bytes_accessed=20 * 10**6, transcendentals=0),
        name="border_rows",
    )(first_got, second_got, edge, inner_feature, wc, *sums, *in_hbm(low, high, kernel_low, kernel_high, adapter_low, adapter_high, mismatch))

    total, got = sum_over_devices(keep, send, clips, tiles)
    low_rows, high_rows = low_ch // clips, high_ch // clips
    glow, gklow, ghigh, gkhigh = pl.pallas_call(
        unpack_kernel,
        out_shape=(
            jax.ShapeDtypeStruct((low_rows, out), F32),
            jax.ShapeDtypeStruct((3, 3, 3, low_rows), F32),
            jax.ShapeDtypeStruct((high_rows, out), F32),
            jax.ShapeDtypeStruct((3, 3, 3, high_rows), F32),
        ),
        in_specs=[VMEM] * (1 + len(got)),
        out_specs=(VMEM,) * 4,
        scratch_shapes=[pltpu.VMEM(shard[1:], F32)],
        compiler_params=pltpu.CompilerParams(vmem_limit_bytes=4 * MIB),
        name="unpack",
    )(total, *got)
    return glow, gklow, ghigh, gkhigh, mismatch.reshape(held, frames, 2 * rows, 2 * cols, out)


def solution(mesh):
    tiled = P("clip", None, "space", None, None)
    return jax.shard_map(
        on_device,
        mesh=mesh,
        in_specs=(tiled, P(), P(), tiled, tiled, P(), P(), P(), P()),
        out_specs=(P("clip", None), P(None, None, None, "clip"), P("clip", None), P(None, None, None, "clip"), tiled),
        check_vma=False,
    )
```

```python
import functools

import jax
import jax.numpy as jnp
from jax import lax
from jax.experimental import pallas as pl
from jax.experimental.pallas import tpu as pltpu
from jax.sharding import PartitionSpec as P

F32, BF16 = jnp.float32, jnp.bfloat16
HBM = pl.BlockSpec(memory_space=pltpu.HBM)
VMEM = pl.BlockSpec(memory_space=pltpu.VMEM)
MIB = 1 << 20


def in_hbm(*arrays):
    return [pltpu.with_memory_space_constraint(array, pltpu.HBM) for array in arrays]


def shift_cols(value, by):
    axis = value.ndim - 2
    count = value.shape[axis]
    column = lax.broadcasted_iota(jnp.int32, value.shape, axis)
    edge = 0 if by > 0 else count - 1
    return jnp.where(column == edge, 0.0, pltpu.roll(value, by % count, axis))


def silu(value):
    return value / (1.0 + jnp.exp(-value))


def dot(a, b):
    return jnp.dot(a, b, preferred_element_type=F32)


def dot_nt(a, b):
    return lax.dot_general(a, b, (((1,), (1,)), ((), ())), preferred_element_type=F32)


def dot_tn(a, b):
    return lax.dot_general(a, b, (((0,), (0,)), ((), ())), preferred_element_type=F32)


def frame_spans(frames):
    spans = []
    for tap in (1, 0, 2):
        off = tap - 1
        count = frames - abs(off)
        if count > 0:
            spans.append((tap, max(0, -off), max(0, off), count))
    return spans


def near_frames(cell, frames):
    frame = cell % frames
    near = [cell + t for t in (-1, 0, 1) if 0 <= frame + t < frames]
    return near, near[0] - cell + 1


class Copies:
    def __init__(self, sems):
        self.sems, self.count = sems, 0

    def start(self, src, dst):
        copy = pltpu.make_async_copy(src, dst, self.sems.at[self.count])
        self.count += 1
        copy.start()
        return copy


def phase_weights(w_ref, wc_ref):
    depth = w_ref.shape[-2]
    chunk = 16

    def step(tap, at):
        rows = slice(at, at + chunk)
        taps = [[w_ref[tap, h, w, rows].astype(F32) for w in range(3)] for h in range(3)]
        for p in range(2):
            if p == 0:
                merged = (taps[0], [taps[1][w] + taps[2][w] for w in range(3)])
            else:
                merged = ([taps[0][w] + taps[1][w] for w in range(3)], taps[2])
            for a in range(2):
                m = merged[a]
                wc_ref[p, 0, tap, a, 0, rows] = m[0].astype(BF16)
                wc_ref[p, 0, tap, a, 1, rows] = (m[1] + m[2]).astype(BF16)
                wc_ref[p, 1, tap, a, 0, rows] = (m[0] + m[1]).astype(BF16)
                wc_ref[p, 1, tap, a, 1, rows] = m[2].astype(BF16)

    return [functools.partial(step, tap, at) for tap in range(3) for at in range(0, depth, chunk)]


def widen(field, wide):
    def step(cell, row):
        wide[cell, row] = field[cell, row].astype(F32)

    return [functools.partial(step, cell, row) for cell in range(field.shape[0]) for row in range(field.shape[1])]


def gate_rows(feature):
    gated = silu(feature)
    return shift_cols(gated, 1).astype(BF16), gated.astype(BF16), shift_cols(gated, -1).astype(BF16)


def second_feature(frames, gated, wc_ref, count, fine):
    _, groups, cells, _, cols, out = gated.shape
    for cell in range(cells):
        near, first_tap = near_frames(cell, frames)
        for p in range(2):
            for q in range(2):
                field = jnp.concatenate(
                    [
                        gated[q + b, :, other, p + a : p + a + count].reshape(groups * count * cols, out)
                        for other in near
                        for a in range(2)
                        for b in range(2)
                    ],
                    axis=1,
                )
                weight = wc_ref[p, q, first_tap : first_tap + len(near)].reshape(-1, out)
                product = dot(field, weight).reshape(groups, count, cols, out)
                for group in range(groups):
                    for row in range(count):
                        for block in range(out // 128):
                            fine[group, cell, row, p, block, pl.ds(q, cols, stride=2), :] = product[
                                group, row, :, 128 * block : 128 * block + 128
                            ]


def depthwise(frames, padded, kernel_ref, student):
    cells, rows, _, channels = student.shape

    def step(cell, row, lane):
        near, first_tap = near_frames(cell, frames)
        lanes = pl.ds(lane, 128)
        sums = [None, None, None]
        for t, other in enumerate(near):
            for h in range(3):
                field = padded[other, row + h, :, lanes]
                for w in range(3):
                    term = field * kernel_ref[t + first_tap, h, w : w + 1, lanes]
                    sums[w] = term if sums[w] is None else sums[w] + term
        total = padded[cell, row + 1, :, lanes] + sums[1] + shift_cols(sums[0], 1) + shift_cols(sums[2], -1)
        student[cell, row, :, lanes] = total.astype(BF16)

    return [
        functools.partial(step, cell, row, lane)
        for cell in range(cells)
        for lane in range(0, channels, 128)
        for row in range(rows)
    ]


def kernel_gradient(frames, padded, back, total, first):
    cells, rows, _, channels = back.shape
    for lane in range(0, channels, 128):
        lanes = pl.ds(lane, 128)
        sums = tuple(jnp.zeros((8, 128), F32) for _ in range(27))
        for cell in range(cells):
            near, first_tap = near_frames(cell, frames)

            def body(row, sums, cell=cell, near=near, first_tap=first_tap, lanes=lanes):
                sums = list(sums)
                center = back[cell, row, :, lanes]
                moved = (shift_cols(center, -1), center, shift_cols(center, 1))
                for t, other in enumerate(near):
                    for h in range(3):
                        field = padded[other, row + h, :, lanes]
                        for w in range(3):
                            k = 9 * (t + first_tap) + 3 * h + w
                            term = (moved[w] * field).reshape(-1, 8, 128)
                            sums[k] = sums[k] + jnp.sum(term, axis=0)
                return tuple(sums)

            sums = lax.fori_loop(0, rows, body, sums)
        for k in range(27):
            value = jnp.sum(sums[k], axis=0, keepdims=True)
            total[k : k + 1, lanes] = value if first else total[k : k + 1, lanes] + value


def level(student, target, adapter, scale, grad):
    mismatch = dot(student, adapter) - target
    residual = (mismatch * scale).astype(BF16)
    grad[...] += dot_tn(student, residual)
    return mismatch, dot_nt(residual, adapter)


def fine_target(fine, rows):
    blocks = fine.shape[2]
    value = jnp.concatenate([fine[rows, :, block].reshape(-1, 128) for block in range(blocks)], axis=1)
    return value.astype(BF16).astype(F32)


def first_kernel(
    frames, x_hbm, w_hbm, w2_hbm, low_hbm, high_hbm, klow_hbm, khigh_hbm, plow_hbm, phigh_hbm,
    inner, edge, first, second, wc, low_wide, high_wide, low_student, high_student, klow, khigh, plow, phigh,
    x_ref, w_buf, w2, acc, low, high, sems,
):
    cells, rows, cols, depth = x_ref.shape
    out = w_buf.shape[-1]
    clips = cells // frames
    spans = frame_spans(frames)
    copies = Copies(sems)
    load_x = copies.start(x_hbm, x_ref)
    loads = {}
    for tap_h in (1, 0, 2):
        loads[1, tap_h] = copies.start(w_hbm.at[1, tap_h], w_buf.at[1, tap_h])
    fields = [
        copies.start(high_hbm, high),
        copies.start(khigh_hbm, khigh),
        copies.start(low_hbm, low),
        copies.start(klow_hbm, klow),
    ]
    load_w2 = copies.start(w2_hbm, w2)
    for tap, _, _, _ in spans[1:]:
        for tap_h in (1, 0, 2):
            loads[tap, tap_h] = copies.start(w_hbm.at[tap, tap_h], w_buf.at[tap, tap_h])
    late = [copies.start(plow_hbm, plow), copies.start(phigh_hbm, phigh)]
    for tap_w in range(3):
        acc[tap_w, :, 0:1] = jnp.zeros((cells, 1, cols, out), F32)
        acc[tap_w, :, rows + 1 : rows + 2] = jnp.zeros((cells, 1, cols, out), F32)

    students = (
        widen(high, high_wide)
        + widen(low, low_wide)
        + depthwise(frames, high_wide.at[:, 3 : 2 * rows - 3], khigh, high_student)
        + depthwise(frames, low_wide, klow, low_student)
    )
    load_x.wait()
    pending, share = [], 0
    for number, (tap, to, src, count) in enumerate(spans):
        for tap_h in (1, 0, 2):
            loads[tap, tap_h].wait()
            if number == 0 and tap_h == 0:
                for copy in fields:
                    copy.wait()
                pending = list(students)
                share = -(-len(pending) // 6)
            if number == min(1, len(spans) - 1) and tap_h == (1 if number else 2):
                for step in pending:
                    step()
                load_w2.wait()
                pending = phase_weights(w2, wc)
                share = -(-len(pending) // (9 * max(1, len(spans) - 1)))
            at = 2 - tap_h
            for tap_w in range(3):
                weight = w_buf[tap, tap_h, tap_w]
                for clip in range(clips):
                    base = clip * frames
                    rowset = x_ref[base + src : base + src + count].reshape(-1, depth)
                    product = dot(rowset, weight).reshape(count, rows, cols, out)
                    spot = (tap_w, pl.ds(base + to, count), pl.ds(at, rows))
                    if tap == 1 and tap_h == 1:
                        acc[spot] = product
                    else:
                        acc[spot] = acc[spot] + product
                for step in pending[:share]:
                    step()
                pending = pending[share:]
    for step in pending:
        step()

    def gathered(cell, row):
        return acc[1, cell, row] + shift_cols(acc[0, cell, row], 1) + shift_cols(acc[2, cell, row], -1)

    for copy in late:
        copy.wait()
    low_ch, high_ch = low.shape[-1], high.shape[-1]
    even = lax.rem(lax.axis_index("space"), 2) == 0
    for cell in range(cells):
        for j in range(2):
            up, down = gathered(cell, j), gathered(cell, rows + j)
            edge[0, cell, j], edge[1, cell, j] = up, down
            first[cell, j, :, 0:out] = jnp.where(even, down, up).astype(BF16)
            second[cell, j, :, 0:out] = jnp.where(even, up, down).astype(BF16)
        up, down = low_wide[cell, 0], low_wide[cell, rows - 1]
        first[cell, 2, :, 0:low_ch] = jnp.where(even, down, up).astype(BF16)
        second[cell, 2, :, 0:low_ch] = jnp.where(even, up, down).astype(BF16)
        for half in range(2):
            here, lanes = slice(half * cols, (half + 1) * cols), slice(half * high_ch, (half + 1) * high_ch)
            up, down = high_wide[cell, 0, here], high_wide[cell, 2 * rows - 1, here]
            first[cell, 3, :, lanes] = jnp.where(even, down, up).astype(BF16)
            second[cell, 3, :, lanes] = jnp.where(even, up, down).astype(BF16)
    for cell in range(cells):

        def gather(row, _, cell=cell):
            inner[cell, row] = gathered(cell, row + 2).astype(BF16)
            return 0

        lax.fori_loop(0, rows - 2, gather, 0)


def second_kernel(
    frames, scale_low, scale_high,
    feature, wc, low_wide, high_wide, low_student, high_student, plow, phigh,
    mismatch_hbm, glow, ghigh, gklow, gkhigh,
    mismatch, gated, fine, low_back, high_back, sems,
):
    cells, count, cols, out = feature.shape
    rows = count + 2
    inner = rows - 4
    copies = Copies(sems)
    for cell in range(cells):

        def gate(row, _, cell=cell):
            for k, value in enumerate(gate_rows(feature[cell, row].astype(F32))):
                gated[k, 0, cell, row] = value
            return 0

        lax.fori_loop(0, count, gate, 0)
    second_feature(frames, gated, wc, inner, fine)

    glow[...] = jnp.zeros_like(glow)
    ghigh[...] = jnp.zeros_like(ghigh)
    gklow[...] = jnp.zeros_like(gklow)
    gkhigh[...] = jnp.zeros_like(gkhigh)
    for cell in range(cells):
        student = high_student[cell].reshape(-1, high_student.shape[-1])
        target = fine_target(fine.at[0, cell], slice(0, inner))
        value, back = level(student, target, phigh[...], scale_high, ghigh)
        mismatch[cell] = value.astype(BF16).reshape(2 * inner, 2 * cols, out)
        high_back[cell] = back.reshape(2 * inner, 2 * cols, -1)
    store = copies.start(mismatch, mismatch_hbm.at[:, pl.ds(4, 2 * inner)])
    student = low_student[...].reshape(-1, low_student.shape[-1])
    target = feature[...].reshape(-1, out).astype(F32)
    _, back = level(student, target, plow[...], scale_low, glow)
    low_back[...] = back.reshape(low_back.shape)
    kernel_gradient(frames, low_wide, low_back, gklow, True)
    kernel_gradient(frames, high_wide.at[:, 3 : 2 * rows - 3], high_back, gkhigh, True)
    store.wait()


def third_kernel(
    frames, shards, tiles, scale_low, scale_high,
    first, second, edge, inner, wc, glow_in, ghigh_in, gklow_in, gkhigh_in, low_wide, high_wide, klow, khigh, plow, phigh, mismatch_in,
    mismatch_hbm, keep, send,
    glow, ghigh, gklow, gkhigh, mismatch,
    feature, gated, fine, low_pad, high_pad, low_student, high_student, low_back, high_back, shard_sums, sems,
):
    del mismatch_in
    _, cells, _, cols, out = edge.shape
    rows = inner.shape[1] + 2
    low_ch, high_ch = low_wide.shape[-1], high_wide.shape[-1]
    mine, tile = lax.axis_index("clip"), lax.axis_index("space")
    even = lax.rem(tile, 2) == 0
    outside = (tile == 0, tile == tiles - 1)
    copies = Copies(sems)
    for total, part in ((glow, glow_in), (ghigh, ghigh_in), (gklow, gklow_in), (gkhigh, gkhigh_in)):
        total[...] = part[...]

    def halo(side, cell, row):
        ours, other = first[cell, row].astype(F32), second[cell, row].astype(F32)
        return jnp.where(even, other, ours) if side == 0 else jnp.where(even, ours, other)

    for side in range(2):
        for cell in range(cells):
            for k in range(2):
                whole = (edge[side, cell, k] + halo(side, cell, k)[:, 0:out]).astype(BF16).astype(F32)
                if k == side:
                    whole = jnp.where(outside[side], 0.0, whole)
                else:
                    feature[side, cell] = whole
                for j, value in enumerate(gate_rows(whole)):
                    gated[j, side, cell, 2 * side + k] = value
                for j, value in enumerate(gate_rows(inner[cell, side * (rows - 4) + k].astype(F32))):
                    gated[j, side, cell, 2 - 2 * side + k] = value

    second_feature(frames, gated, wc, 2, fine)

    for side in range(2):
        for cell in range(cells):
            low_halo, high_halo = halo(side, cell, 2), halo(side, cell, 3)
            at = 0 if side == 0 else 2
            low_pad[side, cell, at] = low_halo[:, 0:low_ch]
            low_pad[side, cell, pl.ds(1 - side, 2)] = low_wide[cell, pl.ds(side * (rows - 2), 2)]
            at = 0 if side == 0 else 5
            high_pad[side, cell, at, 0:cols] = high_halo[:, 0:high_ch]
            high_pad[side, cell, at, cols:] = high_halo[:, high_ch : 2 * high_ch]
            high_pad[side, cell, pl.ds(1 - side, 5)] = high_wide[cell, pl.ds(side * (2 * rows - 5), 5)]
        for step in depthwise(frames, high_pad.at[side], khigh, high_student.at[side]):
            step()
        for step in depthwise(frames, low_pad.at[side], klow, low_student.at[side]):
            step()

    student = low_student[...].reshape(-1, low_ch)
    _, back = level(student, feature[...].reshape(-1, out), plow[...], scale_low, glow)
    low_back[...] = back.reshape(low_back.shape)
    for side in range(2):
        kernel_gradient(frames, low_pad.at[side], low_back.at[side], gklow, False)

    student = high_student[...].reshape(-1, high_ch)
    target = jnp.concatenate(
        [fine_target(fine.at[side, cell], slice(0, 2)) for side in range(2) for cell in range(cells)], axis=0
    )
    value, back = level(student, target, phigh[...], scale_high, ghigh)
    mismatch[...] = value.astype(BF16).reshape(mismatch.shape)
    high_back[...] = back.reshape(high_back.shape)
    stores = [
        copies.start(mismatch.at[0], mismatch_hbm.at[:, pl.ds(0, 4)]),
        copies.start(mismatch.at[1], mismatch_hbm.at[:, pl.ds(2 * rows - 4, 4)]),
    ]
    for side in range(2):
        kernel_gradient(frames, high_pad.at[side], high_back.at[side], gkhigh, False)

    low_rows, high_rows = low_ch // shards, high_ch // shards
    shard_sums[...] = jnp.zeros_like(shard_sums)
    width = gklow.shape[1]
    lane = lax.broadcasted_iota(jnp.int32, gklow.shape, 1)
    wide_high = gkhigh[...]
    if high_ch < width:
        wide_high = jnp.concatenate([wide_high, jnp.zeros((wide_high.shape[0], width - high_ch), F32)], axis=1)
    for s in range(shards):
        shard_sums[s, 0:low_rows, 0:out] = glow[s * low_rows : (s + 1) * low_rows]
        shard_sums[s, low_rows : low_rows + high_rows, 0:out] = ghigh[s * high_rows : (s + 1) * high_rows]
        from_low = pltpu.roll(gklow[...], (width - s * low_rows) % width, 1)
        from_high = pltpu.roll(wide_high, (width + low_rows - s * high_rows) % width, 1)
        both = jnp.where(lane < low_rows, from_low, jnp.where(lane < low_rows + high_rows, from_high, 0.0))
        shard_sums[s, low_rows + high_rows : low_rows + high_rows + 32, 0:width] = both
    if shards == 1:
        keep[0] = shard_sums[0]
        send[0] = shard_sums[0].astype(BF16)
    else:
        bit = lax.rem(mine, 2)
        for k in range(shards // 2):
            keep[k] = shard_sums[2 * k + bit]
            send[k] = shard_sums[2 * k + 1 - bit].astype(BF16)
    for copy in stores:
        copy.wait()


def swaps(start, count):
    lower = range(start, count - 1, 2)
    return [(i, i + 1) for i in lower] + [(i + 1, i) for i in lower]


def pairs(count, bit):
    return [(i, i ^ bit) for i in range(count)]


def sum_over_devices(keep, send, clips, tiles):
    if clips > 1:
        mine = lax.axis_index("clip")
        keep = keep + lax.ppermute(send, "clip", pairs(clips, 1)).astype(F32)
        bit = 2
        while bit < clips:
            halves = keep.reshape((keep.shape[0] // 2, 2) + keep.shape[1:])
            own = lax.rem(lax.div(mine, bit), 2)
            send = lax.dynamic_index_in_dim(halves, 1 - own, 1, False).astype(BF16)
            keep = lax.dynamic_index_in_dim(halves, own, 1, False)
            keep = keep + lax.ppermute(send, "clip", pairs(clips, bit)).astype(F32)
            bit *= 2
    total = keep[0]
    bit = 1
    while bit < tiles:
        bits = (bit, 2 * bit, 3 * bit) if 2 * bit < tiles else (bit,)
        out = total.astype(BF16)
        got = [lax.ppermute(out, "space", pairs(tiles, b)) for b in bits]
        bit *= 2 ** (2 if len(bits) > 1 else 1)
        if bit >= tiles:
            return total, got
        for part in got:
            total = total + part.astype(F32)
    return total, []


def unpack_kernel(total_ref, *refs):
    got, (glow, gklow, ghigh, gkhigh), sums = refs[:-5], refs[-5:-1], refs[-1]
    value = total_ref[...]
    for part in got:
        value = value + part[...].astype(F32)
    sums[...] = value
    low_rows, high_rows, out = glow.shape[0], ghigh.shape[0], glow.shape[1]
    top = low_rows + high_rows
    glow[...] = sums[0:low_rows, 0:out]
    ghigh[...] = sums[low_rows:top, 0:out]
    for t in range(3):
        for h in range(3):
            at = top + 9 * t + 3 * h
            gklow[t, h] = sums[at : at + 3, 0:low_rows]
            gkhigh[t, h] = sums[at : at + 3, low_rows:top]


def on_device(teacher_input, conv_first, conv_second, student_low, student_high, kernel_low, kernel_high, adapter_low, adapter_high):
    clips, tiles = lax.axis_size("clip"), lax.axis_size("space")
    held, frames, rows, cols, depth = teacher_input.shape
    cells = held * frames
    out = conv_first.shape[-1]
    low_ch, high_ch = student_low.shape[-1], student_high.shape[-1]
    low_count = held * frames * rows * cols * clips * tiles
    scales = (1.0 / low_count, 1.0 / (4 * low_count))
    inner = rows - 4
    x = teacher_input.reshape(cells, rows, cols, depth)
    low = student_low.reshape(cells, rows, cols, low_ch)
    high = student_high.reshape(cells, 2 * rows, 2 * cols, high_ch)
    sems = pltpu.SemaphoreType.DMA

    def vm(*specs):
        return [pltpu.VMEM(shape, dtype) for shape, dtype in specs]

    packet = ((cells, 4, cols, max(out, low_ch, 2 * high_ch)), BF16)
    inner_spec = ((cells, rows - 2, cols, out), BF16)
    edge_spec = ((2, cells, 2, cols, out), F32)
    wc_spec = ((2, 2, 3, 2, 2, out, out), BF16)
    weights = ((kernel_low.shape, F32), (kernel_high.shape, F32), (adapter_low.shape, BF16), (adapter_high.shape, BF16))
    inner_feature, edge, first, second, wc, low_wide, high_wide, low_student, high_student, klow, khigh, plow, phigh = pl.pallas_call(
        functools.partial(first_kernel, frames),
        out_shape=tuple(
            vm(
                inner_spec,
                edge_spec,
                packet,
                packet,
                wc_spec,
                (low.shape, F32),
                (high.shape, F32),
                ((cells, rows - 2, cols, low_ch), BF16),
                ((cells, 2 * inner, 2 * cols, high_ch), BF16),
                *weights,
            )
        ),
        in_specs=[HBM] * 9,
        out_specs=(VMEM,) * 13,
        scratch_shapes=vm(
            (x.shape, BF16),
            (conv_first.shape, BF16),
            (conv_second.shape, BF16),
            ((3, cells, rows + 2, cols, out), F32),
            (low.shape, BF16),
            (high.shape, BF16),
        )
        + [sems((18,))],
        compiler_params=pltpu.CompilerParams(vmem_limit_bytes=20 * MIB),
        cost_estimate=pl.CostEstimate(flops=3 * 10**9, bytes_accessed=9 * 10**6, transcendentals=0),
        name="teacher_first",
    )(*in_hbm(x, conv_first, conv_second, low, high, kernel_low, kernel_high, adapter_low, adapter_high))

    first_got = lax.ppermute(first, "space", swaps(0, tiles))
    second_got = lax.ppermute(second, "space", swaps(1, tiles))

    grads = (((low_ch, out), F32), ((high_ch, out), F32), ((32, low_ch), F32), ((32, high_ch), F32))
    mismatch, *sums = pl.pallas_call(
        functools.partial(second_kernel, frames, *scales),
        out_shape=(pltpu.HBM((cells, 2 * rows, 2 * cols, out), BF16), *vm(*grads)),
        in_specs=[VMEM] * 8,
        out_specs=(HBM,) + (VMEM,) * 4,
        scratch_shapes=vm(
            ((cells, 2 * inner, 2 * cols, out), BF16),
            ((3, 1, cells, rows - 2, cols, out), BF16),
            ((1, cells, inner, 2, out // 128, 2 * cols, 128), F32),
            ((cells, rows - 2, cols, low_ch), F32),
            ((cells, 2 * inner, 2 * cols, high_ch), F32),
        )
        + [sems((1,))],
        compiler_params=pltpu.CompilerParams(vmem_limit_bytes=20 * MIB),
        cost_estimate=pl.CostEstimate(flops=5 * 10**9, bytes_accessed=20 * 10**6, transcendentals=0),
        name="inner_rows",
    )(inner_feature, wc, low_wide, high_wide, low_student, high_student, plow, phigh)

    shard_rows = low_ch // clips + high_ch // clips + 32
    shard_rows += -shard_rows % 16
    shard = (max(clips // 2, 1), shard_rows, out)
    mismatch, keep, send = pl.pallas_call(
        functools.partial(third_kernel, frames, clips, tiles, *scales),
        out_shape=(pltpu.HBM(mismatch.shape, BF16), *vm((shard, F32), (shard, BF16))),
        in_specs=[VMEM] * 15 + [HBM],
        out_specs=(HBM, VMEM, VMEM),
        input_output_aliases={15: 0},
        scratch_shapes=vm(
            *grads,
            ((2, cells, 4, 2 * cols, out), BF16),
            ((2, cells, cols, out), F32),
            ((3, 2, cells, 4, cols, out), BF16),
            ((2, cells, 2, 2, out // 128, 2 * cols, 128), F32),
            ((2, cells, 3, cols, low_ch), F32),
            ((2, cells, 6, 2 * cols, high_ch), F32),
            ((2, cells, 1, cols, low_ch), BF16),
            ((2, cells, 4, 2 * cols, high_ch), BF16),
            ((2, cells, 1, cols, low_ch), F32),
            ((2, cells, 4, 2 * cols, high_ch), F32),
            ((clips, shard_rows, out), F32),
        )
        + [sems((2,))],
        compiler_params=pltpu.CompilerParams(vmem_limit_bytes=20 * MIB),
        cost_estimate=pl.CostEstimate(flops=3 * 10**9, bytes_accessed=20 * 10**6, transcendentals=0),
        name="border_rows",
    )(first_got, second_got, edge, inner_feature, wc, *sums, low_wide, high_wide, klow, khigh, plow, phigh, *in_hbm(mismatch))

    total, got = sum_over_devices(keep, send, clips, tiles)
    low_rows, high_rows = low_ch // clips, high_ch // clips
    glow, gklow, ghigh, gkhigh = pl.pallas_call(
        unpack_kernel,
        out_shape=(
            jax.ShapeDtypeStruct((low_rows, out), F32),
            jax.ShapeDtypeStruct((3, 3, 3, low_rows), F32),
            jax.ShapeDtypeStruct((high_rows, out), F32),
            jax.ShapeDtypeStruct((3, 3, 3, high_rows), F32),
        ),
        in_specs=[VMEM] * (1 + len(got)),
        out_specs=(VMEM,) * 4,
        scratch_shapes=[pltpu.VMEM(shard[1:], F32)],
        compiler_params=pltpu.CompilerParams(vmem_limit_bytes=4 * MIB),
        name="unpack",
    )(total, *got)
    return glow, gklow, ghigh, gkhigh, mismatch.reshape(held, frames, 2 * rows, 2 * cols, out)


def solution(mesh):
    tiled = P("clip", None, "space", None, None)
    return jax.shard_map(
        on_device,
        mesh=mesh,
        in_specs=(tiled, P(), P(), tiled, tiled, P(), P(), P(), P()),
        out_specs=(P("clip", None), P(None, None, None, "clip"), P("clip", None), P(None, None, None, "clip"), tiled),
        check_vma=False,
    )
```

```python
import functools

import jax
import jax.numpy as jnp
from jax import lax
from jax.experimental import pallas as pl
from jax.experimental.pallas import tpu as pltpu
from jax.sharding import PartitionSpec as P

F32, BF16 = jnp.float32, jnp.bfloat16
HBM = pl.BlockSpec(memory_space=pltpu.HBM)
VMEM = pl.BlockSpec(memory_space=pltpu.VMEM)
MIB = 1 << 20


def in_hbm(*arrays):
    return [pltpu.with_memory_space_constraint(array, pltpu.HBM) for array in arrays]


def shift_cols(value, by):
    axis = value.ndim - 2
    count = value.shape[axis]
    column = lax.broadcasted_iota(jnp.int32, value.shape, axis)
    edge = 0 if by > 0 else count - 1
    return jnp.where(column == edge, 0.0, pltpu.roll(value, by % count, axis))


def silu(value):
    return value / (1.0 + jnp.exp(-value))


def dot(a, b):
    return jnp.dot(a, b, preferred_element_type=F32)


def dot_nt(a, b):
    return lax.dot_general(a, b, (((1,), (1,)), ((), ())), preferred_element_type=F32)


def dot_tn(a, b):
    return lax.dot_general(a, b, (((0,), (0,)), ((), ())), preferred_element_type=F32)


def frame_spans(frames):
    spans = []
    for tap in (1, 0, 2):
        off = tap - 1
        count = frames - abs(off)
        if count > 0:
            spans.append((tap, max(0, -off), max(0, off), count))
    return spans


def near_frames(cell, frames):
    frame = cell % frames
    near = [cell + t for t in (-1, 0, 1) if 0 <= frame + t < frames]
    return near, near[0] - cell + 1


class Copies:
    def __init__(self, sems):
        self.sems, self.count = sems, 0

    def start(self, src, dst):
        copy = pltpu.make_async_copy(src, dst, self.sems.at[self.count])
        self.count += 1
        copy.start()
        return copy


def phase_weights(w_ref, wc_ref):
    depth = w_ref.shape[-2]
    chunk = 16

    def step(tap, at):
        rows = slice(at, at + chunk)
        taps = [[w_ref[tap, h, w, rows].astype(F32) for w in range(3)] for h in range(3)]
        for p in range(2):
            if p == 0:
                merged = (taps[0], [taps[1][w] + taps[2][w] for w in range(3)])
            else:
                merged = ([taps[0][w] + taps[1][w] for w in range(3)], taps[2])
            for a in range(2):
                m = merged[a]
                wc_ref[p, 0, tap, a, 0, rows] = m[0].astype(BF16)
                wc_ref[p, 0, tap, a, 1, rows] = (m[1] + m[2]).astype(BF16)
                wc_ref[p, 1, tap, a, 0, rows] = (m[0] + m[1]).astype(BF16)
                wc_ref[p, 1, tap, a, 1, rows] = m[2].astype(BF16)

    return [functools.partial(step, tap, at) for tap in range(3) for at in range(0, depth, chunk)]


def widen(field, wide):
    def step(cell, row):
        wide[cell, row] = field[cell, row].astype(F32)

    return [functools.partial(step, cell, row) for cell in range(field.shape[0]) for row in range(field.shape[1])]


def gate_rows(feature):
    gated = silu(feature)
    return shift_cols(gated, 1).astype(BF16), gated.astype(BF16), shift_cols(gated, -1).astype(BF16)


def second_feature(frames, gated, wc_ref, count, fine):
    _, groups, cells, _, cols, out = gated.shape
    for cell in range(cells):
        near, first_tap = near_frames(cell, frames)
        for p in range(2):
            for q in range(2):
                field = jnp.concatenate(
                    [
                        gated[q + b, :, other, p + a : p + a + count].reshape(groups * count * cols, out)
                        for other in near
                        for a in range(2)
                        for b in range(2)
                    ],
                    axis=1,
                )
                weight = wc_ref[p, q, first_tap : first_tap + len(near)].reshape(-1, out)
                product = dot(field, weight).reshape(groups, count, cols, out)
                for group in range(groups):
                    for row in range(count):
                        for block in range(out // 128):
                            fine[group, cell, row, p, block, pl.ds(q, cols, stride=2), :] = product[
                                group, row, :, 128 * block : 128 * block + 128
                            ]


def depthwise(frames, padded, kernel_ref, student):
    cells, rows, _, channels = student.shape

    def step(cell, row, lane):
        near, first_tap = near_frames(cell, frames)
        lanes = pl.ds(lane, 128)
        sums = [None, None, None]
        for t, other in enumerate(near):
            for h in range(3):
                field = padded[other, row + h, :, lanes]
                for w in range(3):
                    term = field * kernel_ref[t + first_tap, h, w : w + 1, lanes]
                    sums[w] = term if sums[w] is None else sums[w] + term
        total = padded[cell, row + 1, :, lanes] + sums[1] + shift_cols(sums[0], 1) + shift_cols(sums[2], -1)
        student[cell, row, :, lanes] = total.astype(BF16)

    return [
        functools.partial(step, cell, row, lane)
        for cell in range(cells)
        for lane in range(0, channels, 128)
        for row in range(rows)
    ]


def kernel_gradient(frames, padded, back, total, first):
    cells, rows, _, channels = back.shape
    for lane in range(0, channels, 128):
        lanes = pl.ds(lane, 128)
        sums = tuple(jnp.zeros((8, 128), F32) for _ in range(27))
        for cell in range(cells):
            near, first_tap = near_frames(cell, frames)

            def body(row, sums, cell=cell, near=near, first_tap=first_tap, lanes=lanes):
                sums = list(sums)
                center = back[cell, row, :, lanes]
                moved = (shift_cols(center, -1), center, shift_cols(center, 1))
                for t, other in enumerate(near):
                    for h in range(3):
                        field = padded[other, row + h, :, lanes]
                        for w in range(3):
                            k = 9 * (t + first_tap) + 3 * h + w
                            term = (moved[w] * field).reshape(-1, 8, 128)
                            sums[k] = sums[k] + jnp.sum(term, axis=0)
                return tuple(sums)

            sums = lax.fori_loop(0, rows, body, sums)
        for k in range(27):
            value = jnp.sum(sums[k], axis=0, keepdims=True)
            total[k : k + 1, lanes] = value if first else total[k : k + 1, lanes] + value


def level(student, target, adapter, scale, grad):
    mismatch = dot(student, adapter) - target
    residual = (mismatch * scale).astype(BF16)
    grad[...] += dot_tn(student, residual)
    return mismatch, dot_nt(residual, adapter)


def fine_target(fine, rows):
    blocks = fine.shape[2]
    value = jnp.concatenate([fine[rows, :, block].reshape(-1, 128) for block in range(blocks)], axis=1)
    return value.astype(BF16).astype(F32)


def first_kernel(
    frames, x_hbm, w_hbm, w2_hbm, low_hbm, high_hbm, klow_hbm, khigh_hbm, plow_hbm, phigh_hbm,
    inner, edge, first, second, wc, low_wide, high_wide, low_student, high_student, klow, khigh, plow, phigh,
    x_ref, w_buf, w2, acc, low, high, sems,
):
    cells, rows, cols, depth = x_ref.shape
    out = w_buf.shape[-1]
    clips = cells // frames
    spans = frame_spans(frames)
    copies = Copies(sems)
    load_x = copies.start(x_hbm, x_ref)
    loads = {}
    for tap_h in (1, 0, 2):
        loads[1, tap_h] = copies.start(w_hbm.at[1, tap_h], w_buf.at[1, tap_h])
    fields = [
        copies.start(high_hbm, high),
        copies.start(khigh_hbm, khigh),
        copies.start(low_hbm, low),
        copies.start(klow_hbm, klow),
    ]
    load_w2 = copies.start(w2_hbm, w2)
    for tap, _, _, _ in spans[1:]:
        for tap_h in (1, 0, 2):
            loads[tap, tap_h] = copies.start(w_hbm.at[tap, tap_h], w_buf.at[tap, tap_h])
    late = [copies.start(plow_hbm, plow), copies.start(phigh_hbm, phigh)]
    for tap_w in range(3):
        acc[tap_w, :, 0:1] = jnp.zeros((cells, 1, cols, out), F32)
        acc[tap_w, :, rows + 1 : rows + 2] = jnp.zeros((cells, 1, cols, out), F32)

    students = (
        widen(high, high_wide)
        + widen(low, low_wide)
        + depthwise(frames, high_wide.at[:, 3 : 2 * rows - 3], khigh, high_student)
        + depthwise(frames, low_wide, klow, low_student)
    )
    load_x.wait()
    pending, share = [], 0
    for number, (tap, to, src, count) in enumerate(spans):
        for tap_h in (1, 0, 2):
            loads[tap, tap_h].wait()
            if number == 0 and tap_h == 0:
                for copy in fields:
                    copy.wait()
                pending = list(students)
                share = -(-len(pending) // 6)
            if number == min(1, len(spans) - 1) and tap_h == (1 if number else 2):
                for step in pending:
                    step()
                load_w2.wait()
                pending = phase_weights(w2, wc)
                share = -(-len(pending) // (9 * max(1, len(spans) - 1)))
            at = 2 - tap_h
            for tap_w in range(3):
                weight = w_buf[tap, tap_h, tap_w]
                for clip in range(clips):
                    base = clip * frames
                    rowset = x_ref[base + src : base + src + count].reshape(-1, depth)
                    product = dot(rowset, weight).reshape(count, rows, cols, out)
                    spot = (tap_w, pl.ds(base + to, count), pl.ds(at, rows))
                    if tap == 1 and tap_h == 1:
                        acc[spot] = product
                    else:
                        acc[spot] = acc[spot] + product
                for step in pending[:share]:
                    step()
                pending = pending[share:]
    for step in pending:
        step()

    def gathered(cell, row):
        return acc[1, cell, row] + shift_cols(acc[0, cell, row], 1) + shift_cols(acc[2, cell, row], -1)

    for copy in late:
        copy.wait()
    low_ch, high_ch = low.shape[-1], high.shape[-1]
    even = lax.rem(lax.axis_index("space"), 2) == 0
    for cell in range(cells):
        for j in range(2):
            up, down = gathered(cell, j), gathered(cell, rows + j)
            edge[0, cell, j], edge[1, cell, j] = up, down
            first[cell, j, :, 0:out] = jnp.where(even, down, up).astype(BF16)
            second[cell, j, :, 0:out] = jnp.where(even, up, down).astype(BF16)
        up, down = low_wide[cell, 0], low_wide[cell, rows - 1]
        first[cell, 2, :, 0:low_ch] = jnp.where(even, down, up).astype(BF16)
        second[cell, 2, :, 0:low_ch] = jnp.where(even, up, down).astype(BF16)
        for half in range(2):
            here, lanes = slice(half * cols, (half + 1) * cols), slice(half * high_ch, (half + 1) * high_ch)
            up, down = high_wide[cell, 0, here], high_wide[cell, 2 * rows - 1, here]
            first[cell, 3, :, lanes] = jnp.where(even, down, up).astype(BF16)
            second[cell, 3, :, lanes] = jnp.where(even, up, down).astype(BF16)
    for cell in range(cells):

        def gather(row, _, cell=cell):
            inner[cell, row] = gathered(cell, row + 2).astype(BF16)
            return 0

        lax.fori_loop(0, rows - 2, gather, 0)


def second_kernel(
    frames, scale_low, scale_high,
    feature, wc, low_wide, high_wide, low_student, high_student, plow, phigh,
    mismatch_hbm, glow, ghigh, gklow, gkhigh,
    mismatch, gated, fine, low_back, high_back, sems,
):
    cells, count, cols, out = feature.shape
    rows = count + 2
    inner = rows - 4
    copies = Copies(sems)
    for cell in range(cells):

        def gate(row, _, cell=cell):
            for k, value in enumerate(gate_rows(feature[cell, row].astype(F32))):
                gated[k, 0, cell, row] = value
            return 0

        lax.fori_loop(0, count, gate, 0)
    second_feature(frames, gated, wc, inner, fine)

    glow[...] = jnp.zeros_like(glow)
    ghigh[...] = jnp.zeros_like(ghigh)
    gklow[...] = jnp.zeros_like(gklow)
    gkhigh[...] = jnp.zeros_like(gkhigh)
    for cell in range(cells):
        student = high_student[cell].reshape(-1, high_student.shape[-1])
        target = fine_target(fine.at[0, cell], slice(0, inner))
        value, back = level(student, target, phigh[...], scale_high, ghigh)
        mismatch[cell] = value.astype(BF16).reshape(2 * inner, 2 * cols, out)
        high_back[cell] = back.reshape(2 * inner, 2 * cols, -1)
    store = copies.start(mismatch, mismatch_hbm.at[:, pl.ds(4, 2 * inner)])
    student = low_student[...].reshape(-1, low_student.shape[-1])
    target = feature[...].reshape(-1, out).astype(F32)
    _, back = level(student, target, plow[...], scale_low, glow)
    low_back[...] = back.reshape(low_back.shape)
    kernel_gradient(frames, low_wide, low_back, gklow, True)
    kernel_gradient(frames, high_wide.at[:, 3 : 2 * rows - 3], high_back, gkhigh, True)
    store.wait()


def third_kernel(
    frames, shards, tiles, scale_low, scale_high,
    first, second, edge, inner, wc, glow_in, ghigh_in, gklow_in, gkhigh_in, low_wide, high_wide, klow, khigh, plow, phigh, mismatch_in,
    mismatch_hbm, keep, send,
    glow, ghigh, gklow, gkhigh, mismatch,
    feature, gated, fine, low_pad, high_pad, low_student, high_student, low_back, high_back, shard_sums, sems,
):
    del mismatch_in
    _, cells, _, cols, out = edge.shape
    rows = inner.shape[1] + 2
    low_ch, high_ch = low_wide.shape[-1], high_wide.shape[-1]
    mine, tile = lax.axis_index("clip"), lax.axis_index("space")
    even = lax.rem(tile, 2) == 0
    outside = (tile == 0, tile == tiles - 1)
    copies = Copies(sems)
    for total, part in ((glow, glow_in), (ghigh, ghigh_in), (gklow, gklow_in), (gkhigh, gkhigh_in)):
        total[...] = part[...]

    def halo(side, cell, row):
        ours, other = first[cell, row].astype(F32), second[cell, row].astype(F32)
        found = jnp.where(even, other, ours) if side == 0 else jnp.where(even, ours, other)
        return jnp.where(outside[side], 0.0, found)

    for side in range(2):
        for cell in range(cells):
            for k in range(2):
                whole = (edge[side, cell, k] + halo(side, cell, k)[:, 0:out]).astype(BF16).astype(F32)
                if k == side:
                    whole = jnp.where(outside[side], 0.0, whole)
                else:
                    feature[side, cell] = whole
                for j, value in enumerate(gate_rows(whole)):
                    gated[j, side, cell, 2 * side + k] = value
                for j, value in enumerate(gate_rows(inner[cell, side * (rows - 4) + k].astype(F32))):
                    gated[j, side, cell, 2 - 2 * side + k] = value

    second_feature(frames, gated, wc, 2, fine)

    for side in range(2):
        for cell in range(cells):
            low_halo, high_halo = halo(side, cell, 2), halo(side, cell, 3)
            at = 0 if side == 0 else 2
            low_pad[side, cell, at] = low_halo[:, 0:low_ch]
            low_pad[side, cell, pl.ds(1 - side, 2)] = low_wide[cell, pl.ds(side * (rows - 2), 2)]
            at = 0 if side == 0 else 5
            high_pad[side, cell, at, 0:cols] = high_halo[:, 0:high_ch]
            high_pad[side, cell, at, cols:] = high_halo[:, high_ch : 2 * high_ch]
            high_pad[side, cell, pl.ds(1 - side, 5)] = high_wide[cell, pl.ds(side * (2 * rows - 5), 5)]
        for step in depthwise(frames, high_pad.at[side], khigh, high_student.at[side]):
            step()
        for step in depthwise(frames, low_pad.at[side], klow, low_student.at[side]):
            step()

    student = low_student[...].reshape(-1, low_ch)
    _, back = level(student, feature[...].reshape(-1, out), plow[...], scale_low, glow)
    low_back[...] = back.reshape(low_back.shape)
    for side in range(2):
        kernel_gradient(frames, low_pad.at[side], low_back.at[side], gklow, False)

    student = high_student[...].reshape(-1, high_ch)
    target = jnp.concatenate(
        [fine_target(fine.at[side, cell], slice(0, 2)) for side in range(2) for cell in range(cells)], axis=0
    )
    value, back = level(student, target, phigh[...], scale_high, ghigh)
    mismatch[...] = value.astype(BF16).reshape(mismatch.shape)
    high_back[...] = back.reshape(high_back.shape)
    stores = [
        copies.start(mismatch.at[0], mismatch_hbm.at[:, pl.ds(0, 4)]),
        copies.start(mismatch.at[1], mismatch_hbm.at[:, pl.ds(2 * rows - 4, 4)]),
    ]
    for side in range(2):
        kernel_gradient(frames, high_pad.at[side], high_back.at[side], gkhigh, False)

    low_rows, high_rows = low_ch // shards, high_ch // shards
    shard_sums[...] = jnp.zeros_like(shard_sums)
    width = gklow.shape[1]
    half = out // 2
    lane = lax.broadcasted_iota(jnp.int32, gklow.shape, 1)
    wide_high = gkhigh[...]
    if high_ch < width:
        wide_high = jnp.concatenate([wide_high, jnp.zeros((wide_high.shape[0], width - high_ch), F32)], axis=1)
    for s in range(shards):
        shard_sums[s, 0:low_rows, 0:out] = glow[s * low_rows : (s + 1) * low_rows]
        shard_sums[s, low_rows : low_rows + high_rows, 0:out] = ghigh[s * high_rows : (s + 1) * high_rows]
        from_low = pltpu.roll(gklow[...], (width - s * low_rows) % width, 1)
        from_high = pltpu.roll(wide_high, (width + low_rows - s * high_rows) % width, 1)
        both = jnp.where(lane < low_rows, from_low, jnp.where(lane < low_rows + high_rows, from_high, 0.0))
        top = low_rows + high_rows
        shard_sums[s, top : top + 16, 0:half] = both[0:16, 0:half]
        shard_sums[s, top : top + 16, half : 2 * half] = both[16:32, 0:half]
    if shards == 1:
        keep[0] = shard_sums[0]
        send[0] = shard_sums[0].astype(BF16)
    else:
        bit = lax.rem(mine, 2)
        for k in range(shards // 2):
            keep[k] = shard_sums[2 * k + bit]
            send[k] = shard_sums[2 * k + 1 - bit].astype(BF16)
    for copy in stores:
        copy.wait()


def swaps(clips, tiles, start):
    found = []
    for clip in range(clips):
        for tile in range(tiles):
            other = tile + 1 if (tile - start) % 2 == 0 else tile - 1
            if 0 <= other < tiles:
                found.append((clip * tiles + tile, clip * tiles + other))
            elif clips % 2 == 0:
                found.append((clip * tiles + tile, (clip ^ 1) * tiles + tile))
    return found


def pairs(count, bit):
    return [(i, i ^ bit) for i in range(count)]


def split_shards(keep, bit):
    halves = keep.reshape((keep.shape[0] // 2, 2) + keep.shape[1:])
    own = lax.rem(lax.div(lax.axis_index("clip"), bit), 2)
    send = lax.dynamic_index_in_dim(halves, 1 - own, 1, False).astype(BF16)
    return lax.dynamic_index_in_dim(halves, own, 1, False), send


def sum_over_devices(keep, send, clips, tiles):
    clip_bit, tile_bit = 2, 1
    if clips > 1:
        keep = keep + lax.ppermute(send, "clip", pairs(clips, 1)).astype(F32)
    if clips > 2 and tiles > 1:
        keep, send = split_shards(keep, 2)
        across = [(c * tiles + t, (c ^ 2) * tiles + (t ^ 1)) for c in range(clips) for t in range(tiles)]
        got = (
            lax.ppermute(send, "clip", pairs(clips, 2)),
            lax.ppermute(send, ("clip", "space"), across),
            lax.ppermute(keep.astype(BF16), "space", pairs(tiles, 1)),
        )
        for part in got:
            keep = keep + part.astype(F32)
        clip_bit, tile_bit = 4, 2
    while clip_bit < clips:
        keep, send = split_shards(keep, clip_bit)
        keep = keep + lax.ppermute(send, "clip", pairs(clips, clip_bit)).astype(F32)
        clip_bit *= 2
    total, got = keep[0], []
    while tile_bit < tiles:
        for part in got:
            total = total + part.astype(F32)
        bits = (tile_bit, 2 * tile_bit, 3 * tile_bit) if 2 * tile_bit < tiles else (tile_bit,)
        out = total.astype(BF16)
        got = [lax.ppermute(out, "space", pairs(tiles, b)) for b in bits]
        tile_bit *= 2 ** (2 if len(bits) > 1 else 1)
    return total, got


def unpack_kernel(total_ref, *refs):
    got, (glow, gklow, ghigh, gkhigh), sums = refs[:-5], refs[-5:-1], refs[-1]
    value = total_ref[...]
    for part in got:
        value = value + part[...].astype(F32)
    sums[...] = value
    low_rows, high_rows, out = glow.shape[0], ghigh.shape[0], glow.shape[1]
    top = low_rows + high_rows
    glow[...] = sums[0:low_rows, 0:out]
    ghigh[...] = sums[low_rows:top, 0:out]
    for k in range(27):
        at, lane = top + k % 16, k // 16 * (out // 2)
        tap, row, col = k // 9, k // 3 % 3, k % 3
        gklow[tap, row, col : col + 1] = sums[at : at + 1, lane : lane + low_rows]
        gkhigh[tap, row, col : col + 1] = sums[at : at + 1, lane + low_rows : lane + top]


def on_device(teacher_input, conv_first, conv_second, student_low, student_high, kernel_low, kernel_high, adapter_low, adapter_high):
    clips, tiles = lax.axis_size("clip"), lax.axis_size("space")
    held, frames, rows, cols, depth = teacher_input.shape
    cells = held * frames
    out = conv_first.shape[-1]
    low_ch, high_ch = student_low.shape[-1], student_high.shape[-1]
    low_count = held * frames * rows * cols * clips * tiles
    scales = (1.0 / low_count, 1.0 / (4 * low_count))
    inner = rows - 4
    x = teacher_input.reshape(cells, rows, cols, depth)
    low = student_low.reshape(cells, rows, cols, low_ch)
    high = student_high.reshape(cells, 2 * rows, 2 * cols, high_ch)
    sems = pltpu.SemaphoreType.DMA

    def vm(*specs):
        return [pltpu.VMEM(shape, dtype) for shape, dtype in specs]

    packet = ((cells, 4, cols, max(out, low_ch, 2 * high_ch)), BF16)
    inner_spec = ((cells, rows - 2, cols, out), BF16)
    edge_spec = ((2, cells, 2, cols, out), F32)
    wc_spec = ((2, 2, 3, 2, 2, out, out), BF16)
    weights = ((kernel_low.shape, F32), (kernel_high.shape, F32), (adapter_low.shape, BF16), (adapter_high.shape, BF16))
    inner_feature, edge, first, second, wc, low_wide, high_wide, low_student, high_student, klow, khigh, plow, phigh = pl.pallas_call(
        functools.partial(first_kernel, frames),
        out_shape=tuple(
            vm(
                inner_spec,
                edge_spec,
                packet,
                packet,
                wc_spec,
                (low.shape, F32),
                (high.shape, F32),
                ((cells, rows - 2, cols, low_ch), BF16),
                ((cells, 2 * inner, 2 * cols, high_ch), BF16),
                *weights,
            )
        ),
        in_specs=[HBM] * 9,
        out_specs=(VMEM,) * 13,
        scratch_shapes=vm(
            (x.shape, BF16),
            (conv_first.shape, BF16),
            (conv_second.shape, BF16),
            ((3, cells, rows + 2, cols, out), F32),
            (low.shape, BF16),
            (high.shape, BF16),
        )
        + [sems((18,))],
        compiler_params=pltpu.CompilerParams(vmem_limit_bytes=20 * MIB),
        cost_estimate=pl.CostEstimate(flops=3 * 10**9, bytes_accessed=9 * 10**6, transcendentals=0),
        name="teacher_first",
    )(*in_hbm(x, conv_first, conv_second, low, high, kernel_low, kernel_high, adapter_low, adapter_high))

    first_got = lax.ppermute(first, ("clip", "space"), swaps(clips, tiles, 0))
    second_got = lax.ppermute(second, ("clip", "space"), swaps(clips, tiles, 1))

    grads = (((low_ch, out), F32), ((high_ch, out), F32), ((32, low_ch), F32), ((32, high_ch), F32))
    mismatch, *sums = pl.pallas_call(
        functools.partial(second_kernel, frames, *scales),
        out_shape=(pltpu.HBM((cells, 2 * rows, 2 * cols, out), BF16), *vm(*grads)),
        in_specs=[VMEM] * 8,
        out_specs=(HBM,) + (VMEM,) * 4,
        scratch_shapes=vm(
            ((cells, 2 * inner, 2 * cols, out), BF16),
            ((3, 1, cells, rows - 2, cols, out), BF16),
            ((1, cells, inner, 2, out // 128, 2 * cols, 128), F32),
            ((cells, rows - 2, cols, low_ch), F32),
            ((cells, 2 * inner, 2 * cols, high_ch), F32),
        )
        + [sems((1,))],
        compiler_params=pltpu.CompilerParams(vmem_limit_bytes=20 * MIB),
        cost_estimate=pl.CostEstimate(flops=5 * 10**9, bytes_accessed=20 * 10**6, transcendentals=0),
        name="inner_rows",
    )(inner_feature, wc, low_wide, high_wide, low_student, high_student, plow, phigh)

    shard_rows = low_ch // clips + high_ch // clips + 16
    shard_rows += -shard_rows % 16
    shard = (max(clips // 2, 1), shard_rows, out)
    mismatch, keep, send = pl.pallas_call(
        functools.partial(third_kernel, frames, clips, tiles, *scales),
        out_shape=(pltpu.HBM(mismatch.shape, BF16), *vm((shard, F32), (shard, BF16))),
        in_specs=[VMEM] * 15 + [HBM],
        out_specs=(HBM, VMEM, VMEM),
        input_output_aliases={15: 0},
        scratch_shapes=vm(
            *grads,
            ((2, cells, 4, 2 * cols, out), BF16),
            ((2, cells, cols, out), F32),
            ((3, 2, cells, 4, cols, out), BF16),
            ((2, cells, 2, 2, out // 128, 2 * cols, 128), F32),
            ((2, cells, 3, cols, low_ch), F32),
            ((2, cells, 6, 2 * cols, high_ch), F32),
            ((2, cells, 1, cols, low_ch), BF16),
            ((2, cells, 4, 2 * cols, high_ch), BF16),
            ((2, cells, 1, cols, low_ch), F32),
            ((2, cells, 4, 2 * cols, high_ch), F32),
            ((clips, shard_rows, out), F32),
        )
        + [sems((2,))],
        compiler_params=pltpu.CompilerParams(vmem_limit_bytes=20 * MIB),
        cost_estimate=pl.CostEstimate(flops=3 * 10**9, bytes_accessed=20 * 10**6, transcendentals=0),
        name="border_rows",
    )(first_got, second_got, edge, inner_feature, wc, *sums, low_wide, high_wide, klow, khigh, plow, phigh, *in_hbm(mismatch))

    total, got = sum_over_devices(keep, send, clips, tiles)
    low_rows, high_rows = low_ch // clips, high_ch // clips
    glow, gklow, ghigh, gkhigh = pl.pallas_call(
        unpack_kernel,
        out_shape=(
            jax.ShapeDtypeStruct((low_rows, out), F32),
            jax.ShapeDtypeStruct((3, 3, 3, low_rows), F32),
            jax.ShapeDtypeStruct((high_rows, out), F32),
            jax.ShapeDtypeStruct((3, 3, 3, high_rows), F32),
        ),
        in_specs=[VMEM] * (1 + len(got)),
        out_specs=(VMEM,) * 4,
        scratch_shapes=[pltpu.VMEM(shard[1:], F32)],
        compiler_params=pltpu.CompilerParams(vmem_limit_bytes=4 * MIB),
        name="unpack",
    )(total, *got)
    return glow, gklow, ghigh, gkhigh, mismatch.reshape(held, frames, 2 * rows, 2 * cols, out)


def solution(mesh):
    tiled = P("clip", None, "space", None, None)
    return jax.shard_map(
        on_device,
        mesh=mesh,
        in_specs=(tiled, P(), P(), tiled, tiled, P(), P(), P(), P()),
        out_specs=(P("clip", None), P(None, None, None, "clip"), P("clip", None), P(None, None, None, "clip"), tiled),
        check_vma=False,
    )
```

```python
import functools

import jax
import jax.numpy as jnp
from jax import lax
from jax.experimental import pallas as pl
from jax.experimental.pallas import tpu as pltpu
from jax.sharding import PartitionSpec as P

F32, BF16 = jnp.float32, jnp.bfloat16
HBM = pl.BlockSpec(memory_space=pltpu.HBM)
VMEM = pl.BlockSpec(memory_space=pltpu.VMEM)
MIB = 1 << 20


def in_hbm(*arrays):
    return [pltpu.with_memory_space_constraint(array, pltpu.HBM) for array in arrays]


def shift_cols(value, by):
    axis = value.ndim - 2
    count = value.shape[axis]
    column = lax.broadcasted_iota(jnp.int32, value.shape, axis)
    edge = 0 if by > 0 else count - 1
    return jnp.where(column == edge, 0.0, pltpu.roll(value, by % count, axis))


def silu(value):
    return value / (1.0 + jnp.exp(-value))


def dot(a, b):
    return jnp.dot(a, b, preferred_element_type=F32)


def dot_nt(a, b):
    return lax.dot_general(a, b, (((1,), (1,)), ((), ())), preferred_element_type=F32)


def dot_tn(a, b):
    return lax.dot_general(a, b, (((0,), (0,)), ((), ())), preferred_element_type=F32)


def frame_spans(frames):
    spans = []
    for tap in (1, 0, 2):
        off = tap - 1
        count = frames - abs(off)
        if count > 0:
            spans.append((tap, max(0, -off), max(0, off), count))
    return spans


def near_frames(cell, frames):
    frame = cell % frames
    near = [cell + t for t in (-1, 0, 1) if 0 <= frame + t < frames]
    return near, near[0] - cell + 1


class Copies:
    def __init__(self, sems):
        self.sems, self.count = sems, 0

    def start(self, src, dst):
        copy = pltpu.make_async_copy(src, dst, self.sems.at[self.count])
        self.count += 1
        copy.start()
        return copy


def phase_weights(w_ref, wc_ref):
    depth = w_ref.shape[-2]
    chunk = 16

    def step(tap, at):
        rows = slice(at, at + chunk)
        taps = [[w_ref[tap, h, w, rows].astype(F32) for w in range(3)] for h in range(3)]
        for p in range(2):
            if p == 0:
                merged = (taps[0], [taps[1][w] + taps[2][w] for w in range(3)])
            else:
                merged = ([taps[0][w] + taps[1][w] for w in range(3)], taps[2])
            for a in range(2):
                m = merged[a]
                wc_ref[p, 0, tap, a, 0, rows] = m[0].astype(BF16)
                wc_ref[p, 0, tap, a, 1, rows] = (m[1] + m[2]).astype(BF16)
                wc_ref[p, 1, tap, a, 0, rows] = (m[0] + m[1]).astype(BF16)
                wc_ref[p, 1, tap, a, 1, rows] = m[2].astype(BF16)

    return [functools.partial(step, tap, at) for tap in range(3) for at in range(0, depth, chunk)]


def widen(field, wide):
    def step(cell, row):
        wide[cell, row] = field[cell, row].astype(F32)

    return [functools.partial(step, cell, row) for cell in range(field.shape[0]) for row in range(field.shape[1])]


def gate_rows(feature):
    gated = silu(feature)
    return shift_cols(gated, 1).astype(BF16), gated.astype(BF16), shift_cols(gated, -1).astype(BF16)


def second_feature(frames, gated, wc_ref, count, fine):
    _, groups, cells, _, cols, out = gated.shape
    size = groups * count * cols
    for p in range(2):
        for q in range(2):
            fields = [
                jnp.concatenate(
                    [
                        gated[q + b, :, cell, p + a : p + a + count].reshape(size, out)
                        for a in range(2)
                        for b in range(2)
                    ],
                    axis=1,
                )
                for cell in range(cells)
            ]
            weights = [wc_ref[p, q, tap].reshape(4 * out, out) for tap in range(3)]
            center = dot(jnp.concatenate(fields, axis=0), weights[1])
            for cell in range(cells):
                near, first_tap = near_frames(cell, frames)
                product = center[cell * size : (cell + 1) * size]
                for t, other in enumerate(near):
                    if other != cell:
                        product = product + dot(fields[other], weights[t + first_tap])
                product = product.reshape(groups, count, cols, out)
                for group in range(groups):
                    for row in range(count):
                        for block in range(out // 128):
                            fine[group, cell, row, p, block, pl.ds(q, cols, stride=2), :] = product[
                                group, row, :, 128 * block : 128 * block + 128
                            ]


def depthwise(frames, padded, kernel_ref, student):
    cells, rows, _, channels = student.shape

    def step(cell, row, lane):
        near, first_tap = near_frames(cell, frames)
        lanes = pl.ds(lane, 128)
        sums = [None, None, None]
        for t, other in enumerate(near):
            for h in range(3):
                field = padded[other, row + h, :, lanes]
                for w in range(3):
                    term = field * kernel_ref[t + first_tap, h, w : w + 1, lanes]
                    sums[w] = term if sums[w] is None else sums[w] + term
        total = padded[cell, row + 1, :, lanes] + sums[1] + shift_cols(sums[0], 1) + shift_cols(sums[2], -1)
        student[cell, row, :, lanes] = total.astype(BF16)

    return [
        functools.partial(step, cell, row, lane)
        for cell in range(cells)
        for lane in range(0, channels, 128)
        for row in range(rows)
    ]


def kernel_gradient(frames, blocks, start, finish):
    channels = blocks[0][1].shape[-1]
    for lane in range(0, channels, 128):
        lanes = pl.ds(lane, 128)
        sums = tuple(start(k, lanes) for k in range(27))
        for padded, back in blocks:
            cells, rows = back.shape[:2]
            for cell in range(cells):
                near, first_tap = near_frames(cell, frames)

                def body(row, sums, padded=padded, back=back, cell=cell, near=near, first_tap=first_tap, lanes=lanes):
                    sums = list(sums)
                    center = back[cell, row, :, lanes]
                    moved = (shift_cols(center, -1), center, shift_cols(center, 1))
                    for t, other in enumerate(near):
                        for h in range(3):
                            field = padded[other, row + h, :, lanes]
                            for w in range(3):
                                k = 9 * (t + first_tap) + 3 * h + w
                                term = (moved[w] * field).reshape(-1, 8, 128)
                                sums[k] = sums[k] + jnp.sum(term, axis=0)
                    return tuple(sums)

                sums = lax.fori_loop(0, rows, body, sums) if rows > 1 else body(0, sums)
        for k in range(27):
            finish(k, lanes, sums[k])


def level(student, target, adapter, scale, grad):
    mismatch = dot(student, adapter) - target
    residual = (mismatch * scale).astype(BF16)
    grad[...] += dot_tn(student, residual)
    return mismatch, dot_nt(residual, adapter)


def fine_target(fine, rows):
    blocks = fine.shape[2]
    value = jnp.concatenate([fine[rows, :, block].reshape(-1, 128) for block in range(blocks)], axis=1)
    return value.astype(BF16).astype(F32)


def first_kernel(
    frames, x_hbm, w_hbm, w2_hbm, low_hbm, high_hbm, klow_hbm, khigh_hbm, plow_hbm, phigh_hbm,
    inner, edge, first, second, w2, low_wide, high_wide, high_student, klow, khigh, plow, phigh,
    x_ref, w_buf, acc, low, high, sems,
):
    cells, rows, cols, depth = x_ref.shape
    out = w_buf.shape[-1]
    clips = cells // frames
    spans = frame_spans(frames)
    copies = Copies(sems)
    load_x = copies.start(x_hbm, x_ref)
    loads = {}
    for tap_h in (1, 0, 2):
        loads[1, tap_h] = copies.start(w_hbm.at[1, tap_h], w_buf.at[1, tap_h])
    fields = [
        copies.start(high_hbm, high),
        copies.start(khigh_hbm, khigh),
        copies.start(low_hbm, low),
        copies.start(klow_hbm, klow),
    ]
    for tap, _, _, _ in spans[1:]:
        for tap_h in (1, 0, 2):
            loads[tap, tap_h] = copies.start(w_hbm.at[tap, tap_h], w_buf.at[tap, tap_h])
    late = [copies.start(plow_hbm, plow), copies.start(phigh_hbm, phigh), copies.start(w2_hbm, w2)]
    for tap_w in range(3):
        acc[tap_w, :, 0:1] = jnp.zeros((cells, 1, cols, out), F32)
        acc[tap_w, :, rows + 1 : rows + 2] = jnp.zeros((cells, 1, cols, out), F32)

    students = (
        widen(high, high_wide)
        + widen(low, low_wide)
        + depthwise(frames, high_wide.at[:, 3 : 2 * rows - 3], khigh, high_student)
    )
    load_x.wait()
    pending, share = [], 0
    for number, (tap, to, src, count) in enumerate(spans):
        for tap_h in (1, 0, 2):
            loads[tap, tap_h].wait()
            if number == 0 and tap_h == 0:
                for copy in fields:
                    copy.wait()
                pending = list(students)
                share = -(-len(pending) // (9 * len(spans) - 3))
            at = 2 - tap_h
            for tap_w in range(3):
                weight = w_buf[tap, tap_h, tap_w]
                for clip in range(clips):
                    base = clip * frames
                    rowset = x_ref[base + src : base + src + count].reshape(-1, depth)
                    product = dot(rowset, weight).reshape(count, rows, cols, out)
                    spot = (tap_w, pl.ds(base + to, count), pl.ds(at, rows))
                    if tap == 1 and tap_h == 1:
                        acc[spot] = product
                    else:
                        acc[spot] = acc[spot] + product
                for step in pending[:share]:
                    step()
                pending = pending[share:]
    for step in pending:
        step()

    def gathered(cell, row):
        return acc[1, cell, row] + shift_cols(acc[0, cell, row], 1) + shift_cols(acc[2, cell, row], -1)

    for copy in late:
        copy.wait()
    low_ch, high_ch = low.shape[-1], high.shape[-1]
    even = lax.rem(lax.axis_index("space"), 2) == 0
    for cell in range(cells):
        for j in range(2):
            up, down = gathered(cell, j), gathered(cell, rows + j)
            edge[0, cell, j], edge[1, cell, j] = up, down
            first[cell, j, :, 0:out] = jnp.where(even, down, up).astype(BF16)
            second[cell, j, :, 0:out] = jnp.where(even, up, down).astype(BF16)
        up, down = low_wide[cell, 0], low_wide[cell, rows - 1]
        first[cell, 2, :, 0:low_ch] = jnp.where(even, down, up).astype(BF16)
        second[cell, 2, :, 0:low_ch] = jnp.where(even, up, down).astype(BF16)
        for half in range(2):
            here, lanes = slice(half * cols, (half + 1) * cols), slice(half * high_ch, (half + 1) * high_ch)
            up, down = high_wide[cell, 0, here], high_wide[cell, 2 * rows - 1, here]
            first[cell, 3, :, lanes] = jnp.where(even, down, up).astype(BF16)
            second[cell, 3, :, lanes] = jnp.where(even, up, down).astype(BF16)
    for cell in range(cells):

        def gather(row, _, cell=cell):
            inner[cell, row] = gathered(cell, row + 2).astype(BF16)
            return 0

        lax.fori_loop(0, rows - 2, gather, 0)


def second_kernel(
    frames, scale_low, scale_high,
    feature, w2, low_wide, high_wide, high_student, klow, khigh, plow, phigh,
    mismatch_hbm, wc, border_student, glow, ghigh, gklow, gkhigh,
    mismatch, gated, fine, low_student, low_back, high_back, sems,
):
    cells, count, cols, out = feature.shape
    rows = count + 2
    inner = rows - 4
    copies = Copies(sems)
    for cell in range(cells):

        def gate(row, _, cell=cell):
            for k, value in enumerate(gate_rows(feature[cell, row].astype(F32))):
                gated[k, 0, cell, row] = value
            return 0

        lax.fori_loop(0, count, gate, 0)
    for step in depthwise(frames, low_wide, klow, low_student) + phase_weights(w2, wc):
        step()
    second_feature(frames, gated, wc, inner, fine)
    for side, top in ((0, 0), (1, 2 * rows - 5)):
        for step in depthwise(frames, high_wide.at[:, top : top + 5], khigh, border_student.at[side]):
            step()

    glow[...] = jnp.zeros_like(glow)
    ghigh[...] = jnp.zeros_like(ghigh)
    for cell in range(cells):
        student = high_student[cell].reshape(-1, high_student.shape[-1])
        target = fine_target(fine.at[0, cell], slice(0, inner))
        value, back = level(student, target, phigh[...], scale_high, ghigh)
        mismatch[cell] = value.astype(BF16).reshape(2 * inner, 2 * cols, out)
        high_back[cell] = back.reshape(2 * inner, 2 * cols, -1)
    store = copies.start(mismatch, mismatch_hbm.at[:, pl.ds(4, 2 * inner)])
    student = low_student[...].reshape(-1, low_student.shape[-1])
    target = feature[...].reshape(-1, out).astype(F32)
    _, back = level(student, target, plow[...], scale_low, glow)
    low_back[...] = back.reshape(low_back.shape)
    for blocks, total in (([(low_wide, low_back)], gklow), ([(high_wide.at[:, 3 : 2 * rows - 3], high_back)], gkhigh)):

        def keep(k, lanes, sums, total=total):
            total[k, :, lanes] = sums

        kernel_gradient(frames, blocks, lambda k, lanes: jnp.zeros((8, 128), F32), keep)
    store.wait()


def third_kernel(
    frames, shards, tiles, scale_low, scale_high,
    first, second, edge, inner, wc, border_student, glow_in, ghigh_in, gklow_in, gkhigh_in, low_wide, high_wide, klow, khigh, plow, phigh, mismatch_in,
    mismatch_hbm, keep, send,
    glow, ghigh, gklow, gkhigh, mismatch,
    feature, gated, fine, low_pad, high_pad, low_student, high_student, low_back, high_back, shard_sums, sems,
):
    del mismatch_in
    _, cells, _, cols, out = edge.shape
    rows = inner.shape[1] + 2
    low_ch, high_ch = low_wide.shape[-1], high_wide.shape[-1]
    mine, tile = lax.axis_index("clip"), lax.axis_index("space")
    even = lax.rem(tile, 2) == 0
    outside = (tile == 0, tile == tiles - 1)
    copies = Copies(sems)
    glow[...] = glow_in[...]
    ghigh[...] = ghigh_in[...]
    gklow[27:] = jnp.zeros_like(gklow[27:])
    gkhigh[27:] = jnp.zeros_like(gkhigh[27:])

    def border_gradient(padded, back, part, total):
        def finish(k, lanes, sums):
            total[k : k + 1, lanes] = jnp.sum(sums, axis=0, keepdims=True)

        kernel_gradient(
            frames, [(padded.at[side], back.at[side]) for side in range(2)], lambda k, lanes: part[k, :, lanes], finish
        )

    def halo(side, cell, row):
        ours, other = first[cell, row].astype(F32), second[cell, row].astype(F32)
        found = jnp.where(even, other, ours) if side == 0 else jnp.where(even, ours, other)
        return jnp.where(outside[side], 0.0, found)

    for side in range(2):
        for cell in range(cells):
            for k in range(2):
                whole = (edge[side, cell, k] + halo(side, cell, k)[:, 0:out]).astype(BF16).astype(F32)
                if k == side:
                    whole = jnp.where(outside[side], 0.0, whole)
                else:
                    feature[side, cell] = whole
                for j, value in enumerate(gate_rows(whole)):
                    gated[j, side, cell, 2 * side + k] = value
                for j, value in enumerate(gate_rows(inner[cell, side * (rows - 4) + k].astype(F32))):
                    gated[j, side, cell, 2 - 2 * side + k] = value

    second_feature(frames, gated, wc, 2, fine)

    for side in range(2):
        for cell in range(cells):
            low_halo, high_halo = halo(side, cell, 2), halo(side, cell, 3)
            at = 0 if side == 0 else 2
            low_pad[side, cell, at] = low_halo[:, 0:low_ch]
            low_pad[side, cell, pl.ds(1 - side, 2)] = low_wide[cell, pl.ds(side * (rows - 2), 2)]
            at = 0 if side == 0 else 5
            high_pad[side, cell, at, 0:cols] = high_halo[:, 0:high_ch]
            high_pad[side, cell, at, cols:] = high_halo[:, high_ch : 2 * high_ch]
            high_pad[side, cell, pl.ds(1 - side, 5)] = high_wide[cell, pl.ds(side * (2 * rows - 5), 5)]
        at = 3 * side
        for step in depthwise(frames, high_pad.at[side, :, at : at + 3], khigh, high_student.at[side, :, at : at + 1]):
            step()
        for cell in range(cells):
            high_student[side, cell, 1 - side : 4 - side] = border_student[side, cell]
        for step in depthwise(frames, low_pad.at[side], klow, low_student.at[side]):
            step()

    student = low_student[...].reshape(-1, low_ch)
    _, back = level(student, feature[...].reshape(-1, out), plow[...], scale_low, glow)
    low_back[...] = back.reshape(low_back.shape)
    border_gradient(low_pad, low_back, gklow_in, gklow)

    student = high_student[...].reshape(-1, high_ch)
    target = jnp.concatenate(
        [fine_target(fine.at[side, cell], slice(0, 2)) for side in range(2) for cell in range(cells)], axis=0
    )
    value, back = level(student, target, phigh[...], scale_high, ghigh)
    mismatch[...] = value.astype(BF16).reshape(mismatch.shape)
    high_back[...] = back.reshape(high_back.shape)
    stores = [
        copies.start(mismatch.at[0], mismatch_hbm.at[:, pl.ds(0, 4)]),
        copies.start(mismatch.at[1], mismatch_hbm.at[:, pl.ds(2 * rows - 4, 4)]),
    ]
    border_gradient(high_pad, high_back, gkhigh_in, gkhigh)

    low_rows, high_rows = low_ch // shards, high_ch // shards
    shard_sums[...] = jnp.zeros_like(shard_sums)
    width = gklow.shape[1]
    half = out // 2
    lane = lax.broadcasted_iota(jnp.int32, gklow.shape, 1)
    wide_high = gkhigh[...]
    if high_ch < width:
        wide_high = jnp.concatenate([wide_high, jnp.zeros((wide_high.shape[0], width - high_ch), F32)], axis=1)
    for s in range(shards):
        shard_sums[s, 0:low_rows, 0:out] = glow[s * low_rows : (s + 1) * low_rows]
        shard_sums[s, low_rows : low_rows + high_rows, 0:out] = ghigh[s * high_rows : (s + 1) * high_rows]
        from_low = pltpu.roll(gklow[...], (width - s * low_rows) % width, 1)
        from_high = pltpu.roll(wide_high, (width + low_rows - s * high_rows) % width, 1)
        both = jnp.where(lane < low_rows, from_low, jnp.where(lane < low_rows + high_rows, from_high, 0.0))
        top = low_rows + high_rows
        shard_sums[s, top : top + 16, 0:half] = both[0:16, 0:half]
        shard_sums[s, top : top + 16, half : 2 * half] = both[16:32, 0:half]
    if shards == 1:
        keep[0] = shard_sums[0]
        send[0] = shard_sums[0].astype(BF16)
    else:
        bit = lax.rem(mine, 2)
        for k in range(shards // 2):
            keep[k] = shard_sums[2 * k + bit]
            send[k] = shard_sums[2 * k + 1 - bit].astype(BF16)
    for copy in stores:
        copy.wait()


def swaps(clips, tiles, start):
    found = []
    for clip in range(clips):
        for tile in range(tiles):
            other = tile + 1 if (tile - start) % 2 == 0 else tile - 1
            if 0 <= other < tiles:
                found.append((clip * tiles + tile, clip * tiles + other))
            elif clips % 2 == 0:
                found.append((clip * tiles + tile, (clip ^ 1) * tiles + tile))
    return found


def pairs(count, bit):
    return [(i, i ^ bit) for i in range(count)]


def split_shards(keep, bit):
    halves = keep.reshape((keep.shape[0] // 2, 2) + keep.shape[1:])
    own = lax.rem(lax.div(lax.axis_index("clip"), bit), 2)
    send = lax.dynamic_index_in_dim(halves, 1 - own, 1, False).astype(BF16)
    return lax.dynamic_index_in_dim(halves, own, 1, False), send


def sum_over_devices(keep, send, clips, tiles):
    clip_bit, tile_bit = 2, 1
    if clips > 1:
        keep = keep + lax.ppermute(send, "clip", pairs(clips, 1)).astype(F32)
    if clips > 2 and tiles > 1:
        keep, send = split_shards(keep, 2)
        across = [(c * tiles + t, (c ^ 2) * tiles + (t ^ 1)) for c in range(clips) for t in range(tiles)]
        got = (
            lax.ppermute(keep.astype(BF16), "space", pairs(tiles, 1)),
            lax.ppermute(send, "clip", pairs(clips, 2)),
            lax.ppermute(send, ("clip", "space"), across),
        )
        for part in got:
            keep = keep + part.astype(F32)
        clip_bit, tile_bit = 4, 2
    while clip_bit < clips:
        keep, send = split_shards(keep, clip_bit)
        keep = keep + lax.ppermute(send, "clip", pairs(clips, clip_bit)).astype(F32)
        clip_bit *= 2
    total, got = keep[0], []
    while tile_bit < tiles:
        for part in got:
            total = total + part.astype(F32)
        bits = (tile_bit, 2 * tile_bit, 3 * tile_bit) if 2 * tile_bit < tiles else (tile_bit,)
        out = total.astype(BF16)
        got = [lax.ppermute(out, "space", pairs(tiles, b)) for b in bits[::-1]]
        tile_bit *= 2 ** (2 if len(bits) > 1 else 1)
    return total, got


def unpack_kernel(total_ref, *refs):
    got, (glow, gklow, ghigh, gkhigh), sums = refs[:-5], refs[-5:-1], refs[-1]
    value = total_ref[...]
    for part in got:
        value = value + part[...].astype(F32)
    sums[...] = value
    low_rows, high_rows, out = glow.shape[0], ghigh.shape[0], glow.shape[1]
    top = low_rows + high_rows
    glow[...] = sums[0:low_rows, 0:out]
    ghigh[...] = sums[low_rows:top, 0:out]
    for k in range(27):
        at, lane = top + k % 16, k // 16 * (out // 2)
        tap, row, col = k // 9, k // 3 % 3, k % 3
        gklow[tap, row, col : col + 1] = sums[at : at + 1, lane : lane + low_rows]
        gkhigh[tap, row, col : col + 1] = sums[at : at + 1, lane + low_rows : lane + top]


def on_device(teacher_input, conv_first, conv_second, student_low, student_high, kernel_low, kernel_high, adapter_low, adapter_high):
    clips, tiles = lax.axis_size("clip"), lax.axis_size("space")
    held, frames, rows, cols, depth = teacher_input.shape
    cells = held * frames
    out = conv_first.shape[-1]
    low_ch, high_ch = student_low.shape[-1], student_high.shape[-1]
    low_count = held * frames * rows * cols * clips * tiles
    scales = (1.0 / low_count, 1.0 / (4 * low_count))
    inner = rows - 4
    x = teacher_input.reshape(cells, rows, cols, depth)
    low = student_low.reshape(cells, rows, cols, low_ch)
    high = student_high.reshape(cells, 2 * rows, 2 * cols, high_ch)
    sems = pltpu.SemaphoreType.DMA

    def vm(*specs):
        return [pltpu.VMEM(shape, dtype) for shape, dtype in specs]

    packet = ((cells, 4, cols, max(out, low_ch, 2 * high_ch)), BF16)
    inner_spec = ((cells, rows - 2, cols, out), BF16)
    edge_spec = ((2, cells, 2, cols, out), F32)
    wc_spec = ((2, 2, 3, 2, 2, out, out), BF16)
    weights = ((kernel_low.shape, F32), (kernel_high.shape, F32), (adapter_low.shape, BF16), (adapter_high.shape, BF16))
    inner_feature, edge, first, second, w2, low_wide, high_wide, high_student, klow, khigh, plow, phigh = pl.pallas_call(
        functools.partial(first_kernel, frames),
        out_shape=tuple(
            vm(
                inner_spec,
                edge_spec,
                packet,
                packet,
                (conv_second.shape, BF16),
                (low.shape, F32),
                (high.shape, F32),
                ((cells, 2 * inner, 2 * cols, high_ch), BF16),
                *weights,
            )
        ),
        in_specs=[HBM] * 9,
        out_specs=(VMEM,) * 12,
        scratch_shapes=vm(
            (x.shape, BF16),
            (conv_first.shape, BF16),
            ((3, cells, rows + 2, cols, out), F32),
            (low.shape, BF16),
            (high.shape, BF16),
        )
        + [sems((18,))],
        compiler_params=pltpu.CompilerParams(vmem_limit_bytes=20 * MIB),
        cost_estimate=pl.CostEstimate(flops=3 * 10**9, bytes_accessed=9 * 10**6, transcendentals=0),
        name="teacher_first",
    )(*in_hbm(x, conv_first, conv_second, low, high, kernel_low, kernel_high, adapter_low, adapter_high))

    first_got = lax.ppermute(first, ("clip", "space"), swaps(clips, tiles, 0))
    second_got = lax.ppermute(second, ("clip", "space"), swaps(clips, tiles, 1))

    adapters = (((low_ch, out), F32), ((high_ch, out), F32))
    partial_sums = (((27, 8, low_ch), F32), ((27, 8, high_ch), F32))
    kernels = (((32, low_ch), F32), ((32, high_ch), F32))
    mismatch, wc, border_student, *sums = pl.pallas_call(
        functools.partial(second_kernel, frames, *scales),
        out_shape=(
            pltpu.HBM((cells, 2 * rows, 2 * cols, out), BF16),
            *vm(wc_spec, ((2, cells, 3, 2 * cols, high_ch), BF16), *adapters, *partial_sums),
        ),
        in_specs=[VMEM] * 9,
        out_specs=(HBM,) + (VMEM,) * 6,
        scratch_shapes=vm(
            ((cells, 2 * inner, 2 * cols, out), BF16),
            ((3, 1, cells, rows - 2, cols, out), BF16),
            ((1, cells, inner, 2, out // 128, 2 * cols, 128), F32),
            ((cells, rows - 2, cols, low_ch), BF16),
            ((cells, rows - 2, cols, low_ch), F32),
            ((cells, 2 * inner, 2 * cols, high_ch), F32),
        )
        + [sems((1,))],
        compiler_params=pltpu.CompilerParams(vmem_limit_bytes=20 * MIB),
        cost_estimate=pl.CostEstimate(flops=5 * 10**9, bytes_accessed=20 * 10**6, transcendentals=0),
        name="inner_rows",
    )(inner_feature, w2, low_wide, high_wide, high_student, klow, khigh, plow, phigh)

    shard_rows = low_ch // clips + high_ch // clips + 16
    shard_rows += -shard_rows % 16
    shard = (max(clips // 2, 1), shard_rows, out)
    mismatch, keep, send = pl.pallas_call(
        functools.partial(third_kernel, frames, clips, tiles, *scales),
        out_shape=(pltpu.HBM(mismatch.shape, BF16), *vm((shard, F32), (shard, BF16))),
        in_specs=[VMEM] * 16 + [HBM],
        out_specs=(HBM, VMEM, VMEM),
        input_output_aliases={16: 0},
        scratch_shapes=vm(
            *adapters,
            *kernels,
            ((2, cells, 4, 2 * cols, out), BF16),
            ((2, cells, cols, out), F32),
            ((3, 2, cells, 4, cols, out), BF16),
            ((2, cells, 2, 2, out // 128, 2 * cols, 128), F32),
            ((2, cells, 3, cols, low_ch), F32),
            ((2, cells, 6, 2 * cols, high_ch), F32),
            ((2, cells, 1, cols, low_ch), BF16),
            ((2, cells, 4, 2 * cols, high_ch), BF16),
            ((2, cells, 1, cols, low_ch), F32),
            ((2, cells, 4, 2 * cols, high_ch), F32),
            ((clips, shard_rows, out), F32),
        )
        + [sems((2,))],
        compiler_params=pltpu.CompilerParams(vmem_limit_bytes=20 * MIB),
        cost_estimate=pl.CostEstimate(flops=3 * 10**9, bytes_accessed=20 * 10**6, transcendentals=0),
        name="border_rows",
    )(first_got, second_got, edge, inner_feature, wc, border_student, *sums, low_wide, high_wide, klow, khigh, plow, phigh, *in_hbm(mismatch))

    total, got = sum_over_devices(keep, send, clips, tiles)
    low_rows, high_rows = low_ch // clips, high_ch // clips
    glow, gklow, ghigh, gkhigh = pl.pallas_call(
        unpack_kernel,
        out_shape=(
            jax.ShapeDtypeStruct((low_rows, out), F32),
            jax.ShapeDtypeStruct((3, 3, 3, low_rows), F32),
            jax.ShapeDtypeStruct((high_rows, out), F32),
            jax.ShapeDtypeStruct((3, 3, 3, high_rows), F32),
        ),
        in_specs=[VMEM] * (1 + len(got)),
        out_specs=(VMEM,) * 4,
        scratch_shapes=[pltpu.VMEM(shard[1:], F32)],
        compiler_params=pltpu.CompilerParams(vmem_limit_bytes=4 * MIB),
        name="unpack",
    )(total, *got)
    return glow, gklow, ghigh, gkhigh, mismatch.reshape(held, frames, 2 * rows, 2 * cols, out)


def solution(mesh):
    tiled = P("clip", None, "space", None, None)
    return jax.shard_map(
        on_device,
        mesh=mesh,
        in_specs=(tiled, P(), P(), tiled, tiled, P(), P(), P(), P()),
        out_specs=(P("clip", None), P(None, None, None, "clip"), P("clip", None), P(None, None, None, "clip"), tiled),
        check_vma=False,
    )
```

```python
import functools

import jax
import jax.numpy as jnp
from jax import lax
from jax.experimental import pallas as pl
from jax.experimental.pallas import tpu as pltpu
from jax.sharding import PartitionSpec as P

F32, BF16 = jnp.float32, jnp.bfloat16
HBM = pl.BlockSpec(memory_space=pltpu.HBM)
VMEM = pl.BlockSpec(memory_space=pltpu.VMEM)
MIB = 1 << 20


def in_hbm(*arrays):
    return [pltpu.with_memory_space_constraint(array, pltpu.HBM) for array in arrays]


def shift_cols(value, by):
    axis = value.ndim - 2
    count = value.shape[axis]
    column = lax.broadcasted_iota(jnp.int32, value.shape, axis)
    edge = 0 if by > 0 else count - 1
    return jnp.where(column == edge, 0.0, pltpu.roll(value, by % count, axis))


def silu(value):
    return value / (1.0 + jnp.exp(-value))


def dot(a, b):
    return jnp.dot(a, b, preferred_element_type=F32)


def dot_nt(a, b):
    return lax.dot_general(a, b, (((1,), (1,)), ((), ())), preferred_element_type=F32)


def dot_tn(a, b):
    return lax.dot_general(a, b, (((0,), (0,)), ((), ())), preferred_element_type=F32)


def frame_spans(frames):
    spans = []
    for tap in (1, 0, 2):
        off = tap - 1
        count = frames - abs(off)
        if count > 0:
            spans.append((tap, max(0, -off), max(0, off), count))
    return spans


def near_frames(cell, frames):
    frame = cell % frames
    near = [cell + t for t in (-1, 0, 1) if 0 <= frame + t < frames]
    return near, near[0] - cell + 1


class Copies:
    def __init__(self, sems):
        self.sems, self.count = sems, 0

    def start(self, src, dst):
        copy = pltpu.make_async_copy(src, dst, self.sems.at[self.count])
        self.count += 1
        copy.start()
        return copy


def phase_weights(w_ref, wc_ref):
    depth = w_ref.shape[-2]
    chunk = 16

    def step(tap, at):
        rows = slice(at, at + chunk)
        taps = [[w_ref[tap, h, w, rows].astype(F32) for w in range(3)] for h in range(3)]
        for p in range(2):
            if p == 0:
                merged = (taps[0], [taps[1][w] + taps[2][w] for w in range(3)])
            else:
                merged = ([taps[0][w] + taps[1][w] for w in range(3)], taps[2])
            for a in range(2):
                m = merged[a]
                wc_ref[p, 0, tap, a, 0, rows] = m[0].astype(BF16)
                wc_ref[p, 0, tap, a, 1, rows] = (m[1] + m[2]).astype(BF16)
                wc_ref[p, 1, tap, a, 0, rows] = (m[0] + m[1]).astype(BF16)
                wc_ref[p, 1, tap, a, 1, rows] = m[2].astype(BF16)

    return [functools.partial(step, tap, at) for tap in range(3) for at in range(0, depth, chunk)]


def widen(field, wide):
    def step(cell, row):
        wide[cell, row] = field[cell, row].astype(F32)

    return [functools.partial(step, cell, row) for cell in range(field.shape[0]) for row in range(field.shape[1])]


def gate_rows(feature):
    gated = silu(feature)
    return shift_cols(gated, 1).astype(BF16), gated.astype(BF16), shift_cols(gated, -1).astype(BF16)


def second_feature(frames, gated, wc_ref, count, fine):
    _, groups, cells, _, cols, out = gated.shape
    size = groups * count * cols
    for p in range(2):
        for q in range(2):
            fields = [
                jnp.concatenate(
                    [
                        gated[q + b, :, cell, p + a : p + a + count].reshape(size, out)
                        for a in range(2)
                        for b in range(2)
                    ],
                    axis=1,
                )
                for cell in range(cells)
            ]
            weights = [wc_ref[p, q, tap].reshape(4 * out, out) for tap in range(3)]
            center = dot(jnp.concatenate(fields, axis=0), weights[1])
            for cell in range(cells):
                near, first_tap = near_frames(cell, frames)
                product = center[cell * size : (cell + 1) * size]
                for t, other in enumerate(near):
                    if other != cell:
                        product = product + dot(fields[other], weights[t + first_tap])
                product = product.reshape(groups, count, cols, out)
                for group in range(groups):
                    for row in range(count):
                        for block in range(out // 128):
                            fine[group, cell, row, p, block, pl.ds(q, cols, stride=2), :] = product[
                                group, row, :, 128 * block : 128 * block + 128
                            ]


def depthwise(frames, padded, kernel_ref, student):
    cells, rows, _, channels = student.shape

    def step(cell, row, lane):
        near, first_tap = near_frames(cell, frames)
        lanes = pl.ds(lane, 128)
        sums = [None, None, None]
        for t, other in enumerate(near):
            for h in range(3):
                field = padded[other, row + h, :, lanes]
                for w in range(3):
                    term = field * kernel_ref[t + first_tap, h, w : w + 1, lanes]
                    sums[w] = term if sums[w] is None else sums[w] + term
        total = padded[cell, row + 1, :, lanes] + sums[1] + shift_cols(sums[0], 1) + shift_cols(sums[2], -1)
        student[cell, row, :, lanes] = total.astype(BF16)

    return [
        functools.partial(step, cell, row, lane)
        for cell in range(cells)
        for lane in range(0, channels, 128)
        for row in range(rows)
    ]


def kernel_gradient(frames, blocks, start, finish):
    channels = blocks[0][1].shape[-1]
    for lane in range(0, channels, 128):
        lanes = pl.ds(lane, 128)
        sums = tuple(start(k, lanes) for k in range(27))
        for padded, back in blocks:
            cells, rows = back.shape[:2]
            for cell in range(cells):
                near, first_tap = near_frames(cell, frames)

                def body(row, sums, padded=padded, back=back, cell=cell, near=near, first_tap=first_tap, lanes=lanes):
                    sums = list(sums)
                    center = back[cell, row, :, lanes]
                    moved = (shift_cols(center, -1), center, shift_cols(center, 1))
                    for t, other in enumerate(near):
                        for h in range(3):
                            field = padded[other, row + h, :, lanes]
                            for w in range(3):
                                k = 9 * (t + first_tap) + 3 * h + w
                                term = (moved[w] * field).reshape(-1, 8, 128)
                                sums[k] = sums[k] + jnp.sum(term, axis=0)
                    return tuple(sums)

                sums = lax.fori_loop(0, rows, body, sums) if rows > 1 else body(0, sums)
        for k in range(27):
            finish(k, lanes, sums[k])


def level(student, target, adapter, scale, grad):
    mismatch = dot(student, adapter) - target
    residual = (mismatch * scale).astype(BF16)
    grad[...] += dot_tn(student, residual)
    return mismatch, dot_nt(residual, adapter)


def fine_target(fine, rows):
    blocks = fine.shape[2]
    value = jnp.concatenate([fine[rows, :, block].reshape(-1, 128) for block in range(blocks)], axis=1)
    return value.astype(BF16).astype(F32)


def first_kernel(
    frames, x_hbm, w_hbm, w2_hbm, low_hbm, high_hbm, klow_hbm, khigh_hbm, plow_hbm, phigh_hbm,
    inner, edge, first, second, w2, low_wide, high_wide, high_student, klow, khigh, plow, phigh,
    x_ref, w_buf, acc, low, high, sems,
):
    cells, rows, cols, depth = x_ref.shape
    out = w_buf.shape[-1]
    clips = cells // frames
    spans = frame_spans(frames)
    copies = Copies(sems)
    load_x = copies.start(x_hbm, x_ref)
    loads = {}
    for tap_h in (1, 0, 2):
        loads[1, tap_h] = copies.start(w_hbm.at[1, tap_h], w_buf.at[1, tap_h])
    fields = [
        copies.start(high_hbm, high),
        copies.start(khigh_hbm, khigh),
        copies.start(low_hbm, low),
        copies.start(klow_hbm, klow),
    ]
    for tap, _, _, _ in spans[1:]:
        for tap_h in (1, 0, 2):
            loads[tap, tap_h] = copies.start(w_hbm.at[tap, tap_h], w_buf.at[tap, tap_h])
    late = [copies.start(plow_hbm, plow), copies.start(phigh_hbm, phigh), copies.start(w2_hbm, w2)]
    for tap_w in range(3):
        acc[tap_w, :, 0:1] = jnp.zeros((cells, 1, cols, out), F32)
        acc[tap_w, :, rows + 1 : rows + 2] = jnp.zeros((cells, 1, cols, out), F32)

    students = (
        widen(high, high_wide)
        + widen(low, low_wide)
        + depthwise(frames, high_wide.at[:, 3 : 2 * rows - 3], khigh, high_student)
    )
    load_x.wait()
    pending, share = [], 0
    for number, (tap, to, src, count) in enumerate(spans):
        for tap_h in (1, 0, 2):
            loads[tap, tap_h].wait()
            if number == 0 and tap_h == 0:
                for copy in fields:
                    copy.wait()
                pending = list(students)
                share = -(-len(pending) // (9 * len(spans) - 3))
            at = 2 - tap_h
            for tap_w in range(3):
                weight = w_buf[tap, tap_h, tap_w]
                for clip in range(clips):
                    base = clip * frames
                    rowset = x_ref[base + src : base + src + count].reshape(-1, depth)
                    product = dot(rowset, weight).reshape(count, rows, cols, out)
                    spot = (tap_w, pl.ds(base + to, count), pl.ds(at, rows))
                    if tap == 1 and tap_h == 1:
                        acc[spot] = product
                    else:
                        acc[spot] = acc[spot] + product
                for step in pending[:share]:
                    step()
                pending = pending[share:]
    for step in pending:
        step()

    def gathered(cell, row):
        return acc[1, cell, row] + shift_cols(acc[0, cell, row], 1) + shift_cols(acc[2, cell, row], -1)

    for copy in late:
        copy.wait()
    low_ch, high_ch = low.shape[-1], high.shape[-1]
    even = lax.rem(lax.axis_index("space"), 2) == 0
    for cell in range(cells):
        for j in range(2):
            up, down = gathered(cell, j), gathered(cell, rows + j)
            edge[0, cell, j], edge[1, cell, j] = up, down
            first[cell, j, :, 0:out] = jnp.where(even, down, up).astype(BF16)
            second[cell, j, :, 0:out] = jnp.where(even, up, down).astype(BF16)
        up, down = low_wide[cell, 0], low_wide[cell, rows - 1]
        first[cell, 2, :, 0:low_ch] = jnp.where(even, down, up).astype(BF16)
        second[cell, 2, :, 0:low_ch] = jnp.where(even, up, down).astype(BF16)
        for half in range(2):
            here, lanes = slice(half * cols, (half + 1) * cols), slice(half * high_ch, (half + 1) * high_ch)
            up, down = high_wide[cell, 0, here], high_wide[cell, 2 * rows - 1, here]
            first[cell, 3, :, lanes] = jnp.where(even, down, up).astype(BF16)
            second[cell, 3, :, lanes] = jnp.where(even, up, down).astype(BF16)
    for cell in range(cells):

        def gather(row, _, cell=cell):
            inner[cell, row] = gathered(cell, row + 2).astype(BF16)
            return 0

        lax.fori_loop(0, rows - 2, gather, 0)


def second_kernel(
    frames, scale_low, scale_high,
    feature, w2, low_wide, high_wide, high_student, klow, khigh, plow, phigh,
    mismatch_hbm, wc, border_student, glow, ghigh, gklow, gkhigh,
    mismatch, gated, fine, low_student, low_back, high_back, sems,
):
    cells, count, cols, out = feature.shape
    rows = count + 2
    inner = rows - 4
    copies = Copies(sems)
    for cell in range(cells):

        def gate(row, _, cell=cell):
            for k, value in enumerate(gate_rows(feature[cell, row].astype(F32))):
                gated[k, 0, cell, row] = value
            return 0

        lax.fori_loop(0, count, gate, 0)
    for step in depthwise(frames, low_wide, klow, low_student) + phase_weights(w2, wc):
        step()
    second_feature(frames, gated, wc, inner, fine)
    for side, top in ((0, 0), (1, 2 * rows - 5)):
        for step in depthwise(frames, high_wide.at[:, top : top + 5], khigh, border_student.at[side]):
            step()

    glow[...] = jnp.zeros_like(glow)
    ghigh[...] = jnp.zeros_like(ghigh)
    for cell in range(cells):
        student = high_student[cell].reshape(-1, high_student.shape[-1])
        target = fine_target(fine.at[0, cell], slice(0, inner))
        value, back = level(student, target, phigh[...], scale_high, ghigh)
        mismatch[cell] = value.astype(BF16).reshape(2 * inner, 2 * cols, out)
        high_back[cell] = back.reshape(2 * inner, 2 * cols, -1)
    store = copies.start(mismatch, mismatch_hbm.at[:, pl.ds(4, 2 * inner)])
    student = low_student[...].reshape(-1, low_student.shape[-1])
    target = feature[...].reshape(-1, out).astype(F32)
    _, back = level(student, target, plow[...], scale_low, glow)
    low_back[...] = back.reshape(low_back.shape)
    for blocks, total in (([(low_wide, low_back)], gklow), ([(high_wide.at[:, 3 : 2 * rows - 3], high_back)], gkhigh)):

        def keep(k, lanes, sums, total=total):
            total[k, :, lanes] = sums

        kernel_gradient(frames, blocks, lambda k, lanes: jnp.zeros((8, 128), F32), keep)
    store.wait()


def third_kernel(
    frames, shards, tiles, scale_low, scale_high,
    first, second, edge, inner, wc, border_student, glow_in, ghigh_in, gklow_in, gkhigh_in, low_wide, high_wide, klow, khigh, plow, phigh, mismatch_in,
    mismatch_hbm, keep, send,
    glow, ghigh, gklow, gkhigh, mismatch,
    feature, gated, fine, low_pad, high_pad, low_student, high_student, low_back, high_back, shard_sums, sems,
):
    del mismatch_in
    _, cells, _, cols, out = edge.shape
    rows = inner.shape[1] + 2
    low_ch, high_ch = low_wide.shape[-1], high_wide.shape[-1]
    mine, tile = lax.axis_index("clip"), lax.axis_index("space")
    even = lax.rem(tile, 2) == 0
    outside = (tile == 0, tile == tiles - 1)
    copies = Copies(sems)
    glow[...] = glow_in[...]
    ghigh[...] = ghigh_in[...]
    gklow[27:] = jnp.zeros_like(gklow[27:])
    gkhigh[27:] = jnp.zeros_like(gkhigh[27:])

    def border_gradient(padded, back, part, total):
        def finish(k, lanes, sums):
            total[k : k + 1, lanes] = jnp.sum(sums, axis=0, keepdims=True)

        kernel_gradient(
            frames, [(padded.at[side], back.at[side]) for side in range(2)], lambda k, lanes: part[k, :, lanes], finish
        )

    def halo(side, cell, row):
        ours, other = first[cell, row].astype(F32), second[cell, row].astype(F32)
        found = jnp.where(even, other, ours) if side == 0 else jnp.where(even, ours, other)
        return jnp.where(outside[side], 0.0, found)

    for side in range(2):
        for cell in range(cells):
            for k in range(2):
                whole = (edge[side, cell, k] + halo(side, cell, k)[:, 0:out]).astype(BF16).astype(F32)
                if k == side:
                    whole = jnp.where(outside[side], 0.0, whole)
                else:
                    feature[side, cell] = whole
                for j, value in enumerate(gate_rows(whole)):
                    gated[j, side, cell, 2 * side + k] = value
                for j, value in enumerate(gate_rows(inner[cell, side * (rows - 4) + k].astype(F32))):
                    gated[j, side, cell, 2 - 2 * side + k] = value

    second_feature(frames, gated, wc, 2, fine)

    for side in range(2):
        for cell in range(cells):
            low_halo, high_halo = halo(side, cell, 2), halo(side, cell, 3)
            at = 0 if side == 0 else 2
            low_pad[side, cell, at] = low_halo[:, 0:low_ch]
            low_pad[side, cell, pl.ds(1 - side, 2)] = low_wide[cell, pl.ds(side * (rows - 2), 2)]
            at = 0 if side == 0 else 5
            high_pad[side, cell, at, 0:cols] = high_halo[:, 0:high_ch]
            high_pad[side, cell, at, cols:] = high_halo[:, high_ch : 2 * high_ch]
            high_pad[side, cell, pl.ds(1 - side, 5)] = high_wide[cell, pl.ds(side * (2 * rows - 5), 5)]
        at = 3 * side
        for step in depthwise(frames, high_pad.at[side, :, at : at + 3], khigh, high_student.at[side, :, at : at + 1]):
            step()
        for cell in range(cells):
            high_student[side, cell, 1 - side : 4 - side] = border_student[side, cell]
        for step in depthwise(frames, low_pad.at[side], klow, low_student.at[side]):
            step()

    student = low_student[...].reshape(-1, low_ch)
    _, back = level(student, feature[...].reshape(-1, out), plow[...], scale_low, glow)
    low_back[...] = back.reshape(low_back.shape)
    border_gradient(low_pad, low_back, gklow_in, gklow)

    for side in range(2):
        student = high_student[side].reshape(-1, high_ch)
        target = jnp.concatenate([fine_target(fine.at[side, cell], slice(0, 2)) for cell in range(cells)], axis=0)
        value, back = level(student, target, phigh[...], scale_high, ghigh)
        mismatch[side] = value.astype(BF16).reshape(mismatch.shape[1:])
        high_back[side] = back.reshape(high_back.shape[1:])
    stores = [
        copies.start(mismatch.at[0], mismatch_hbm.at[:, pl.ds(0, 4)]),
        copies.start(mismatch.at[1], mismatch_hbm.at[:, pl.ds(2 * rows - 4, 4)]),
    ]
    border_gradient(high_pad, high_back, gkhigh_in, gkhigh)

    low_rows, high_rows = low_ch // shards, high_ch // shards
    shard_sums[...] = jnp.zeros_like(shard_sums)
    width = gklow.shape[1]
    half = out // 2
    lane = lax.broadcasted_iota(jnp.int32, gklow.shape, 1)
    wide_high = gkhigh[...]
    if high_ch < width:
        wide_high = jnp.concatenate([wide_high, jnp.zeros((wide_high.shape[0], width - high_ch), F32)], axis=1)
    for s in range(shards):
        shard_sums[s, 0:low_rows, 0:out] = glow[s * low_rows : (s + 1) * low_rows]
        shard_sums[s, low_rows : low_rows + high_rows, 0:out] = ghigh[s * high_rows : (s + 1) * high_rows]
        from_low = pltpu.roll(gklow[...], (width - s * low_rows) % width, 1)
        from_high = pltpu.roll(wide_high, (width + low_rows - s * high_rows) % width, 1)
        both = jnp.where(lane < low_rows, from_low, jnp.where(lane < low_rows + high_rows, from_high, 0.0))
        top = low_rows + high_rows
        shard_sums[s, top : top + 16, 0:half] = both[0:16, 0:half]
        shard_sums[s, top : top + 16, half : 2 * half] = both[16:32, 0:half]
    if shards == 1:
        keep[0] = shard_sums[0]
        send[0] = shard_sums[0].astype(BF16)
    else:
        bit = lax.rem(mine, 2)
        for k in range(shards // 2):
            keep[k] = shard_sums[2 * k + bit]
            send[k] = shard_sums[2 * k + 1 - bit].astype(BF16)
    for copy in stores:
        copy.wait()


def swaps(clips, tiles, start):
    found = []
    for clip in range(clips):
        for tile in range(tiles):
            other = tile + 1 if (tile - start) % 2 == 0 else tile - 1
            if 0 <= other < tiles:
                found.append((clip * tiles + tile, clip * tiles + other))
            elif clips % 2 == 0:
                found.append((clip * tiles + tile, (clip ^ 1) * tiles + tile))
    return found


def pairs(count, bit):
    return [(i, i ^ bit) for i in range(count)]


def split_shards(keep, bit):
    halves = keep.reshape((keep.shape[0] // 2, 2) + keep.shape[1:])
    own = lax.rem(lax.div(lax.axis_index("clip"), bit), 2)
    send = lax.dynamic_index_in_dim(halves, 1 - own, 1, False).astype(BF16)
    return lax.dynamic_index_in_dim(halves, own, 1, False), send


def sum_over_devices(keep, send, clips, tiles):
    clip_bit, tile_bit = 2, 1
    if clips > 1:
        keep = keep + lax.ppermute(send, "clip", pairs(clips, 1)).astype(F32)
    if clips > 2 and tiles > 1:
        keep, send = split_shards(keep, 2)
        across = [(c * tiles + t, (c ^ 2) * tiles + (t ^ 1)) for c in range(clips) for t in range(tiles)]
        got = (
            lax.ppermute(keep.astype(BF16), "space", pairs(tiles, 1)),
            lax.ppermute(send, "clip", pairs(clips, 2)),
            lax.ppermute(send, ("clip", "space"), across),
        )
        for part in got:
            keep = keep + part.astype(F32)
        clip_bit, tile_bit = 4, 2
    while clip_bit < clips:
        keep, send = split_shards(keep, clip_bit)
        keep = keep + lax.ppermute(send, "clip", pairs(clips, clip_bit)).astype(F32)
        clip_bit *= 2
    total, got = keep[0], []
    while tile_bit < tiles:
        for part in got:
            total = total + part.astype(F32)
        bits = (tile_bit, 2 * tile_bit, 3 * tile_bit) if 2 * tile_bit < tiles else (tile_bit,)
        out = total.astype(BF16)
        got = [lax.ppermute(out, "space", pairs(tiles, b)) for b in bits[::-1]]
        tile_bit *= 2 ** (2 if len(bits) > 1 else 1)
    return total, got


def unpack_kernel(total_ref, *refs):
    got, (glow, gklow, ghigh, gkhigh), sums = refs[:-5], refs[-5:-1], refs[-1]
    value = total_ref[...]
    for part in got:
        value = value + part[...].astype(F32)
    sums[...] = value
    low_rows, high_rows, out = glow.shape[0], ghigh.shape[0], glow.shape[1]
    top = low_rows + high_rows
    glow[...] = sums[0:low_rows, 0:out]
    ghigh[...] = sums[low_rows:top, 0:out]
    for k in range(27):
        at, lane = top + k % 16, k // 16 * (out // 2)
        tap, row, col = k // 9, k // 3 % 3, k % 3
        gklow[tap, row, col : col + 1] = sums[at : at + 1, lane : lane + low_rows]
        gkhigh[tap, row, col : col + 1] = sums[at : at + 1, lane + low_rows : lane + top]


def on_device(teacher_input, conv_first, conv_second, student_low, student_high, kernel_low, kernel_high, adapter_low, adapter_high):
    clips, tiles = lax.axis_size("clip"), lax.axis_size("space")
    held, frames, rows, cols, depth = teacher_input.shape
    cells = held * frames
    out = conv_first.shape[-1]
    low_ch, high_ch = student_low.shape[-1], student_high.shape[-1]
    low_count = held * frames * rows * cols * clips * tiles
    scales = (1.0 / low_count, 1.0 / (4 * low_count))
    inner = rows - 4
    x = teacher_input.reshape(cells, rows, cols, depth)
    low = student_low.reshape(cells, rows, cols, low_ch)
    high = student_high.reshape(cells, 2 * rows, 2 * cols, high_ch)
    sems = pltpu.SemaphoreType.DMA

    def vm(*specs):
        return [pltpu.VMEM(shape, dtype) for shape, dtype in specs]

    packet = ((cells, 4, cols, max(out, low_ch, 2 * high_ch)), BF16)
    inner_spec = ((cells, rows - 2, cols, out), BF16)
    edge_spec = ((2, cells, 2, cols, out), F32)
    wc_spec = ((2, 2, 3, 2, 2, out, out), BF16)
    weights = ((kernel_low.shape, F32), (kernel_high.shape, F32), (adapter_low.shape, BF16), (adapter_high.shape, BF16))
    inner_feature, edge, first, second, w2, low_wide, high_wide, high_student, klow, khigh, plow, phigh = pl.pallas_call(
        functools.partial(first_kernel, frames),
        out_shape=tuple(
            vm(
                inner_spec,
                edge_spec,
                packet,
                packet,
                (conv_second.shape, BF16),
                (low.shape, F32),
                (high.shape, F32),
                ((cells, 2 * inner, 2 * cols, high_ch), BF16),
                *weights,
            )
        ),
        in_specs=[HBM] * 9,
        out_specs=(VMEM,) * 12,
        scratch_shapes=vm(
            (x.shape, BF16),
            (conv_first.shape, BF16),
            ((3, cells, rows + 2, cols, out), F32),
            (low.shape, BF16),
            (high.shape, BF16),
        )
        + [sems((18,))],
        compiler_params=pltpu.CompilerParams(vmem_limit_bytes=20 * MIB),
        cost_estimate=pl.CostEstimate(flops=3 * 10**9, bytes_accessed=9 * 10**6, transcendentals=0),
        name="teacher_first",
    )(*in_hbm(x, conv_first, conv_second, low, high, kernel_low, kernel_high, adapter_low, adapter_high))

    first_got = lax.ppermute(first, ("clip", "space"), swaps(clips, tiles, 0))
    second_got = lax.ppermute(second, ("clip", "space"), swaps(clips, tiles, 1))

    adapters = (((low_ch, out), F32), ((high_ch, out), F32))
    partial_sums = (((27, 8, low_ch), F32), ((27, 8, high_ch), F32))
    kernels = (((32, low_ch), F32), ((32, high_ch), F32))
    mismatch, wc, border_student, *sums = pl.pallas_call(
        functools.partial(second_kernel, frames, *scales),
        out_shape=(
            pltpu.HBM((cells, 2 * rows, 2 * cols, out), BF16),
            *vm(wc_spec, ((2, cells, 3, 2 * cols, high_ch), BF16), *adapters, *partial_sums),
        ),
        in_specs=[VMEM] * 9,
        out_specs=(HBM,) + (VMEM,) * 6,
        scratch_shapes=vm(
            ((cells, 2 * inner, 2 * cols, out), BF16),
            ((3, 1, cells, rows - 2, cols, out), BF16),
            ((1, cells, inner, 2, out // 128, 2 * cols, 128), F32),
            ((cells, rows - 2, cols, low_ch), BF16),
            ((cells, rows - 2, cols, low_ch), F32),
            ((cells, 2 * inner, 2 * cols, high_ch), F32),
        )
        + [sems((1,))],
        compiler_params=pltpu.CompilerParams(vmem_limit_bytes=20 * MIB),
        cost_estimate=pl.CostEstimate(flops=5 * 10**9, bytes_accessed=20 * 10**6, transcendentals=0),
        name="inner_rows",
    )(inner_feature, w2, low_wide, high_wide, high_student, klow, khigh, plow, phigh)

    shard_rows = low_ch // clips + high_ch // clips + 16
    shard_rows += -shard_rows % 16
    shard = (max(clips // 2, 1), shard_rows, out)
    mismatch, keep, send = pl.pallas_call(
        functools.partial(third_kernel, frames, clips, tiles, *scales),
        out_shape=(pltpu.HBM(mismatch.shape, BF16), *vm((shard, F32), (shard, BF16))),
        in_specs=[VMEM] * 16 + [HBM],
        out_specs=(HBM, VMEM, VMEM),
        input_output_aliases={16: 0},
        scratch_shapes=vm(
            *adapters,
            *kernels,
            ((2, cells, 4, 2 * cols, out), BF16),
            ((2, cells, cols, out), F32),
            ((3, 2, cells, 4, cols, out), BF16),
            ((2, cells, 2, 2, out // 128, 2 * cols, 128), F32),
            ((2, cells, 3, cols, low_ch), F32),
            ((2, cells, 6, 2 * cols, high_ch), F32),
            ((2, cells, 1, cols, low_ch), BF16),
            ((2, cells, 4, 2 * cols, high_ch), BF16),
            ((2, cells, 1, cols, low_ch), F32),
            ((2, cells, 4, 2 * cols, high_ch), F32),
            ((clips, shard_rows, out), F32),
        )
        + [sems((2,))],
        compiler_params=pltpu.CompilerParams(vmem_limit_bytes=20 * MIB),
        cost_estimate=pl.CostEstimate(flops=3 * 10**9, bytes_accessed=20 * 10**6, transcendentals=0),
        name="border_rows",
    )(first_got, second_got, edge, inner_feature, wc, border_student, *sums, low_wide, high_wide, klow, khigh, plow, phigh, *in_hbm(mismatch))

    total, got = sum_over_devices(keep, send, clips, tiles)
    low_rows, high_rows = low_ch // clips, high_ch // clips
    glow, gklow, ghigh, gkhigh = pl.pallas_call(
        unpack_kernel,
        out_shape=(
            jax.ShapeDtypeStruct((low_rows, out), F32),
            jax.ShapeDtypeStruct((3, 3, 3, low_rows), F32),
            jax.ShapeDtypeStruct((high_rows, out), F32),
            jax.ShapeDtypeStruct((3, 3, 3, high_rows), F32),
        ),
        in_specs=[VMEM] * (1 + len(got)),
        out_specs=(VMEM,) * 4,
        scratch_shapes=[pltpu.VMEM(shard[1:], F32)],
        compiler_params=pltpu.CompilerParams(vmem_limit_bytes=4 * MIB),
        name="unpack",
    )(total, *got)
    return glow, gklow, ghigh, gkhigh, mismatch.reshape(held, frames, 2 * rows, 2 * cols, out)


def solution(mesh):
    tiled = P("clip", None, "space", None, None)
    return jax.shard_map(
        on_device,
        mesh=mesh,
        in_specs=(tiled, P(), P(), tiled, tiled, P(), P(), P(), P()),
        out_specs=(P("clip", None), P(None, None, None, "clip"), P("clip", None), P(None, None, None, "clip"), tiled),
        check_vma=False,
    )
```

```python
import functools

import jax
import jax.numpy as jnp
from jax import lax
from jax.experimental import pallas as pl
from jax.experimental.pallas import tpu as pltpu
from jax.sharding import PartitionSpec as P

F32, BF16 = jnp.float32, jnp.bfloat16
HBM = pl.BlockSpec(memory_space=pltpu.HBM)
VMEM = pl.BlockSpec(memory_space=pltpu.VMEM)
MIB = 1 << 20


def in_hbm(*arrays):
    return [pltpu.with_memory_space_constraint(array, pltpu.HBM) for array in arrays]


def shift_cols(value, by):
    axis = value.ndim - 2
    count = value.shape[axis]
    column = lax.broadcasted_iota(jnp.int32, value.shape, axis)
    edge = 0 if by > 0 else count - 1
    return jnp.where(column == edge, 0.0, pltpu.roll(value, by % count, axis))


def silu(value):
    return value / (1.0 + jnp.exp(-value))


def dot(a, b):
    return jnp.dot(a, b, preferred_element_type=F32)


def dot_nt(a, b):
    return lax.dot_general(a, b, (((1,), (1,)), ((), ())), preferred_element_type=F32)


def dot_tn(a, b):
    return lax.dot_general(a, b, (((0,), (0,)), ((), ())), preferred_element_type=F32)


def frame_spans(frames):
    spans = []
    for tap in (1, 0, 2):
        off = tap - 1
        count = frames - abs(off)
        if count > 0:
            spans.append((tap, max(0, -off), max(0, off), count))
    return spans


def near_frames(cell, frames):
    frame = cell % frames
    near = [cell + t for t in (-1, 0, 1) if 0 <= frame + t < frames]
    return near, near[0] - cell + 1


class Copies:
    def __init__(self, sems):
        self.sems, self.count = sems, 0

    def start(self, src, dst):
        copy = pltpu.make_async_copy(src, dst, self.sems.at[self.count])
        self.count += 1
        copy.start()
        return copy


def phase_weights(w_ref, wc_ref):
    depth = w_ref.shape[-2]
    chunk = 16

    def step(tap, at):
        rows = slice(at, at + chunk)
        taps = [[w_ref[tap, h, w, rows].astype(F32) for w in range(3)] for h in range(3)]
        for p in range(2):
            if p == 0:
                merged = (taps[0], [taps[1][w] + taps[2][w] for w in range(3)])
            else:
                merged = ([taps[0][w] + taps[1][w] for w in range(3)], taps[2])
            for a in range(2):
                m = merged[a]
                wc_ref[p, 0, tap, a, 0, rows] = m[0].astype(BF16)
                wc_ref[p, 0, tap, a, 1, rows] = (m[1] + m[2]).astype(BF16)
                wc_ref[p, 1, tap, a, 0, rows] = (m[0] + m[1]).astype(BF16)
                wc_ref[p, 1, tap, a, 1, rows] = m[2].astype(BF16)

    return [functools.partial(step, tap, at) for tap in range(3) for at in range(0, depth, chunk)]


def widen(field, wide):
    def step(cell, row):
        wide[cell, row] = field[cell, row].astype(F32)

    return [functools.partial(step, cell, row) for cell in range(field.shape[0]) for row in range(field.shape[1])]


def gate_rows(feature):
    gated = silu(feature)
    return shift_cols(gated, 1).astype(BF16), gated.astype(BF16), shift_cols(gated, -1).astype(BF16)


def second_feature(frames, gated, wc_ref, count, fine):
    _, groups, cells, _, cols, out = gated.shape
    size = groups * count * cols
    for p in range(2):
        for q in range(2):
            fields = [
                jnp.concatenate(
                    [
                        gated[q + b, :, cell, p + a : p + a + count].reshape(size, out)
                        for a in range(2)
                        for b in range(2)
                    ],
                    axis=1,
                )
                for cell in range(cells)
            ]
            weights = [wc_ref[p, q, tap].reshape(4 * out, out) for tap in range(3)]
            center = dot(jnp.concatenate(fields, axis=0), weights[1])
            for cell in range(cells):
                near, first_tap = near_frames(cell, frames)
                product = center[cell * size : (cell + 1) * size]
                for t, other in enumerate(near):
                    if other != cell:
                        product = product + dot(fields[other], weights[t + first_tap])
                product = product.reshape(groups, count, cols, out)
                for group in range(groups):
                    for row in range(count):
                        for block in range(out // 128):
                            fine[group, cell, row, p, block, pl.ds(q, cols, stride=2), :] = product[
                                group, row, :, 128 * block : 128 * block + 128
                            ]


def depthwise(frames, padded, kernel_ref, student):
    cells, rows, _, channels = student.shape

    def step(cell, row, lane):
        near, first_tap = near_frames(cell, frames)
        lanes = pl.ds(lane, 128)
        sums = [None, None, None]
        for t, other in enumerate(near):
            for h in range(3):
                field = padded[other, row + h, :, lanes]
                for w in range(3):
                    term = field * kernel_ref[t + first_tap, h, w : w + 1, lanes]
                    sums[w] = term if sums[w] is None else sums[w] + term
        total = padded[cell, row + 1, :, lanes] + sums[1] + shift_cols(sums[0], 1) + shift_cols(sums[2], -1)
        student[cell, row, :, lanes] = total.astype(BF16)

    return [
        functools.partial(step, cell, row, lane)
        for cell in range(cells)
        for lane in range(0, channels, 128)
        for row in range(rows)
    ]


def kernel_gradient(frames, blocks, start, finish):
    channels = blocks[0][1].shape[-1]
    for lane in range(0, channels, 128):
        lanes = pl.ds(lane, 128)
        sums = tuple(start(k, lanes) for k in range(27))
        for padded, back in blocks:
            cells, rows = back.shape[:2]
            for cell in range(cells):
                near, first_tap = near_frames(cell, frames)

                def body(row, sums, padded=padded, back=back, cell=cell, near=near, first_tap=first_tap, lanes=lanes):
                    sums = list(sums)
                    center = back[cell, row, :, lanes]
                    moved = (shift_cols(center, -1), center, shift_cols(center, 1))
                    for t, other in enumerate(near):
                        for h in range(3):
                            field = padded[other, row + h, :, lanes]
                            for w in range(3):
                                k = 9 * (t + first_tap) + 3 * h + w
                                term = (moved[w] * field).reshape(-1, 8, 128)
                                sums[k] = sums[k] + jnp.sum(term, axis=0)
                    return tuple(sums)

                sums = lax.fori_loop(0, rows, body, sums) if rows > 1 else body(0, sums)
        for k in range(27):
            finish(k, lanes, sums[k])


def level(student, target, adapter, scale, grad):
    mismatch = dot(student, adapter) - target
    residual = (mismatch * scale).astype(BF16)
    grad[...] += dot_tn(student, residual)
    return mismatch, dot_nt(residual, adapter)


def fine_target(fine, rows):
    blocks = fine.shape[2]
    value = jnp.concatenate([fine[rows, :, block].reshape(-1, 128) for block in range(blocks)], axis=1)
    return value.astype(BF16).astype(F32)


def first_kernel(
    frames, x_hbm, w_hbm, w2_hbm, low_hbm, high_hbm, klow_hbm, khigh_hbm, plow_hbm, phigh_hbm,
    inner, edge, first, second, w2, low_wide, high_wide, high_student, klow, khigh, plow, phigh,
    x_ref, w_buf, acc, low, high, sems,
):
    cells, rows, cols, depth = x_ref.shape
    out = w_buf.shape[-1]
    clips = cells // frames
    spans = frame_spans(frames)
    copies = Copies(sems)
    load_x = copies.start(x_hbm, x_ref)
    loads = {}
    for tap_h in (1, 0, 2):
        loads[1, tap_h] = copies.start(w_hbm.at[1, tap_h], w_buf.at[1, tap_h])
    fields = [
        copies.start(high_hbm, high),
        copies.start(khigh_hbm, khigh),
        copies.start(low_hbm, low),
        copies.start(klow_hbm, klow),
    ]
    for tap, _, _, _ in spans[1:]:
        for tap_h in (1, 0, 2):
            loads[tap, tap_h] = copies.start(w_hbm.at[tap, tap_h], w_buf.at[tap, tap_h])
    late = [copies.start(plow_hbm, plow), copies.start(phigh_hbm, phigh), copies.start(w2_hbm, w2)]
    for tap_w in range(3):
        acc[tap_w, :, 0:1] = jnp.zeros((cells, 1, cols, out), F32)
        acc[tap_w, :, rows + 1 : rows + 2] = jnp.zeros((cells, 1, cols, out), F32)

    students = (
        widen(high, high_wide)
        + widen(low, low_wide)
        + depthwise(frames, high_wide.at[:, 3 : 2 * rows - 3], khigh, high_student)
    )
    load_x.wait()
    pending, share = [], 0
    for number, (tap, to, src, count) in enumerate(spans):
        for tap_h in (1, 0, 2):
            loads[tap, tap_h].wait()
            if number == 0 and tap_h == 0:
                for copy in fields:
                    copy.wait()
                pending = list(students)
                share = -(-len(pending) // (9 * len(spans) - 3))
            at = 2 - tap_h
            for tap_w in range(3):
                weight = w_buf[tap, tap_h, tap_w]
                for clip in range(clips):
                    base = clip * frames
                    rowset = x_ref[base + src : base + src + count].reshape(-1, depth)
                    product = dot(rowset, weight).reshape(count, rows, cols, out)
                    spot = (tap_w, pl.ds(base + to, count), pl.ds(at, rows))
                    if tap == 1 and tap_h == 1:
                        acc[spot] = product
                    else:
                        acc[spot] = acc[spot] + product
                for step in pending[:share]:
                    step()
                pending = pending[share:]
    for step in pending:
        step()

    def gathered(cell, row):
        return acc[1, cell, row] + shift_cols(acc[0, cell, row], 1) + shift_cols(acc[2, cell, row], -1)

    for copy in late:
        copy.wait()
    low_ch, high_ch = low.shape[-1], high.shape[-1]
    even = lax.rem(lax.axis_index("space"), 2) == 0
    for cell in range(cells):
        for j in range(2):
            up, down = gathered(cell, j), gathered(cell, rows + j)
            edge[0, cell, j], edge[1, cell, j] = up, down
            first[cell, j, :, 0:out] = jnp.where(even, down, up).astype(BF16)
            second[cell, j, :, 0:out] = jnp.where(even, up, down).astype(BF16)
        up, down = low_wide[cell, 0], low_wide[cell, rows - 1]
        first[cell, 2, :, 0:low_ch] = jnp.where(even, down, up).astype(BF16)
        second[cell, 2, :, 0:low_ch] = jnp.where(even, up, down).astype(BF16)
        for half in range(2):
            here, lanes = slice(half * cols, (half + 1) * cols), slice(half * high_ch, (half + 1) * high_ch)
            up, down = high_wide[cell, 0, here], high_wide[cell, 2 * rows - 1, here]
            first[cell, 3, :, lanes] = jnp.where(even, down, up).astype(BF16)
            second[cell, 3, :, lanes] = jnp.where(even, up, down).astype(BF16)
    for cell in range(cells):

        def gather(row, _, cell=cell):
            inner[cell, row] = gathered(cell, row + 2).astype(BF16)
            return 0

        lax.fori_loop(0, rows - 2, gather, 0)


def second_kernel(
    frames, scale_low, scale_high,
    feature, w2, low_wide, high_wide, high_student, klow, khigh, plow, phigh,
    mismatch_hbm, gated, wc, border_student, glow, ghigh, gklow, gkhigh,
    mismatch, fine, low_student, low_back, high_back, sems,
):
    cells, count, cols, out = feature.shape
    rows = count + 2
    inner = rows - 4
    copies = Copies(sems)
    for cell in range(cells):

        def gate(row, _, cell=cell):
            for k, value in enumerate(gate_rows(feature[cell, row].astype(F32))):
                gated[k, 0, cell, row] = value
            return 0

        lax.fori_loop(0, count, gate, 0)
    for step in depthwise(frames, low_wide, klow, low_student) + phase_weights(w2, wc):
        step()
    second_feature(frames, gated, wc, inner, fine)
    for side, top in ((0, 0), (1, 2 * rows - 5)):
        for step in depthwise(frames, high_wide.at[:, top : top + 5], khigh, border_student.at[side]):
            step()

    glow[...] = jnp.zeros_like(glow)
    ghigh[...] = jnp.zeros_like(ghigh)
    for cell in range(cells):
        student = high_student[cell].reshape(-1, high_student.shape[-1])
        target = fine_target(fine.at[0, cell], slice(0, inner))
        value, back = level(student, target, phigh[...], scale_high, ghigh)
        mismatch[cell] = value.astype(BF16).reshape(2 * inner, 2 * cols, out)
        high_back[cell] = back.reshape(2 * inner, 2 * cols, -1)
    store = copies.start(mismatch, mismatch_hbm.at[:, pl.ds(4, 2 * inner)])
    student = low_student[...].reshape(-1, low_student.shape[-1])
    target = feature[...].reshape(-1, out).astype(F32)
    _, back = level(student, target, plow[...], scale_low, glow)
    low_back[...] = back.reshape(low_back.shape)
    for blocks, total in (([(low_wide, low_back)], gklow), ([(high_wide.at[:, 3 : 2 * rows - 3], high_back)], gkhigh)):

        def keep(k, lanes, sums, total=total):
            total[k, :, lanes] = sums

        kernel_gradient(frames, blocks, lambda k, lanes: jnp.zeros((8, 128), F32), keep)
    store.wait()


def third_kernel(
    frames, shards, tiles, scale_low, scale_high,
    first, second, edge, inner, wc, border_student, glow_in, ghigh_in, gklow_in, gkhigh_in, low_wide, high_wide, klow, khigh, plow, phigh, mismatch_in,
    mismatch_hbm, keep, send,
    glow, ghigh, gklow, gkhigh, mismatch,
    feature, gated, fine, low_pad, high_pad, low_student, high_student, low_back, high_back, shard_sums, sems,
):
    del mismatch_in
    _, cells, _, cols, out = edge.shape
    rows = inner.shape[3] + 2
    low_ch, high_ch = low_wide.shape[-1], high_wide.shape[-1]
    mine, tile = lax.axis_index("clip"), lax.axis_index("space")
    even = lax.rem(tile, 2) == 0
    outside = (tile == 0, tile == tiles - 1)
    copies = Copies(sems)
    glow[...] = glow_in[...]
    ghigh[...] = ghigh_in[...]
    gklow[27:] = jnp.zeros_like(gklow[27:])
    gkhigh[27:] = jnp.zeros_like(gkhigh[27:])

    def border_gradient(padded, back, part, total):
        def finish(k, lanes, sums):
            total[k : k + 1, lanes] = jnp.sum(sums, axis=0, keepdims=True)

        kernel_gradient(
            frames, [(padded.at[side], back.at[side]) for side in range(2)], lambda k, lanes: part[k, :, lanes], finish
        )

    def halo(side, cell, row):
        ours, other = first[cell, row].astype(F32), second[cell, row].astype(F32)
        found = jnp.where(even, other, ours) if side == 0 else jnp.where(even, ours, other)
        return jnp.where(outside[side], 0.0, found)

    for side in range(2):
        for cell in range(cells):
            for k in range(2):
                whole = (edge[side, cell, k] + halo(side, cell, k)[:, 0:out]).astype(BF16).astype(F32)
                if k == side:
                    whole = jnp.where(outside[side], 0.0, whole)
                else:
                    feature[side, cell] = whole
                for j, value in enumerate(gate_rows(whole)):
                    gated[j, side, cell, 2 * side + k] = value
                for j in range(3):
                    gated[j, side, cell, 2 - 2 * side + k] = inner[j, 0, cell, side * (rows - 4) + k]

    second_feature(frames, gated, wc, 2, fine)

    for side in range(2):
        for cell in range(cells):
            low_halo, high_halo = halo(side, cell, 2), halo(side, cell, 3)
            at = 0 if side == 0 else 2
            low_pad[side, cell, at] = low_halo[:, 0:low_ch]
            low_pad[side, cell, pl.ds(1 - side, 2)] = low_wide[cell, pl.ds(side * (rows - 2), 2)]
            at = 0 if side == 0 else 5
            high_pad[side, cell, at, 0:cols] = high_halo[:, 0:high_ch]
            high_pad[side, cell, at, cols:] = high_halo[:, high_ch : 2 * high_ch]
            high_pad[side, cell, pl.ds(1 - side, 5)] = high_wide[cell, pl.ds(side * (2 * rows - 5), 5)]
        at = 3 * side
        for step in depthwise(frames, high_pad.at[side, :, at : at + 3], khigh, high_student.at[side, :, at : at + 1]):
            step()
        for cell in range(cells):
            high_student[side, cell, 1 - side : 4 - side] = border_student[side, cell]
        for step in depthwise(frames, low_pad.at[side], klow, low_student.at[side]):
            step()

    student = low_student[...].reshape(-1, low_ch)
    _, back = level(student, feature[...].reshape(-1, out), plow[...], scale_low, glow)
    low_back[...] = back.reshape(low_back.shape)
    border_gradient(low_pad, low_back, gklow_in, gklow)

    for side in range(2):
        student = high_student[side].reshape(-1, high_ch)
        target = jnp.concatenate([fine_target(fine.at[side, cell], slice(0, 2)) for cell in range(cells)], axis=0)
        value, back = level(student, target, phigh[...], scale_high, ghigh)
        mismatch[side] = value.astype(BF16).reshape(mismatch.shape[1:])
        high_back[side] = back.reshape(high_back.shape[1:])
    stores = [
        copies.start(mismatch.at[0], mismatch_hbm.at[:, pl.ds(0, 4)]),
        copies.start(mismatch.at[1], mismatch_hbm.at[:, pl.ds(2 * rows - 4, 4)]),
    ]
    border_gradient(high_pad, high_back, gkhigh_in, gkhigh)

    low_rows, high_rows = low_ch // shards, high_ch // shards
    shard_sums[...] = jnp.zeros_like(shard_sums)
    width = gklow.shape[1]
    half = out // 2
    lane = lax.broadcasted_iota(jnp.int32, gklow.shape, 1)
    wide_high = gkhigh[...]
    if high_ch < width:
        wide_high = jnp.concatenate([wide_high, jnp.zeros((wide_high.shape[0], width - high_ch), F32)], axis=1)
    for s in range(shards):
        shard_sums[s, 0:low_rows, 0:out] = glow[s * low_rows : (s + 1) * low_rows]
        shard_sums[s, low_rows : low_rows + high_rows, 0:out] = ghigh[s * high_rows : (s + 1) * high_rows]
        from_low = pltpu.roll(gklow[...], (width - s * low_rows) % width, 1)
        from_high = pltpu.roll(wide_high, (width + low_rows - s * high_rows) % width, 1)
        both = jnp.where(lane < low_rows, from_low, jnp.where(lane < low_rows + high_rows, from_high, 0.0))
        top = low_rows + high_rows
        shard_sums[s, top : top + 16, 0:half] = both[0:16, 0:half]
        shard_sums[s, top : top + 16, half : 2 * half] = both[16:32, 0:half]
    if shards == 1:
        keep[0] = shard_sums[0]
        send[0] = shard_sums[0].astype(BF16)
    else:
        bit = lax.rem(mine, 2)
        for k in range(shards // 2):
            keep[k] = shard_sums[2 * k + bit]
            send[k] = shard_sums[2 * k + 1 - bit].astype(BF16)
    for copy in stores:
        copy.wait()


def swaps(clips, tiles, start):
    found = []
    for clip in range(clips):
        for tile in range(tiles):
            other = tile + 1 if (tile - start) % 2 == 0 else tile - 1
            if 0 <= other < tiles:
                found.append((clip * tiles + tile, clip * tiles + other))
            elif clips % 2 == 0:
                found.append((clip * tiles + tile, (clip ^ 1) * tiles + tile))
    return found


def pairs(count, bit):
    return [(i, i ^ bit) for i in range(count)]


def split_shards(keep, bit):
    halves = keep.reshape((keep.shape[0] // 2, 2) + keep.shape[1:])
    own = lax.rem(lax.div(lax.axis_index("clip"), bit), 2)
    send = lax.dynamic_index_in_dim(halves, 1 - own, 1, False).astype(BF16)
    return lax.dynamic_index_in_dim(halves, own, 1, False), send


def sum_over_devices(keep, send, clips, tiles):
    clip_bit, tile_bit = 2, 1
    if clips > 1:
        keep = keep + lax.ppermute(send, "clip", pairs(clips, 1)).astype(F32)
    if clips > 2 and tiles > 1:
        keep, send = split_shards(keep, 2)
        across = [(c * tiles + t, (c ^ 2) * tiles + (t ^ 1)) for c in range(clips) for t in range(tiles)]
        got = (
            lax.ppermute(keep.astype(BF16), "space", pairs(tiles, 1)),
            lax.ppermute(send, "clip", pairs(clips, 2)),
            lax.ppermute(send, ("clip", "space"), across),
        )
        for part in got:
            keep = keep + part.astype(F32)
        clip_bit, tile_bit = 4, 2
    while clip_bit < clips:
        keep, send = split_shards(keep, clip_bit)
        keep = keep + lax.ppermute(send, "clip", pairs(clips, clip_bit)).astype(F32)
        clip_bit *= 2
    total, got = keep[0], []
    while tile_bit < tiles:
        for part in got:
            total = total + part.astype(F32)
        bits = (tile_bit, 2 * tile_bit, 3 * tile_bit) if 2 * tile_bit < tiles else (tile_bit,)
        out = total.astype(BF16)
        got = [lax.ppermute(out, "space", pairs(tiles, b)) for b in bits[::-1]]
        tile_bit *= 2 ** (2 if len(bits) > 1 else 1)
    return total, got


def unpack_kernel(total_ref, *refs):
    got, (glow, gklow, ghigh, gkhigh), sums = refs[:-5], refs[-5:-1], refs[-1]
    value = total_ref[...]
    for part in got:
        value = value + part[...].astype(F32)
    sums[...] = value
    low_rows, high_rows, out = glow.shape[0], ghigh.shape[0], glow.shape[1]
    top = low_rows + high_rows
    glow[...] = sums[0:low_rows, 0:out]
    ghigh[...] = sums[low_rows:top, 0:out]
    for k in range(27):
        at, lane = top + k % 16, k // 16 * (out // 2)
        tap, row, col = k // 9, k // 3 % 3, k % 3
        gklow[tap, row, col : col + 1] = sums[at : at + 1, lane : lane + low_rows]
        gkhigh[tap, row, col : col + 1] = sums[at : at + 1, lane + low_rows : lane + top]


def on_device(teacher_input, conv_first, conv_second, student_low, student_high, kernel_low, kernel_high, adapter_low, adapter_high):
    clips, tiles = lax.axis_size("clip"), lax.axis_size("space")
    held, frames, rows, cols, depth = teacher_input.shape
    cells = held * frames
    out = conv_first.shape[-1]
    low_ch, high_ch = student_low.shape[-1], student_high.shape[-1]
    low_count = held * frames * rows * cols * clips * tiles
    scales = (1.0 / low_count, 1.0 / (4 * low_count))
    inner = rows - 4
    x = teacher_input.reshape(cells, rows, cols, depth)
    low = student_low.reshape(cells, rows, cols, low_ch)
    high = student_high.reshape(cells, 2 * rows, 2 * cols, high_ch)
    sems = pltpu.SemaphoreType.DMA

    def vm(*specs):
        return [pltpu.VMEM(shape, dtype) for shape, dtype in specs]

    packet = ((cells, 4, cols, max(out, low_ch, 2 * high_ch)), BF16)
    inner_spec = ((cells, rows - 2, cols, out), BF16)
    edge_spec = ((2, cells, 2, cols, out), F32)
    wc_spec = ((2, 2, 3, 2, 2, out, out), BF16)
    weights = ((kernel_low.shape, F32), (kernel_high.shape, F32), (adapter_low.shape, BF16), (adapter_high.shape, BF16))
    inner_feature, edge, first, second, w2, low_wide, high_wide, high_student, klow, khigh, plow, phigh = pl.pallas_call(
        functools.partial(first_kernel, frames),
        out_shape=tuple(
            vm(
                inner_spec,
                edge_spec,
                packet,
                packet,
                (conv_second.shape, BF16),
                (low.shape, F32),
                (high.shape, F32),
                ((cells, 2 * inner, 2 * cols, high_ch), BF16),
                *weights,
            )
        ),
        in_specs=[HBM] * 9,
        out_specs=(VMEM,) * 12,
        scratch_shapes=vm(
            (x.shape, BF16),
            (conv_first.shape, BF16),
            ((3, cells, rows + 2, cols, out), F32),
            (low.shape, BF16),
            (high.shape, BF16),
        )
        + [sems((18,))],
        compiler_params=pltpu.CompilerParams(vmem_limit_bytes=20 * MIB),
        cost_estimate=pl.CostEstimate(flops=3 * 10**9, bytes_accessed=9 * 10**6, transcendentals=0),
        name="teacher_first",
    )(*in_hbm(x, conv_first, conv_second, low, high, kernel_low, kernel_high, adapter_low, adapter_high))

    first_got = lax.ppermute(first, ("clip", "space"), swaps(clips, tiles, 0))
    second_got = lax.ppermute(second, ("clip", "space"), swaps(clips, tiles, 1))

    adapters = (((low_ch, out), F32), ((high_ch, out), F32))
    partial_sums = (((27, 8, low_ch), F32), ((27, 8, high_ch), F32))
    kernels = (((32, low_ch), F32), ((32, high_ch), F32))
    mismatch, inner_gated, wc, border_student, *sums = pl.pallas_call(
        functools.partial(second_kernel, frames, *scales),
        out_shape=(
            pltpu.HBM((cells, 2 * rows, 2 * cols, out), BF16),
            *vm(((3, 1, cells, rows - 2, cols, out), BF16), wc_spec, ((2, cells, 3, 2 * cols, high_ch), BF16), *adapters, *partial_sums),
        ),
        in_specs=[VMEM] * 9,
        out_specs=(HBM,) + (VMEM,) * 7,
        scratch_shapes=vm(
            ((cells, 2 * inner, 2 * cols, out), BF16),
            ((1, cells, inner, 2, out // 128, 2 * cols, 128), F32),
            ((cells, rows - 2, cols, low_ch), BF16),
            ((cells, rows - 2, cols, low_ch), F32),
            ((cells, 2 * inner, 2 * cols, high_ch), F32),
        )
        + [sems((1,))],
        compiler_params=pltpu.CompilerParams(vmem_limit_bytes=20 * MIB),
        cost_estimate=pl.CostEstimate(flops=5 * 10**9, bytes_accessed=20 * 10**6, transcendentals=0),
        name="inner_rows",
    )(inner_feature, w2, low_wide, high_wide, high_student, klow, khigh, plow, phigh)

    shard_rows = low_ch // clips + high_ch // clips + 16
    shard_rows += -shard_rows % 16
    shard = (max(clips // 2, 1), shard_rows, out)
    mismatch, keep, send = pl.pallas_call(
        functools.partial(third_kernel, frames, clips, tiles, *scales),
        out_shape=(pltpu.HBM(mismatch.shape, BF16), *vm((shard, F32), (shard, BF16))),
        in_specs=[VMEM] * 16 + [HBM],
        out_specs=(HBM, VMEM, VMEM),
        input_output_aliases={16: 0},
        scratch_shapes=vm(
            *adapters,
            *kernels,
            ((2, cells, 4, 2 * cols, out), BF16),
            ((2, cells, cols, out), F32),
            ((3, 2, cells, 4, cols, out), BF16),
            ((2, cells, 2, 2, out // 128, 2 * cols, 128), F32),
            ((2, cells, 3, cols, low_ch), F32),
            ((2, cells, 6, 2 * cols, high_ch), F32),
            ((2, cells, 1, cols, low_ch), BF16),
            ((2, cells, 4, 2 * cols, high_ch), BF16),
            ((2, cells, 1, cols, low_ch), F32),
            ((2, cells, 4, 2 * cols, high_ch), F32),
            ((clips, shard_rows, out), F32),
        )
        + [sems((2,))],
        compiler_params=pltpu.CompilerParams(vmem_limit_bytes=20 * MIB),
        cost_estimate=pl.CostEstimate(flops=3 * 10**9, bytes_accessed=20 * 10**6, transcendentals=0),
        name="border_rows",
    )(first_got, second_got, edge, inner_gated, wc, border_student, *sums, low_wide, high_wide, klow, khigh, plow, phigh, *in_hbm(mismatch))

    total, got = sum_over_devices(keep, send, clips, tiles)
    low_rows, high_rows = low_ch // clips, high_ch // clips
    glow, gklow, ghigh, gkhigh = pl.pallas_call(
        unpack_kernel,
        out_shape=(
            jax.ShapeDtypeStruct((low_rows, out), F32),
            jax.ShapeDtypeStruct((3, 3, 3, low_rows), F32),
            jax.ShapeDtypeStruct((high_rows, out), F32),
            jax.ShapeDtypeStruct((3, 3, 3, high_rows), F32),
        ),
        in_specs=[VMEM] * (1 + len(got)),
        out_specs=(VMEM,) * 4,
        scratch_shapes=[pltpu.VMEM(shard[1:], F32)],
        compiler_params=pltpu.CompilerParams(vmem_limit_bytes=4 * MIB),
        name="unpack",
    )(total, *got)
    return glow, gklow, ghigh, gkhigh, mismatch.reshape(held, frames, 2 * rows, 2 * cols, out)


def solution(mesh):
    tiled = P("clip", None, "space", None, None)
    return jax.shard_map(
        on_device,
        mesh=mesh,
        in_specs=(tiled, P(), P(), tiled, tiled, P(), P(), P(), P()),
        out_specs=(P("clip", None), P(None, None, None, "clip"), P("clip", None), P(None, None, None, "clip"), tiled),
        check_vma=False,
    )
```
